256 devices in a mesh: tm: 4 (over z_hi, core), clip: 64 (over y, z_lo, x).
Axes of the slice: x: 4, y: 4, z: 8 (z_hi: 2, z_lo: 4; z = z_hi * 4 + z_lo), core: 2. Of those that a mesh axis runs over, the one named last changes fastest.
Arguments:
- latents: bfloat16 [64, 16, 128, 4, 128], P('clip', 'tm'), may hold values from -16 to 16
- norm_gain: float32 [128], replicated, may hold values from 0.1 to 1.9
- norm_shift: float32 [128], replicated, may hold values from -3 to 3
- kernel: bfloat16 [27, 128, 128], replicated, may hold values from -0.109375 to 0.109375
- cotangent: bfloat16 [64, 16, 128, 4, 128], P('clip', 'tm'), may hold values from -8 to 8
Outputs:
- output: bfloat16 [64, 16, 128, 4, 128], P('clip', 'tm')
- input_adjoint: bfloat16 [64, 16, 128, 4, 128], P('clip', 'tm')
- kernel_grad: float32 [27, 128, 128], replicated
The draws below stay inside these ranges and needn't reach their ends.
All inputs are finite; a program needn't handle non-finite values.
Results may differ from the reference program's by a relative error of at most 0.0027.
Values may be sent and summed in bfloat16 or wider, within the bound.
No kernel may reach another device: no remote copies, remote signals or barrier semaphores. Data moves between devices by JAX's collectives and lax.ppermute only.
A program may use at most 128 MiB of HBM per device.

```python
import jax
import jax.numpy as jnp
from jax import lax

C = 128
GROUPS = 32
T_DEV = 4
HEIGHT = 4
WIDTH = 128
CLIPS = 64
TIME = 16


def draw_latents(key, part):
    noise_key = jax.random.fold_in(key, 11)
    offset_key = jax.random.fold_in(key, 12)
    ramp = (jnp.arange(TIME, dtype=jnp.float32) / (TIME - 1))[None, :, None, None, None]
    offsets = jax.random.truncated_normal(offset_key, -2.0, 2.0, (C,), jnp.float32)[None, None, :, None, None]
    shape = (CLIPS, TIME, C, HEIGHT, WIDTH)
    noise = jax.random.truncated_normal(noise_key, -4.0, 4.0, shape, jnp.float32)
    scales = jnp.ones((C,), jnp.float32)[None, None, :, None, None]
    values = (0.6 + 1.2 * ramp) * scales * noise + 0.8 * ramp * offsets
    return values.astype(jnp.bfloat16)


def draw_cotangent(key, part):
    key = jax.random.fold_in(key, 21)
    noise_key = jax.random.fold_in(key, 1)
    offset_key = jax.random.fold_in(key, 2)
    shape = (CLIPS, TIME, C, HEIGHT, WIDTH)
    slabs = TIME // T_DEV
    noise = jax.random.truncated_normal(noise_key, -4.0, 4.0, shape, jnp.float32)
    offsets = 0.8 * jax.random.truncated_normal(offset_key, -2.5, 2.5, (CLIPS, slabs, C), jnp.float32)
    offsets = jnp.repeat(offsets, T_DEV, axis=1)[:, :, :, None, None]
    values = noise + offsets
    return values.astype(jnp.bfloat16)


def centred(rng, extent, deviation, reach, kind=jnp.bfloat16):
    drawn = deviation * jax.random.normal(rng, extent, jnp.float32)
    return jnp.clip(drawn, min=-reach, max=reach).astype(kind)


def setup_inputs(seed: int = 0) -> dict:
    key_of = jax.random.split(jax.random.key(seed), 6)
    return {
        "latents": draw_latents(jax.random.fold_in(key_of[5], 71), 0),
        "norm_gain": jnp.clip(1.0 + 0.18 * jax.random.normal(key_of[1], (C,), jnp.float32), 0.1, 1.9),
        "norm_shift": centred(key_of[2], (C,), 0.5, 3.0, jnp.float32),
        "kernel": centred(key_of[3], (27, C, C), (27 * C) ** -0.5, 0.109375),
        "cotangent": draw_cotangent(jax.random.fold_in(key_of[5], 71), 0),
    }


def group_totals(values):
    return lax.optimization_barrier(jnp.sum(values, axis=(0, 2, 3))).reshape(GROUPS, -1).sum(axis=1)

def per_channel(values):
    return jnp.repeat(values, C // GROUPS)[None, :, None, None]

def one_clip(frames_in, adjoint_in, norm_gain, norm_shift, kernel):
    frames = frames_in.astype(jnp.float32)
    members = TIME * (C // GROUPS) * HEIGHT * WIDTH
    center = group_totals(frames) / members
    inverse = lax.rsqrt(group_totals(frames * frames) / members - center * center + 1e-06)
    unit = (frames - per_channel(center)) * per_channel(inverse)
    gain_c = norm_gain[None, :, None, None]
    normed = unit * gain_c + norm_shift[None, :, None, None]
    active = jax.nn.silu(normed).astype(jnp.bfloat16)
    before = jnp.zeros((2, C, HEIGHT, WIDTH), jnp.bfloat16)
    padded = jnp.pad(jnp.concatenate([before, active], 0), ((0, 0), (0, 0), (1, 1), (1, 1))).astype(jnp.float32)
    adjoint = adjoint_in.astype(jnp.float32)
    after = jnp.zeros((2, C, HEIGHT, WIDTH), jnp.float32)
    adj_padded = jnp.pad(jnp.concatenate([adjoint, after], 0), ((0, 0), (0, 0), (1, 1), (1, 1)))
    weights = kernel.astype(jnp.float32)
    conv = jnp.zeros((TIME, C, HEIGHT, WIDTH), jnp.float32)
    back = jnp.zeros((TIME, C, HEIGHT, WIDTH), jnp.float32)
    grads = []
    for kt in range(3):
        for ki in range(3):
            for kj in range(3):
                tap_index = 9 * kt + 3 * ki + kj
                window = padded[kt:kt + TIME, :, ki:ki + HEIGHT, kj:kj + WIDTH]
                conv = conv + jnp.einsum('oc,tchw->tohw', weights[tap_index], window)
                grads.append(jnp.einsum('tohw,tchw->oc', adjoint, window))
                adj_window = adj_padded[2 - kt:2 - kt + TIME, :, 2 - ki:2 - ki + HEIGHT, 2 - kj:2 - kj + WIDTH]
                back = back + jnp.einsum('oc,tohw->tchw', weights[tap_index], adj_window)
    output = (frames + conv).astype(jnp.bfloat16)
    logistic = jax.nn.sigmoid(normed)
    scaled = back * logistic * (1.0 + normed * (1.0 - logistic)) * gain_c
    first = group_totals(scaled) / members
    second = group_totals(scaled * unit) / members
    result = adjoint + per_channel(inverse) * (scaled - per_channel(first) - unit * per_channel(second))
    return (output, result.astype(jnp.bfloat16), jnp.stack(grads, 0))

def reference(latents, norm_gain, norm_shift, kernel, cotangent):

    def step_clip(carry, inputs):
        output, result, grads = one_clip(inputs[0], inputs[1], norm_gain, norm_shift, kernel)
        return (carry + grads, (output, result))
    start = jnp.zeros((27, C, C), jnp.float32)
    kernel_grad, outputs = lax.scan(step_clip, start, (latents, cotangent))
    return (outputs[0], outputs[1], kernel_grad)
```

```python
import functools

import jax
import jax.numpy as jnp
from jax import lax
from jax.experimental import pallas as pl
from jax.experimental.pallas import tpu as pltpu
from jax.sharding import Mesh
from jax.sharding import PartitionSpec as P

C = 128
H = 4
W = 128
T = 4
HALO = 2
GROUPS = 32
PER = C // GROUPS
SLABS = 4
MEMBERS = SLABS * T * PER * H * W
ROWS = H * C
HALF = 27 * (C // 2)
COMM = HALF + 64
SIDE = 16
PART = COMM // SIDE
F32 = jnp.float32
BF16 = jnp.bfloat16
LIMIT = pltpu.CompilerParams(vmem_limit_bytes=48 * 1024 * 1024)


def lanes():
    return lax.broadcasted_iota(jnp.int32, (C, W), 1)


def rows():
    return lax.broadcasted_iota(jnp.int32, (C, W), 0)


def shifted(block):
    left = jnp.where(lanes() == 0, 0.0, pltpu.roll(block, 1, 1))
    right = jnp.where(lanes() == W - 1, 0.0, pltpu.roll(block, W - 1, 1))
    return left, block, right


def row_of(column, offset):
    lane = lax.broadcasted_iota(jnp.int32, (GROUPS, W), 1)
    sub = lax.broadcasted_iota(jnp.int32, (GROUPS, W), 0)
    return jnp.sum(jnp.where(lane == sub + offset, column, 0.0), axis=0, keepdims=True)


def channel_column(row):
    return jnp.sum(jnp.where(lanes() == rows(), row, 0.0), axis=1, keepdims=True)


def group_column(row, offset, per_channel):
    lane = lax.broadcasted_iota(jnp.int32, (GROUPS * per_channel, W), 1)
    sub = lax.broadcasted_iota(jnp.int32, (GROUPS * per_channel, W), 0)
    return jnp.sum(jnp.where(lane == sub // per_channel + offset, row, 0.0), axis=1, keepdims=True)


def center_inverse(totals, per_channel):
    row = jnp.sum(totals[...].reshape(-1, 8, W), axis=0)[0:1] / MEMBERS
    center = group_column(row, 0, per_channel)
    square = group_column(row, GROUPS, per_channel)
    return center, lax.rsqrt(square - center * center + 1e-06)


def sums_kernel(lat, out):
    total = jnp.zeros((ROWS, W), F32)
    square = jnp.zeros((ROWS, W), F32)
    for t in range(T):
        x = lat[t].astype(F32)
        total = total + x
        square = square + x * x
    total = jnp.sum(jnp.sum(total.reshape(GROUPS, -1, W), axis=1), axis=1, keepdims=True)
    square = jnp.sum(jnp.sum(square.reshape(GROUPS, -1, W), axis=1), axis=1, keepdims=True)
    row = row_of(total, 0) + row_of(square, GROUPS)
    out[...] = jnp.broadcast_to(row, (8, W))


def by_row(frame, tmp):
    tmp[...] = frame.astype(F32)
    return [tmp[pl.ds(h, C, stride=H), :] for h in range(H)]


def back_kernel(cot, following, kernel, back, tmp, window, taps):
    for f in range(T + HALO):
        blocks = by_row(cot[f] if f < T else following[f - T], tmp)
        for h in range(H):
            for s, moved in enumerate(shifted(blocks[h])):
                at = (s * H + h) * C
                window[at : at + C, f * W : (f + 1) * W] = moved.astype(BF16)
    taps[...] = jnp.zeros_like(taps)
    for kt in range(3):
        for ki in range(3):
            for kj in range(3):
                tap = kernel[9 * kt + 3 * ki + kj].astype(F32).T.astype(BF16)
                for h in range(H):
                    other = h + 1 - ki
                    if 0 <= other < H:
                        at = ((2 - kj) * H + other) * C
                        taps[2 - kt, h * C : (h + 1) * C, at : at + C] = tap
    total = jnp.dot(taps[0], window[:, 0 : T * W], preferred_element_type=F32)
    for f in range(1, 3):
        total = total + jnp.dot(taps[f], window[:, f * W : (f + T) * W], preferred_element_type=F32)
    back[...] = total


def grad_kernel(flags, lat, previous, cot, totals, gain, shift, back, window, scaled, keep, send, tmp, flat, adj):
    has_previous, core = flags[0], flags[1]
    center, inverse = center_inverse(totals, PER)
    gain_c = channel_column(gain[...])
    shift_c = channel_column(shift[...])
    first = jnp.zeros((C, W), F32)
    second = jnp.zeros((C, W), F32)
    for f in range(T + HALO):
        t = f - HALO
        blocks = by_row(previous[f] if t < 0 else lat[t], tmp)
        for h in range(H):
            unit = (blocks[h] - center) * inverse
            normed = unit * gain_c + shift_c
            sig = 1.0 / (1.0 + jnp.exp(-normed))
            active = normed * sig
            if t < 0:
                active = jnp.where(has_previous > 0, active, 0.0)
            else:
                adjoint = back[h * C : (h + 1) * C, t * W : (t + 1) * W]
                value = adjoint * sig * (1.0 + normed * (1.0 - sig)) * gain_c
                first = first + value
                second = second + value * unit
                scaled[t, pl.ds(h, C, stride=H), :] = value
            for s, moved in enumerate(shifted(active.astype(BF16).astype(F32))):
                moved = moved.astype(BF16)
                window[(s * H + h) * C : (s * H + h + 1) * C, f * W : (f + 1) * W] = moved
                flat[s * C : (s + 1) * C, (f * H + h) * W : (f * H + h + 1) * W] = moved
    zero = jnp.zeros((C, W), BF16)
    for t in range(T):
        blocks = by_row(cot[t], tmp)
        for h in range(H):
            for ki in range(3):
                source = h - ki + 1
                block = blocks[source].astype(BF16) if 0 <= source < H else zero
                adj[ki * C : (ki + 1) * C, (t * H + h) * W : (t * H + h + 1) * W] = block
    half = C // 2
    for kt in range(3):
        grads = lax.dot_general(
            adj[...],
            flat[:, kt * H * W : (kt + T) * H * W],
            (((1,), (1,)), ((), ())),
            preferred_element_type=F32,
        )
        for ki in range(3):
            for kj in range(3):
                tap = grads[ki * C : (ki + 1) * C, kj * C : (kj + 1) * C]
                low, high = tap[:half], tap[half:]
                at = (9 * kt + 3 * ki + kj) * half
                keep[at : at + half] = jnp.where(core == 0, low, high)
                send[at : at + half] = jnp.where(core == 0, high, low)
    lane, sub = lanes(), rows()
    first = jnp.sum(jnp.where(lane == sub // PER, jnp.sum(first, axis=1, keepdims=True), 0.0), axis=0, keepdims=True)
    second = jnp.sum(
        jnp.where(lane == sub // PER + GROUPS, jnp.sum(second, axis=1, keepdims=True), 0.0), axis=0, keepdims=True
    )
    tail = jnp.broadcast_to(first + second, (COMM - HALF, W))
    keep[HALF:] = tail
    send[HALF:] = tail


def conv_kernel(lat, kernel, window, output, tmp, taps):
    taps[...] = jnp.zeros_like(taps)
    for kt in range(3):
        for ki in range(3):
            for kj in range(3):
                tap = kernel[9 * kt + 3 * ki + kj]
                for h in range(H):
                    other = h - 1 + ki
                    if 0 <= other < H:
                        at = (kj * H + other) * C
                        taps[kt, h * C : (h + 1) * C, at : at + C] = tap
    total = jnp.dot(taps[0], window[:, 0 : T * W], preferred_element_type=F32)
    for f in range(1, 3):
        total = total + jnp.dot(taps[f], window[:, f * W : (f + T) * W], preferred_element_type=F32)
    for t in range(T):
        for h in range(H):
            tmp[pl.ds(h, C, stride=H), :] = total[h * C : (h + 1) * C, t * W : (t + 1) * W]
        output[t] = (lat[t].astype(F32) + tmp[...]).astype(BF16)


def adjoint_kernel(lat, cot, totals, backward, scaled, result):
    center, inverse = center_inverse(totals, PER * H)
    row = backward[...][0:1] / MEMBERS
    first = group_column(row, 0, PER * H)
    second = group_column(row, GROUPS, PER * H)
    for t in range(T):
        unit = (lat[t].astype(F32) - center) * inverse
        value = cot[t].astype(F32) + inverse * (scaled[t] - first - unit * second)
        result[t] = value.astype(BF16)


def call(body, out, scratch, *operands, scalars=0):
    inside = pl.BlockSpec(memory_space=pltpu.VMEM)
    return pl.pallas_call(
        body,
        out_shape=out,
        in_specs=[pl.BlockSpec(memory_space=pltpu.SMEM)] * scalars + [inside] * (len(operands) - scalars),
        out_specs=jax.tree.map(lambda _: inside, out),
        scratch_shapes=scratch,
        compiler_params=LIMIT,
    )(*operands)


def shape(*dims, dtype=F32):
    return jax.ShapeDtypeStruct(dims, dtype)


def swap(value, axis):
    return lax.ppermute(value, axis, [(0, 1), (1, 0)])


def per_device(latents, norm_gain, norm_shift, kernel, cotangent):
    lat = latents.reshape(T, ROWS, W)
    cot = cotangent.reshape(T, ROWS, W)
    slab = ("zh", "core")
    previous = lax.ppermute(lat[T - HALO :], slab, [(i, i + 1) for i in range(SLABS - 1)])
    following = lax.ppermute(cot[:HALO], slab, [(i + 1, i) for i in range(SLABS - 1)])
    own = call(sums_kernel, shape(8, W), [], lat)
    pair = own + swap(own, "core")
    totals = jnp.concatenate([pair, swap(pair, "zh")], axis=0)
    tmp = pltpu.VMEM((ROWS, W), F32)
    window_scratch = pltpu.VMEM((3 * ROWS, (T + HALO) * W), BF16)
    taps = pltpu.VMEM((3, ROWS, 3 * ROWS), BF16)
    back = call(back_kernel, shape(ROWS, T * W), [tmp, window_scratch, taps], cot, following, kernel)
    zh, core = lax.axis_index("zh"), lax.axis_index("core")
    flags = jnp.stack([zh * 2 + core, core]).astype(jnp.int32)
    window, scaled, keep, send = call(
        grad_kernel,
        (
            shape(3 * ROWS, (T + HALO) * W, dtype=BF16),
            shape(T, ROWS, W),
            shape(COMM, C),
            shape(COMM, C),
        ),
        [
            tmp,
            pltpu.VMEM((3 * C, (T + HALO) * H * W), BF16),
            pltpu.VMEM((3 * C, T * H * W), BF16),
        ],
        flags,
        lat,
        previous,
        cot,
        totals,
        norm_gain.reshape(1, C),
        norm_shift.reshape(1, C),
        back,
        scalars=1,
    )
    chip = keep + swap(send, "core")
    output = call(conv_kernel, shape(T, ROWS, W, dtype=BF16), [tmp, taps], lat, kernel, window)
    parts = lax.all_to_all(chip.astype(WIRE).reshape(SIDE, PART, C), ("y", "x"), 0, 0)
    part = jnp.sum(parts.astype(F32), axis=0)
    packed = jnp.concatenate([part, chip[HALF : HALF + 8]], axis=0)
    size = 8
    over_z = lax.all_to_all(jnp.broadcast_to(packed, (size,) + packed.shape), ("zh", "zl"), 0, 0)
    part = jnp.sum(over_z[:, :PART], axis=0).astype(BF16)
    zl = lax.axis_index("zl")
    backward = lax.dynamic_slice_in_dim(over_z[:4, PART:], zl, 1, 0)[0] + lax.dynamic_slice_in_dim(over_z[4:, PART:], zl, 1, 0)[0]
    result = call(adjoint_kernel, shape(T, ROWS, W, dtype=BF16), [], lat, cot, totals, backward, scaled)
    mine = lax.all_to_all(jnp.broadcast_to(part, (SIDE,) + part.shape), ("y", "x"), 0, 0).reshape(COMM, C)[:HALF]
    other = swap(mine, "core")
    mine, other = mine.reshape(27, C // 2, C), other.reshape(27, C // 2, C)
    low = jnp.where(core == 0, mine, other)
    high = jnp.where(core == 0, other, mine)
    kernel_grad = jnp.concatenate([low, high], axis=1).astype(F32)
    return output.reshape(latents.shape), result.reshape(latents.shape), kernel_grad


WIRE = F32


def solution(mesh):
    fine = Mesh(mesh.devices.reshape(2, 2, 4, 4, 4), ("zh", "core", "y", "zl", "x"))
    frames = P(("y", "zl", "x"), ("zh", "core"), None, None, None)
    return jax.shard_map(
        per_device,
        mesh=fine,
        in_specs=(frames, P(), P(), P(), frames),
        out_specs=(frames, frames, P()),
        check_vma=False,
    )
```

```python
import functools

import jax
import jax.numpy as jnp
from jax import lax
from jax.experimental import pallas as pl
from jax.experimental.pallas import tpu as pltpu
from jax.sharding import Mesh
from jax.sharding import PartitionSpec as P

C = 128
H = 4
W = 128
T = 4
HALO = 2
GROUPS = 32
PER = C // GROUPS
SLABS = 4
MEMBERS = SLABS * T * PER * H * W
ROWS = H * C
HALF = 27 * (C // 2)
COMM = HALF + 64
SIDE = 32
PART = COMM // SIDE
F32 = jnp.float32
BF16 = jnp.bfloat16
LIMIT = pltpu.CompilerParams(vmem_limit_bytes=24 * 1024 * 1024)


def lanes():
    return lax.broadcasted_iota(jnp.int32, (C, W), 1)


def rows():
    return lax.broadcasted_iota(jnp.int32, (C, W), 0)


def shifted(block):
    left = jnp.where(lanes() == 0, 0.0, pltpu.roll(block, 1, 1))
    right = jnp.where(lanes() == W - 1, 0.0, pltpu.roll(block, W - 1, 1))
    return left, block, right


def row_of(column, offset):
    lane = lax.broadcasted_iota(jnp.int32, (GROUPS, W), 1)
    sub = lax.broadcasted_iota(jnp.int32, (GROUPS, W), 0)
    return jnp.sum(jnp.where(lane == sub + offset, column, 0.0), axis=0, keepdims=True)


def channel_column(row):
    return jnp.sum(jnp.where(lanes() == rows(), row, 0.0), axis=1, keepdims=True)


def group_column(row, offset, per_channel):
    lane = lax.broadcasted_iota(jnp.int32, (GROUPS * per_channel, W), 1)
    sub = lax.broadcasted_iota(jnp.int32, (GROUPS * per_channel, W), 0)
    return jnp.sum(jnp.where(lane == sub // per_channel + offset, row, 0.0), axis=1, keepdims=True)


def center_inverse(totals, per_channel):
    row = jnp.sum(totals[...].reshape(-1, 8, W), axis=0)[0:1] / MEMBERS
    center = group_column(row, 0, per_channel)
    square = group_column(row, GROUPS, per_channel)
    return center, lax.rsqrt(square - center * center + 1e-06)


def copies(sem, *pairs):
    started = [pltpu.make_async_copy(source, target, sem.at[i]) for i, (source, target) in enumerate(pairs)]
    for copy in started:
        copy.start()
    return started


def start_kernel(lat, cot, sums, tail, head, first, sem):
    early, late, moved = copies(sem, (lat.at[: T - HALO], first), (lat.at[T - HALO :], tail), (cot.at[:HALO], head))
    total = jnp.zeros((ROWS, W), F32)
    square = jnp.zeros((ROWS, W), F32)
    for copy, frames in ((early, first), (late, tail)):
        copy.wait()
        for t in range(T // 2):
            x = frames[t].astype(F32)
            total = total + x
            square = square + x * x
    total = jnp.sum(jnp.sum(total.reshape(GROUPS, -1, W), axis=1), axis=1, keepdims=True)
    square = jnp.sum(jnp.sum(square.reshape(GROUPS, -1, W), axis=1), axis=1, keepdims=True)
    row = row_of(total, 0) + row_of(square, GROUPS)
    sums[...] = jnp.broadcast_to(row, (8, W))
    moved.wait()


def prepare_kernel(lat, cot, gain, shift, blocks, adj, scales, lat_v, cot_v, tmp, sem):
    from_lat, from_cot = copies(sem, (lat, lat_v), (cot, cot_v))
    scales[0] = jnp.broadcast_to(channel_column(gain[...]), (C, W))
    scales[1] = jnp.broadcast_to(channel_column(shift[...]), (C, W))
    from_lat.wait()
    for t in range(T):
        for h, block in enumerate(by_row(lat_v[t], tmp)):
            blocks[t * H + h] = block
    from_cot.wait()
    zero = jnp.zeros((C, W), BF16)
    for t in range(T):
        mine = by_row(cot_v[t], tmp)
        for h in range(H):
            for ki in range(3):
                source = h - ki + 1
                block = mine[source].astype(BF16) if 0 <= source < H else zero
                adj[ki * C : (ki + 1) * C, (t * H + h) * W : (t * H + h + 1) * W] = block


def by_row(frame, tmp):
    tmp[...] = frame.astype(F32)
    return [tmp[pl.ds(h, C, stride=H), :] for h in range(H)]


def back_kernel(
    lat, cot, following, kernel, totals, scales, scaled, sums, tmp, window, taps, lat_v, cot_v, kernel_v, scaled_v, sem
):
    from_cot, from_kernel, from_lat = copies(sem, (cot, cot_v), (kernel, kernel_v), (lat, lat_v))
    from_cot.wait()
    for f in range(T + HALO):
        blocks = by_row(cot_v[f] if f < T else following[f - T], tmp)
        for h in range(H):
            for s, moved in enumerate(shifted(blocks[h])):
                at = (s * H + h) * C
                window[at : at + C, f * W : (f + 1) * W] = moved.astype(BF16)
    taps[...] = jnp.zeros_like(taps)
    from_kernel.wait()
    for kt in range(3):
        for ki in range(3):
            for kj in range(3):
                tap = kernel_v[9 * kt + 3 * ki + kj].astype(F32).T.astype(BF16)
                for h in range(H):
                    other = h + 1 - ki
                    if 0 <= other < H:
                        at = ((2 - kj) * H + other) * C
                        taps[2 - kt, h * C : (h + 1) * C, at : at + C] = tap
    back = jnp.dot(taps[0], window[:, 0 : T * W], preferred_element_type=F32)
    for f in range(1, 3):
        back = back + jnp.dot(taps[f], window[:, f * W : (f + T) * W], preferred_element_type=F32)
    center, inverse = center_inverse(totals, PER)
    from_lat.wait()
    first = jnp.zeros((C, W), F32)
    second = jnp.zeros((C, W), F32)
    for t in range(T):
        blocks = by_row(lat_v[t], tmp)
        for h in range(H):
            unit = (blocks[h] - center) * inverse
            normed = unit * scales[0] + scales[1]
            sig = 1.0 / (1.0 + jnp.exp(-normed))
            adjoint = back[h * C : (h + 1) * C, t * W : (t + 1) * W]
            value = adjoint * sig * (1.0 + normed * (1.0 - sig)) * scales[0]
            first = first + value
            second = second + value * unit
            scaled_v[t, pl.ds(h, C, stride=H), :] = value
    (to_scaled,) = copies(sem, (scaled_v, scaled))
    lane, sub = lanes(), rows()
    first = jnp.where(lane == sub // PER, jnp.sum(first, axis=1, keepdims=True), 0.0)
    second = jnp.where(lane == sub // PER + GROUPS, jnp.sum(second, axis=1, keepdims=True), 0.0)
    sums[...] = jnp.broadcast_to(jnp.sum(first + second, axis=0, keepdims=True), (8, W))
    to_scaled.wait()


def grad_kernel(flags, blocks, previous, adj, totals, scales, window, keep, send, tmp, flat, window_v, sem):
    has_previous, core = flags[0], flags[1]
    center, inverse = center_inverse(totals, PER)
    for f in range(T + HALO):
        t = f - HALO
        halo = by_row(previous[f], tmp) if t < 0 else None
        for h in range(H):
            block = halo[h] if t < 0 else blocks[t * H + h]
            normed = (block - center) * inverse * scales[0] + scales[1]
            active = normed * (1.0 / (1.0 + jnp.exp(-normed)))
            if t < 0:
                active = jnp.where(has_previous > 0, active, 0.0)
            for s, moved in enumerate(shifted(active.astype(BF16).astype(F32))):
                moved = moved.astype(BF16)
                window_v[(s * H + h) * C : (s * H + h + 1) * C, f * W : (f + 1) * W] = moved
                flat[s * C : (s + 1) * C, (f * H + h) * W : (f * H + h + 1) * W] = moved
    (to_window,) = copies(sem, (window_v, window))
    half = C // 2
    for kt in range(3):
        grads = lax.dot_general(
            adj[...],
            flat[:, kt * H * W : (kt + T) * H * W],
            (((1,), (1,)), ((), ())),
            preferred_element_type=F32,
        )
        for ki in range(3):
            for kj in range(3):
                tap = grads[ki * C : (ki + 1) * C, kj * C : (kj + 1) * C]
                low, high = tap[:half], tap[half:]
                at = (9 * kt + 3 * ki + kj) * half
                keep[at : at + half] = jnp.where(core == 0, low, high)
                send[at : at + half] = jnp.where(core == 0, high, low)
    keep[HALF:] = jnp.zeros((COMM - HALF, C), F32)
    send[HALF:] = jnp.zeros((COMM - HALF, C), F32)
    to_window.wait()


def add_kernel(keep, received, chip):
    chip[...] = (keep[...] + received[...]).astype(chip.dtype)


def part_kernel(parts, sums, packed):
    packed[:PART] = jnp.sum(parts[...].astype(F32), axis=0)
    packed[PART:] = sums[...]


def place_kernel(flags, mine, other, grad):
    half = C // 2
    core = flags[1]
    for tap in range(27):
        a = mine[tap * half : (tap + 1) * half].astype(F32)
        b = other[tap * half : (tap + 1) * half].astype(F32)
        grad[tap, :half] = jnp.where(core == 0, a, b)
        grad[tap, half:] = jnp.where(core == 0, b, a)


def conv_kernel(lat, kernel, window, output, tmp, taps, lat_v, kernel_v, window_v, sem):
    from_kernel, from_window, from_lat = copies(sem, (kernel, kernel_v), (window, window_v), (lat, lat_v))
    taps[...] = jnp.zeros_like(taps)
    from_kernel.wait()
    for kt in range(3):
        for ki in range(3):
            for kj in range(3):
                tap = kernel_v[9 * kt + 3 * ki + kj]
                for h in range(H):
                    other = h - 1 + ki
                    if 0 <= other < H:
                        at = (kj * H + other) * C
                        taps[kt, h * C : (h + 1) * C, at : at + C] = tap
    from_window.wait()
    total = jnp.dot(taps[0], window_v[:, 0 : T * W], preferred_element_type=F32)
    for f in range(1, 3):
        total = total + jnp.dot(taps[f], window_v[:, f * W : (f + T) * W], preferred_element_type=F32)
    from_lat.wait()
    for t in range(T):
        for h in range(H):
            tmp[pl.ds(h, C, stride=H), :] = total[h * C : (h + 1) * C, t * W : (t + 1) * W]
        output[t] = (lat_v[t].astype(F32) + tmp[...]).astype(BF16)


def adjoint_kernel(lat, cot, totals, backward, scaled, result, lat_v, cot_v, scaled_v, sem):
    started = copies(sem, (lat, lat_v), (cot, cot_v), (scaled, scaled_v))
    center, inverse = center_inverse(totals, PER * H)
    row = backward[...][0:1] / MEMBERS
    first = group_column(row, 0, PER * H)
    second = group_column(row, GROUPS, PER * H)
    for copy in started:
        copy.wait()
    for t in range(T):
        unit = (lat_v[t].astype(F32) - center) * inverse
        value = cot_v[t].astype(F32) + inverse * (scaled_v[t] - first - unit * second)
        result[t] = value.astype(BF16)


VMEM, HBM, SMEM = (
    pl.BlockSpec(memory_space=pltpu.VMEM),
    pl.BlockSpec(memory_space=pltpu.HBM),
    pl.BlockSpec(memory_space=pltpu.SMEM),
)


def call(body, out, scratch, *operands, far=(), out_far=(), scalars=0, flops=0, moved=1 << 20):
    single = not isinstance(out, tuple)
    count = 1 if single else len(out)
    outs = tuple(HBM if i in out_far else VMEM for i in range(count))
    shapes = tuple(pltpu.HBM(o.shape, o.dtype) if i in out_far else o for i, o in enumerate((out,) if single else out))
    operands = [pltpu.with_memory_space_constraint(x, pltpu.HBM) if i in far else x for i, x in enumerate(operands)]
    return pl.pallas_call(
        body,
        out_shape=shapes[0] if single else shapes,
        in_specs=[SMEM if i < scalars else HBM if i in far else VMEM for i in range(len(operands))],
        out_specs=outs[0] if single else outs,
        scratch_shapes=scratch,
        compiler_params=LIMIT,
        cost_estimate=pl.CostEstimate(flops=flops, bytes_accessed=moved, transcendentals=0),
    )(*operands)


def shape(*dims, dtype=F32):
    return jax.ShapeDtypeStruct(dims, dtype)


def sems(count):
    return pltpu.SemaphoreType.DMA((count,))


def swap(value, axis):
    return lax.ppermute(value, axis, [(0, 1), (1, 0)])


def exchange(parts, axes):
    return lax.all_to_all(parts, axes, 0, 0)


def same_to_all(part, size, axes):
    return exchange(jnp.broadcast_to(part, (size,) + part.shape), axes)


def per_device(latents, norm_gain, norm_shift, kernel, cotangent):
    lat = latents.reshape(T, ROWS, W)
    cot = cotangent.reshape(T, ROWS, W)
    gain, shift = norm_gain.reshape(1, C), norm_shift.reshape(1, C)
    slab = ("zh", "core")
    halo = shape(HALO, ROWS, W, dtype=BF16)
    frames = pltpu.VMEM((T, ROWS, W), BF16)
    tmp = pltpu.VMEM((ROWS, W), F32)
    window_scratch = pltpu.VMEM((3 * ROWS, (T + HALO) * W), BF16)
    taps = pltpu.VMEM((3, ROWS, 3 * ROWS), BF16)
    kernel_scratch = pltpu.VMEM((27, C, C), BF16)
    scaled_scratch = pltpu.VMEM((T, ROWS, W), F32)
    own, tail, head = call(
        start_kernel,
        (shape(8, W), halo, halo),
        [pltpu.VMEM((T - HALO, ROWS, W), BF16), sems(3)],
        lat,
        cot,
        far=(0, 1),
    )
    blocks, adj, scales = call(
        prepare_kernel,
        (shape(T * H, C, W), shape(3 * C, T * H * W, dtype=BF16), shape(2, C, W)),
        [frames, frames, tmp, sems(2)],
        lat,
        cot,
        gain,
        shift,
        far=(0, 1),
    )
    pair = own + swap(own, "core")
    totals = jnp.concatenate([pair, swap(pair, "zh")], axis=0)
    previous = lax.ppermute(tail, slab, [(i, i + 1) for i in range(SLABS - 1)])
    following = lax.ppermute(head, slab, [(i + 1, i) for i in range(SLABS - 1)])
    zh, core = lax.axis_index("zh"), lax.axis_index("core")
    flags = jnp.stack([zh * 2 + core, core]).astype(jnp.int32)
    window, keep, send = call(
        grad_kernel,
        (shape(3 * ROWS, (T + HALO) * W, dtype=BF16), shape(COMM, C), shape(COMM, C)),
        [tmp, pltpu.VMEM((3 * C, (T + HALO) * H * W), BF16), window_scratch, sems(1)],
        flags,
        blocks,
        previous,
        adj,
        totals,
        scales,
        out_far=(0,),
        scalars=1,
        flops=4 * 10**9,
    )
    chip = call(add_kernel, shape(COMM, C, dtype=WIRE), [], keep, swap(send, "core"))
    parts = exchange(chip.reshape(SIDE, PART, C), ("y", "zn", "x"))
    scaled, sums = call(
        back_kernel,
        (shape(T, ROWS, W), shape(8, W)),
        [tmp, window_scratch, taps, frames, frames, kernel_scratch, scaled_scratch, sems(3)],
        lat,
        cot,
        following,
        kernel,
        totals,
        scales,
        far=(0, 1, 3),
        out_far=(0,),
        flops=4 * 10**9,
    )
    sums = sums + swap(sums, "core")
    packed = call(part_kernel, shape(PART + 8, C), [], parts, sums)
    over_z = same_to_all(packed, 4, ("zh", "zm"))
    part = jnp.sum(over_z[:, :PART], axis=0).astype(BF16)
    zm = lax.axis_index("zm")
    backward = jnp.sum(
        jnp.where(lax.broadcasted_iota(jnp.int32, (2, 2, 8, C), 1) == zm, over_z[:, PART:].reshape(2, 2, 8, C), 0.0),
        axis=(0, 1),
    )
    part, window = lax.optimization_barrier((part, window))
    mine = same_to_all(part, SIDE, ("y", "zn", "x")).reshape(COMM, C)
    output = call(
        conv_kernel,
        shape(T, ROWS, W, dtype=BF16),
        [tmp, taps, frames, kernel_scratch, window_scratch, sems(3)],
        lat,
        kernel,
        window,
        far=(0, 1, 2),
        flops=4 * 10**9,
    )
    mine, output = lax.optimization_barrier((mine, output))
    other = swap(mine, "core")
    result = call(
        adjoint_kernel,
        shape(T, ROWS, W, dtype=BF16),
        [frames, frames, scaled_scratch, sems(3)],
        lat,
        cot,
        totals,
        backward,
        scaled,
        far=(0, 1, 4),
        flops=10**9,
    )
    kernel_grad = call(place_kernel, shape(27, C, C), [], flags, mine, other, scalars=1)
    return output.reshape(latents.shape), result.reshape(latents.shape), kernel_grad


WIRE = F32


def solution(mesh):
    fine = Mesh(mesh.devices.reshape(2, 2, 4, 2, 2, 4), ("zh", "core", "y", "zm", "zn", "x"))
    frames = P(("y", "zm", "zn", "x"), ("zh", "core"), None, None, None)
    return jax.shard_map(
        per_device,
        mesh=fine,
        in_specs=(frames, P(), P(), P(), frames),
        out_specs=(frames, frames, P()),
        check_vma=False,
    )
```

```python
import functools

import jax
import jax.numpy as jnp
from jax import lax
from jax.experimental import pallas as pl
from jax.experimental.pallas import tpu as pltpu
from jax.sharding import Mesh
from jax.sharding import PartitionSpec as P

C = 128
H = 4
W = 128
T = 4
HALO = 2
GROUPS = 32
PER = C // GROUPS
SLABS = 4
MEMBERS = SLABS * T * PER * H * W
ROWS = H * C
HALF = 27 * (C // 2)
COMM = HALF + 64
SIDE = 32
PART = COMM // SIDE
F32 = jnp.float32
BF16 = jnp.bfloat16
LIMIT = pltpu.CompilerParams(vmem_limit_bytes=24 * 1024 * 1024)


def lanes():
    return lax.broadcasted_iota(jnp.int32, (C, W), 1)


def rows():
    return lax.broadcasted_iota(jnp.int32, (C, W), 0)


def shifted(block):
    left = jnp.where(lanes() == 0, 0.0, pltpu.roll(block, 1, 1))
    right = jnp.where(lanes() == W - 1, 0.0, pltpu.roll(block, W - 1, 1))
    return left, block, right


def row_of(column, offset):
    lane = lax.broadcasted_iota(jnp.int32, (GROUPS, W), 1)
    sub = lax.broadcasted_iota(jnp.int32, (GROUPS, W), 0)
    return jnp.sum(jnp.where(lane == sub + offset, column, 0.0), axis=0, keepdims=True)


def channel_column(row):
    return jnp.sum(jnp.where(lanes() == rows(), row, 0.0), axis=1, keepdims=True)


def group_column(row, offset, per_channel):
    lane = lax.broadcasted_iota(jnp.int32, (GROUPS * per_channel, W), 1)
    sub = lax.broadcasted_iota(jnp.int32, (GROUPS * per_channel, W), 0)
    return jnp.sum(jnp.where(lane == sub // per_channel + offset, row, 0.0), axis=1, keepdims=True)


def center_inverse(totals, per_channel):
    row = jnp.sum(totals[...].reshape(-1, 8, W), axis=0)[0:1] / MEMBERS
    center = group_column(row, 0, per_channel)
    square = group_column(row, GROUPS, per_channel)
    return center, lax.rsqrt(square - center * center + 1e-06)


def copies(sem, *pairs):
    started = [pltpu.make_async_copy(source, target, sem.at[i]) for i, (source, target) in enumerate(pairs)]
    for copy in started:
        copy.start()
    return started


def start_kernel(flags, lat, cot, sums, near, far, lat_v, sem, halo_sem):
    tail, head = lat.at[T - HALO :], cot.at[:HALO]

    @pl.when(flags[1] == 0)
    def _():
        copies(halo_sem, (tail, near), (head, far))

    @pl.when(flags[1] != 0)
    def _():
        copies(halo_sem, (head, near), (tail, far))

    parts = copies(sem, (lat.at[: T // 2], lat_v.at[: T // 2]), (lat.at[T // 2 :], lat_v.at[T // 2 :]))
    total = jnp.zeros((ROWS, W), F32)
    square = jnp.zeros((ROWS, W), F32)
    for t in range(T):
        if t % (T // 2) == 0:
            parts[t // (T // 2)].wait()
        x = lat_v[t].astype(F32)
        total = total + x
        square = square + x * x
    total = jnp.sum(jnp.sum(total.reshape(GROUPS, -1, W), axis=1), axis=1, keepdims=True)
    square = jnp.sum(jnp.sum(square.reshape(GROUPS, -1, W), axis=1), axis=1, keepdims=True)
    row = row_of(total, 0) + row_of(square, GROUPS)
    sums[...] = jnp.broadcast_to(row, (8, W))
    pltpu.make_async_copy(tail, near, halo_sem.at[0]).wait()
    pltpu.make_async_copy(head, far, halo_sem.at[1]).wait()


def put_adjoint(adj, f, mine):
    zero = jnp.zeros((C, W), BF16)
    for h in range(H):
        for ki in range(3):
            source = h - ki + 1
            block = mine[source].astype(BF16) if 0 <= source < H else zero
            adj[ki * C : (ki + 1) * C, (f * H + h) * W : (f * H + h + 1) * W] = block


def prepare_kernel(lat, cot, gain, shift, blocks, adj, scales, lat_v, cot_v, gain_v, shift_v, tmp, sem):
    from_lat, from_cot, *small = copies(sem, (lat, lat_v), (cot, cot_v), (gain, gain_v), (shift, shift_v))
    from_lat.wait()
    for t in range(T):
        for h, block in enumerate(by_row(lat_v[t], tmp)):
            blocks[t * H + h] = block
    from_cot.wait()
    for t in range(T):
        put_adjoint(adj, t, by_row(cot_v[t], tmp))
    for copy in small:
        copy.wait()
    scales[0] = jnp.broadcast_to(channel_column(gain_v[...]), (C, W))
    scales[1] = jnp.broadcast_to(channel_column(shift_v[...]), (C, W))


def by_row(frame, tmp):
    tmp[...] = frame.astype(F32)
    return [tmp[pl.ds(h, C, stride=H), :] for h in range(H)]


def pick(condition, first, second):
    return jnp.where(condition, first.astype(F32), second.astype(F32))


def back_kernel(
    flags, lat, cot, near, far, kernel, totals, scales, scaled, sums, tmp, window, taps, lat_v, cot_v, kernel_v, scaled_v, sem
):
    from_cot, from_kernel, from_lat = copies(sem, (cot, cot_v), (kernel, kernel_v), (lat, lat_v))
    from_cot.wait()
    for f in range(T + HALO):
        blocks = by_row(cot_v[f] if f < T else pick(flags[1] == 0, near[f - T], far[f - T]), tmp)
        for h in range(H):
            for s, moved in enumerate(shifted(blocks[h])):
                at = (s * H + h) * C
                window[at : at + C, f * W : (f + 1) * W] = moved.astype(BF16)
    taps[...] = jnp.zeros_like(taps)
    from_kernel.wait()
    for kt in range(3):
        for ki in range(3):
            for kj in range(3):
                tap = kernel_v[9 * kt + 3 * ki + kj].astype(F32).T.astype(BF16)
                for h in range(H):
                    other = h + 1 - ki
                    if 0 <= other < H:
                        at = ((2 - kj) * H + other) * C
                        taps[2 - kt, h * C : (h + 1) * C, at : at + C] = tap
    back = jnp.dot(taps[0], window[:, 0 : T * W], preferred_element_type=F32)
    for f in range(1, 3):
        back = back + jnp.dot(taps[f], window[:, f * W : (f + T) * W], preferred_element_type=F32)
    center, inverse = center_inverse(totals, PER)
    from_lat.wait()
    first = jnp.zeros((C, W), F32)
    second = jnp.zeros((C, W), F32)
    for t in range(T):
        blocks = by_row(lat_v[t], tmp)
        for h in range(H):
            unit = (blocks[h] - center) * inverse
            normed = unit * scales[0] + scales[1]
            sig = 1.0 / (1.0 + jnp.exp(-normed))
            adjoint = back[h * C : (h + 1) * C, t * W : (t + 1) * W]
            value = adjoint * sig * (1.0 + normed * (1.0 - sig)) * scales[0]
            first = first + value
            second = second + value * unit
            scaled_v[t, pl.ds(h, C, stride=H), :] = value
    (to_scaled,) = copies(sem, (scaled_v, scaled))
    lane, sub = lanes(), rows()
    first = jnp.where(lane == sub // PER, jnp.sum(first, axis=1, keepdims=True), 0.0)
    second = jnp.where(lane == sub // PER + GROUPS, jnp.sum(second, axis=1, keepdims=True), 0.0)
    sums[...] = jnp.broadcast_to(jnp.sum(first + second, axis=0, keepdims=True), (8, W))
    to_scaled.wait()


def activated(block, center, inverse, scales):
    normed = (block - center) * inverse * scales[0] + scales[1]
    return (normed * (1.0 / (1.0 + jnp.exp(-normed)))).astype(BF16).astype(F32)


def grad_kernel(flags, blocks, near, far, adj, totals, scales, window, keep, send, tmp, flat, adj_v, window_v, sem):
    core = flags[1]
    center, inverse = center_inverse(totals, PER)
    for f in range(HALO):
        put_adjoint(adj_v, f, by_row(pick(core == 0, near[f], far[f]), tmp))
    for t in range(T):
        for h in range(H):
            for s, moved in enumerate(shifted(activated(blocks[t * H + h], center, inverse, scales))):
                moved = moved.astype(BF16)
                window_v[(s * H + h) * C : (s * H + h + 1) * C, t * W : (t + 1) * W] = moved
                flat[s * C : (s + 1) * C, (t * H + h) * W : (t * H + h + 1) * W] = moved
    (to_window,) = copies(sem, (window_v, window))
    contract = (((1,), (1,)), ((), ()))
    plane = H * W
    half = C // 2
    for kt in range(3):
        ahead = 2 - kt
        own = T - ahead
        grads = lax.dot_general(
            adj[:, ahead * plane :], flat[:, : own * plane], contract, preferred_element_type=F32
        )
        if ahead:
            grads = grads + lax.dot_general(
                adj_v[:, : ahead * plane], flat[:, own * plane :], contract, preferred_element_type=F32
            )
        for ki in range(3):
            for kj in range(3):
                tap = grads[ki * C : (ki + 1) * C, kj * C : (kj + 1) * C]
                low, high = tap[:half], tap[half:]
                at = (9 * kt + 3 * ki + kj) * half
                keep[at : at + half] = jnp.where(core == 0, low, high)
                send[at : at + half] = jnp.where(core == 0, high, low)
    keep[HALF:] = jnp.zeros((COMM - HALF, C), F32)
    send[HALF:] = jnp.zeros((COMM - HALF, C), F32)
    to_window.wait()


def add_kernel(keep, received, chip):
    chip[...] = (keep[...] + received[...]).astype(chip.dtype)


def part_kernel(parts, sums, packed):
    part = jnp.sum(parts[...].astype(F32), axis=0)
    for i in range(4):
        packed[i, :PART] = part
        packed[i, PART:] = sums[...]


def merge_kernel(flags, over_z, parts, backward):
    part = jnp.sum(over_z[:, :PART], axis=0).astype(BF16)
    for i in range(SIDE):
        parts[i] = part
    first = jnp.where(flags[2] == 0, over_z[0, PART:], over_z[1, PART:])
    second = jnp.where(flags[2] == 0, over_z[2, PART:], over_z[3, PART:])
    backward[...] = first + second


def place_kernel(flags, mine, other, grad):
    half = C // 2
    core = flags[1]
    for tap in range(27):
        a = mine[tap * half : (tap + 1) * half].astype(F32)
        b = other[tap * half : (tap + 1) * half].astype(F32)
        grad[tap, :half] = jnp.where(core == 0, a, b)
        grad[tap, half:] = jnp.where(core == 0, b, a)


def conv_kernel(
    flags, lat, near, far, kernel, window, totals, scales, output, tmp, taps, lat_v, kernel_v, window_v, sem
):
    from_kernel, from_window, from_lat = copies(
        sem, (kernel, kernel_v), (window, window_v.at[:, HALO * W :]), (lat, lat_v)
    )
    center, inverse = center_inverse(totals, PER)
    for f in range(HALO):
        blocks = by_row(pick(flags[1] == 0, far[f], near[f]), tmp)
        for h in range(H):
            active = jnp.where(flags[0] > 0, activated(blocks[h], center, inverse, scales), 0.0)
            for s, moved in enumerate(shifted(active)):
                window_v[(s * H + h) * C : (s * H + h + 1) * C, f * W : (f + 1) * W] = moved.astype(BF16)
    taps[...] = jnp.zeros_like(taps)
    from_kernel.wait()
    for kt in range(3):
        for ki in range(3):
            for kj in range(3):
                tap = kernel_v[9 * kt + 3 * ki + kj]
                for h in range(H):
                    other = h - 1 + ki
                    if 0 <= other < H:
                        at = (kj * H + other) * C
                        taps[kt, h * C : (h + 1) * C, at : at + C] = tap
    from_window.wait()
    total = jnp.dot(taps[0], window_v[:, 0 : T * W], preferred_element_type=F32)
    for f in range(1, 3):
        total = total + jnp.dot(taps[f], window_v[:, f * W : (f + T) * W], preferred_element_type=F32)
    from_lat.wait()
    for t in range(T):
        for h in range(H):
            tmp[pl.ds(h, C, stride=H), :] = total[h * C : (h + 1) * C, t * W : (t + 1) * W]
        output[t] = (lat_v[t].astype(F32) + tmp[...]).astype(BF16)


def adjoint_kernel(lat, cot, totals, backward, scaled, result, lat_v, cot_v, scaled_v, sem):
    started = copies(sem, (lat, lat_v), (cot, cot_v), (scaled, scaled_v))
    center, inverse = center_inverse(totals, PER * H)
    row = backward[...][0:1] / MEMBERS
    first = group_column(row, 0, PER * H)
    second = group_column(row, GROUPS, PER * H)
    for copy in started:
        copy.wait()
    for t in range(T):
        unit = (lat_v[t].astype(F32) - center) * inverse
        value = cot_v[t].astype(F32) + inverse * (scaled_v[t] - first - unit * second)
        result[t] = value.astype(BF16)


VMEM, HBM, SMEM = (
    pl.BlockSpec(memory_space=pltpu.VMEM),
    pl.BlockSpec(memory_space=pltpu.HBM),
    pl.BlockSpec(memory_space=pltpu.SMEM),
)


def call(body, out, scratch, *operands, far=(), out_far=(), scalars=0, flops=0, moved=1 << 20):
    single = not isinstance(out, tuple)
    count = 1 if single else len(out)
    outs = tuple(HBM if i in out_far else VMEM for i in range(count))
    shapes = tuple(pltpu.HBM(o.shape, o.dtype) if i in out_far else o for i, o in enumerate((out,) if single else out))
    operands = [pltpu.with_memory_space_constraint(x, pltpu.HBM) if i in far else x for i, x in enumerate(operands)]
    return pl.pallas_call(
        body,
        out_shape=shapes[0] if single else shapes,
        in_specs=[SMEM if i < scalars else HBM if i in far else VMEM for i in range(len(operands))],
        out_specs=outs[0] if single else outs,
        scratch_shapes=scratch,
        compiler_params=LIMIT,
        cost_estimate=pl.CostEstimate(flops=flops, bytes_accessed=moved, transcendentals=0),
    )(*operands)


def shape(*dims, dtype=F32):
    return jax.ShapeDtypeStruct(dims, dtype)


def sems(count):
    return pltpu.SemaphoreType.DMA((count,))


def swap(value, axis):
    return lax.ppermute(value, axis, [(0, 1), (1, 0)])


def exchange(parts, axes):
    return lax.all_to_all(parts, axes, 0, 0)


def per_device(latents, norm_gain, norm_shift, kernel, cotangent):
    lat = latents.reshape(T, ROWS, W)
    cot = cotangent.reshape(T, ROWS, W)
    gain, shift = norm_gain.reshape(1, C), norm_shift.reshape(1, C)
    zh, zm, core = (lax.axis_index(axis) for axis in ("zh", "zm", "core"))
    flags = jnp.stack([zh * 2 + core, core, zm]).astype(jnp.int32)
    halo = shape(HALO, ROWS, W, dtype=BF16)
    frames = pltpu.VMEM((T, ROWS, W), BF16)
    tmp = pltpu.VMEM((ROWS, W), F32)
    row = pltpu.VMEM((1, C), F32)
    window_scratch = pltpu.VMEM((3 * ROWS, (T + HALO) * W), BF16)
    taps = pltpu.VMEM((3, ROWS, 3 * ROWS), BF16)
    kernel_scratch = pltpu.VMEM((27, C, C), BF16)
    scaled_scratch = pltpu.VMEM((T, ROWS, W), F32)
    own, to_near, to_far = call(
        start_kernel,
        (shape(8, W), halo, halo),
        [frames, sems(2), sems(2)],
        flags,
        lat,
        cot,
        far=(1, 2),
        scalars=1,
    )
    blocks, adj, scales = call(
        prepare_kernel,
        (shape(T * H, C, W), shape(3 * C, T * H * W, dtype=BF16), shape(2, C, W)),
        [frames, frames, row, row, tmp, sems(4)],
        lat,
        cot,
        gain,
        shift,
        far=(0, 1, 2, 3),
    )
    far = lax.ppermute(to_far, ("zh", "core"), [(1, 2), (2, 1)])
    across, blocks = lax.optimization_barrier((swap(own, "zh"), blocks))
    pair = own + across
    near = swap(to_near, "core")
    totals = jnp.concatenate([pair, swap(pair, "core")], axis=0)
    window, keep, send = call(
        grad_kernel,
        (shape(3 * ROWS, T * W, dtype=BF16), shape(COMM, C), shape(COMM, C)),
        [
            tmp,
            pltpu.VMEM((3 * C, T * H * W), BF16),
            pltpu.VMEM((3 * C, HALO * H * W), BF16),
            pltpu.VMEM((3 * ROWS, T * W), BF16),
            sems(1),
        ],
        flags,
        blocks,
        near,
        far,
        adj,
        totals,
        scales,
        out_far=(0,),
        scalars=1,
        flops=4 * 10**9,
    )
    chip = call(add_kernel, shape(COMM, C, dtype=WIRE), [], keep, swap(send, "core"))
    parts = exchange(chip.reshape(SIDE, PART, C), ("y", "zn", "x"))
    scaled, sums = call(
        back_kernel,
        (shape(T, ROWS, W), shape(8, W)),
        [tmp, window_scratch, taps, frames, frames, kernel_scratch, scaled_scratch, sems(3)],
        flags,
        lat,
        cot,
        near,
        far,
        kernel,
        totals,
        scales,
        far=(1, 2, 5),
        out_far=(0,),
        scalars=1,
        flops=4 * 10**9,
    )
    sums = sums + swap(sums, "core")
    packed = call(part_kernel, shape(4, PART + 8, C), [], parts, sums)
    over_z = exchange(packed, ("zh", "zm"))
    part, backward = call(
        merge_kernel, (shape(SIDE, PART, C, dtype=BF16), shape(8, C)), [], flags, over_z, scalars=1
    )
    part, window = lax.optimization_barrier((part, window))
    mine = exchange(part, ("y", "zn", "x")).reshape(COMM, C)
    output = call(
        conv_kernel,
        shape(T, ROWS, W, dtype=BF16),
        [tmp, taps, frames, kernel_scratch, window_scratch, sems(3)],
        flags,
        lat,
        near,
        far,
        kernel,
        window,
        totals,
        scales,
        far=(1, 4, 5),
        scalars=1,
        flops=4 * 10**9,
    )
    mine, output = lax.optimization_barrier((mine, output))
    other = swap(mine, "core")
    result = call(
        adjoint_kernel,
        shape(T, ROWS, W, dtype=BF16),
        [frames, frames, scaled_scratch, sems(3)],
        lat,
        cot,
        totals,
        backward,
        scaled,
        far=(0, 1, 4),
        flops=10**9,
    )
    kernel_grad = call(place_kernel, shape(27, C, C), [], flags, mine, other, scalars=1)
    return output.reshape(latents.shape), result.reshape(latents.shape), kernel_grad


WIRE = F32


def solution(mesh):
    fine = Mesh(mesh.devices.reshape(2, 2, 4, 2, 2, 4), ("zh", "core", "y", "zm", "zn", "x"))
    frames = P(("y", "zm", "zn", "x"), ("zh", "core"), None, None, None)
    return jax.shard_map(
        per_device,
        mesh=fine,
        in_specs=(frames, P(), P(), P(), frames),
        out_specs=(frames, frames, P()),
        check_vma=False,
    )
```

```python
import functools

import jax
import jax.numpy as jnp
from jax import lax
from jax.experimental import pallas as pl
from jax.experimental.pallas import tpu as pltpu
from jax.sharding import Mesh
from jax.sharding import PartitionSpec as P

C = 128
H = 4
W = 128
T = 4
HALO = 2
GROUPS = 32
PER = C // GROUPS
SLABS = 4
MEMBERS = SLABS * T * PER * H * W
ROWS = H * C
HALF = 27 * (C // 2)
COMM = HALF + 64
SIDE = 32
PART = COMM // SIDE
F32 = jnp.float32
BF16 = jnp.bfloat16
MIB = 1024 * 1024


def lanes():
    return lax.broadcasted_iota(jnp.int32, (C, W), 1)


def rows():
    return lax.broadcasted_iota(jnp.int32, (C, W), 0)


def shifted(block):
    left = jnp.where(lanes() == 0, 0.0, pltpu.roll(block, 1, 1))
    right = jnp.where(lanes() == W - 1, 0.0, pltpu.roll(block, W - 1, 1))
    return left, block, right


def row_of(column, offset):
    lane = lax.broadcasted_iota(jnp.int32, (GROUPS, W), 1)
    sub = lax.broadcasted_iota(jnp.int32, (GROUPS, W), 0)
    return jnp.sum(jnp.where(lane == sub + offset, column, 0.0), axis=0, keepdims=True)


def channel_column(row):
    return jnp.sum(jnp.where(lanes() == rows(), row, 0.0), axis=1, keepdims=True)


def group_column(row, offset, per_channel):
    lane = lax.broadcasted_iota(jnp.int32, (GROUPS * per_channel, W), 1)
    sub = lax.broadcasted_iota(jnp.int32, (GROUPS * per_channel, W), 0)
    return jnp.sum(jnp.where(lane == sub // per_channel + offset, row, 0.0), axis=1, keepdims=True)


def center_inverse(totals, per_channel):
    row = jnp.sum(totals[...].reshape(-1, 8, W), axis=0)[0:1] / MEMBERS
    center = group_column(row, 0, per_channel)
    square = group_column(row, GROUPS, per_channel)
    return center, lax.rsqrt(square - center * center + 1e-06)


def copies(sem, *pairs):
    started = [pltpu.make_async_copy(source, target, sem.at[i]) for i, (source, target) in enumerate(pairs)]
    for copy in started:
        copy.start()
    return started


def start_kernel(lat, sums, lat_v, sem):
    parts = copies(sem, *((lat.at[t], lat_v.at[t]) for t in range(T)))
    total = jnp.zeros((ROWS, W), F32)
    square = jnp.zeros((ROWS, W), F32)
    for t in range(T):
        parts[t].wait()
        x = lat_v[t].astype(F32)
        total = total + x
        square = square + x * x
    total = jnp.sum(jnp.sum(total.reshape(GROUPS, -1, W), axis=1), axis=1, keepdims=True)
    square = jnp.sum(jnp.sum(square.reshape(GROUPS, -1, W), axis=1), axis=1, keepdims=True)
    row = row_of(total, 0) + row_of(square, GROUPS)
    sums[...] = jnp.broadcast_to(row, (8, W))


def put_adjoint(adj, f, mine):
    zero = jnp.zeros((C, W), BF16)
    for h in range(H):
        for ki in range(3):
            source = h - ki + 1
            block = mine[source].astype(BF16) if 0 <= source < H else zero
            adj[ki * C : (ki + 1) * C, (f * H + h) * W : (f * H + h + 1) * W] = block


def prepare_kernel(lat, cot, gain, shift, adj, scales, head, tail, lat_v, cot_v, gain_v, shift_v, tmp, sem):
    from_lat, from_cot, *small = copies(
        sem,
        (lat, lat_v),
        (cot, cot_v),
        (gain, gain_v),
        (shift, shift_v),
        (cot.at[:HALO], head),
        (lat.at[T - HALO :], tail),
    )
    from_lat.wait()
    for t in range(T):
        for h, block in enumerate(by_row(lat_v[t], tmp)):
            adj[3 * C :, (t * H + h) * W : (t * H + h + 1) * W] = block.astype(BF16)
    from_cot.wait()
    for t in range(T):
        put_adjoint(adj, t, by_row(cot_v[t], tmp))
    for copy in small:
        copy.wait()
    scales[0] = jnp.broadcast_to(channel_column(gain_v[...]), (C, W))
    scales[1] = jnp.broadcast_to(channel_column(shift_v[...]), (C, W))


def by_row(frame, tmp):
    tmp[...] = frame.astype(F32)
    return [tmp[pl.ds(h, C, stride=H), :] for h in range(H)]


def back_kernel(
    lat, cot, following, kernel, totals, scales, scaled, sums, tmp, window, taps, lat_v, cot_v, kernel_v, scaled_v, sem
):
    from_cot, from_kernel, from_lat = copies(sem, (cot, cot_v), (kernel, kernel_v), (lat, lat_v))
    from_cot.wait()
    for f in range(T + HALO):
        blocks = by_row(cot_v[f] if f < T else following[f - T], tmp)
        for h in range(H):
            for s, moved in enumerate(shifted(blocks[h])):
                at = (s * H + h) * C
                window[at : at + C, f * W : (f + 1) * W] = moved.astype(BF16)
    taps[...] = jnp.zeros_like(taps)
    from_kernel.wait()
    for kt in range(3):
        for ki in range(3):
            for kj in range(3):
                tap = kernel_v[9 * kt + 3 * ki + kj].astype(F32).T.astype(BF16)
                for h in range(H):
                    other = h + 1 - ki
                    if 0 <= other < H:
                        at = ((2 - kj) * H + other) * C
                        taps[2 - kt, h * C : (h + 1) * C, at : at + C] = tap
    back = jnp.dot(taps[0], window[:, 0 : T * W], preferred_element_type=F32)
    for f in range(1, 3):
        back = back + jnp.dot(taps[f], window[:, f * W : (f + T) * W], preferred_element_type=F32)
    center, inverse = center_inverse(totals, PER)
    from_lat.wait()
    first = jnp.zeros((C, W), F32)
    second = jnp.zeros((C, W), F32)
    for t in range(T):
        blocks = by_row(lat_v[t], tmp)
        for h in range(H):
            unit = (blocks[h] - center) * inverse
            normed = unit * scales[0] + scales[1]
            sig = 1.0 / (1.0 + jnp.exp(-normed))
            adjoint = back[h * C : (h + 1) * C, t * W : (t + 1) * W]
            value = adjoint * sig * (1.0 + normed * (1.0 - sig)) * scales[0]
            first = first + value
            second = second + value * unit
            scaled_v[t, pl.ds(h, C, stride=H), :] = value
    (to_scaled,) = copies(sem, (scaled_v, scaled))
    lane, sub = lanes(), rows()
    first = jnp.where(lane == sub // PER, jnp.sum(first, axis=1, keepdims=True), 0.0)
    second = jnp.where(lane == sub // PER + GROUPS, jnp.sum(second, axis=1, keepdims=True), 0.0)
    sums[...] = jnp.broadcast_to(jnp.sum(first + second, axis=0, keepdims=True), (8, W))
    to_scaled.wait()


def activated(block, center, inverse, scales):
    normed = (block - center) * inverse * scales[0] + scales[1]
    return (normed * (1.0 / (1.0 + jnp.exp(-normed)))).astype(BF16).astype(F32)


CONTRACT = (((1,), (1,)), ((), ()))
PLANE = H * W


def halves(core, grads):
    half = C // 2
    for ki in range(3):
        for kj in range(3):
            tap = grads[ki * C : (ki + 1) * C, kj * C : (kj + 1) * C]
            low, high = tap[:half], tap[half:]
            at = (3 * ki + kj) * half
            yield at, jnp.where(core == 0, low, high), jnp.where(core == 0, high, low)


def grad_kernel(flags, adj, totals, scales, window, keep, send, last, flat, window_v, sem):
    center, inverse = center_inverse(totals, PER)
    for t in range(T):
        for h in range(H):
            block = adj[3 * C :, (t * H + h) * W : (t * H + h + 1) * W].astype(F32)
            for s, moved in enumerate(shifted(activated(block, center, inverse, scales))):
                moved = moved.astype(BF16)
                window_v[(s * H + h) * C : (s * H + h + 1) * C, t * W : (t + 1) * W] = moved
                flat[s * C : (s + 1) * C, (t * H + h) * W : (t * H + h + 1) * W] = moved
                if t >= T - HALO:
                    at = ((t - T + HALO) * H + h) * W
                    last[s * C : (s + 1) * C, at : at + W] = moved
    (to_window,) = copies(sem, (window_v, window))
    for kt in range(3):
        ahead = 2 - kt
        grads = lax.dot_general(
            adj[: 3 * C, ahead * PLANE :], flat[:, : (T - ahead) * PLANE], CONTRACT, preferred_element_type=F32
        )
        for at, mine, other in halves(flags[1], grads):
            at += 9 * kt * (C // 2)
            keep[at : at + C // 2] = mine
            send[at : at + C // 2] = other
    keep[HALF:] = jnp.zeros((COMM - HALF, C), F32)
    send[HALF:] = jnp.zeros((COMM - HALF, C), F32)
    to_window.wait()


def edge_kernel(flags, keep_in, send_in, following, last, keep, send, tmp, adj):
    for f in range(HALO):
        put_adjoint(adj, f, by_row(following[f], tmp))
    for kt in range(2):
        ahead = 2 - kt
        grads = lax.dot_general(
            adj[:, : ahead * PLANE], last[:, (HALO - ahead) * PLANE :], CONTRACT, preferred_element_type=F32
        )
        for at, mine, other in halves(flags[1], grads):
            at += 9 * kt * (C // 2)
            keep[at : at + C // 2] = keep_in[at : at + C // 2] + mine
            send[at : at + C // 2] = send_in[at : at + C // 2] + other


def add_kernel(keep, received, chip):
    chip[...] = (keep[...] + received[...]).astype(chip.dtype)


def part_kernel(parts, sums, packed):
    part = jnp.sum(parts[...].astype(F32), axis=0)
    for i in range(4):
        packed[i, :PART] = part
        packed[i, PART:] = sums[...]


def merge_kernel(flags, over_z, parts, backward):
    part = jnp.sum(over_z[:, :PART], axis=0).astype(BF16)
    for i in range(SIDE):
        parts[i] = part
    first = jnp.where(flags[2] == 0, over_z[0, PART:], over_z[1, PART:])
    second = jnp.where(flags[2] == 0, over_z[2, PART:], over_z[3, PART:])
    backward[...] = first + second


def place_kernel(flags, mine, other, grad):
    half = C // 2
    core = flags[1]
    for tap in range(27):
        a = mine[tap * half : (tap + 1) * half].astype(F32)
        b = other[tap * half : (tap + 1) * half].astype(F32)
        grad[tap, :half] = jnp.where(core == 0, a, b)
        grad[tap, half:] = jnp.where(core == 0, b, a)


def conv_kernel(
    flags, lat, previous, kernel, window, totals, scales, output, tmp, taps, lat_v, kernel_v, window_v, sem
):
    from_kernel, from_window, from_lat = copies(
        sem, (kernel, kernel_v), (window, window_v.at[:, HALO * W :]), (lat, lat_v)
    )
    center, inverse = center_inverse(totals, PER)
    for f in range(HALO):
        blocks = by_row(previous[f], tmp)
        for h in range(H):
            active = jnp.where(flags[0] > 0, activated(blocks[h], center, inverse, scales), 0.0)
            for s, moved in enumerate(shifted(active)):
                window_v[(s * H + h) * C : (s * H + h + 1) * C, f * W : (f + 1) * W] = moved.astype(BF16)
    taps[...] = jnp.zeros_like(taps)
    from_kernel.wait()
    for kt in range(3):
        for ki in range(3):
            for kj in range(3):
                tap = kernel_v[9 * kt + 3 * ki + kj]
                for h in range(H):
                    other = h - 1 + ki
                    if 0 <= other < H:
                        at = (kj * H + other) * C
                        taps[kt, h * C : (h + 1) * C, at : at + C] = tap
    from_window.wait()
    total = jnp.dot(taps[0], window_v[:, 0 : T * W], preferred_element_type=F32)
    for f in range(1, 3):
        total = total + jnp.dot(taps[f], window_v[:, f * W : (f + T) * W], preferred_element_type=F32)
    from_lat.wait()
    for t in range(T):
        for h in range(H):
            tmp[pl.ds(h, C, stride=H), :] = total[h * C : (h + 1) * C, t * W : (t + 1) * W]
        output[t] = (lat_v[t].astype(F32) + tmp[...]).astype(BF16)


def adjoint_kernel(lat, cot, totals, backward, scaled, result, lat_v, cot_v, scaled_v, sem):
    started = copies(sem, (lat, lat_v), (cot, cot_v), (scaled, scaled_v))
    center, inverse = center_inverse(totals, PER * H)
    row = backward[...][0:1] / MEMBERS
    first = group_column(row, 0, PER * H)
    second = group_column(row, GROUPS, PER * H)
    for copy in started:
        copy.wait()
    for t in range(T):
        unit = (lat_v[t].astype(F32) - center) * inverse
        value = cot_v[t].astype(F32) + inverse * (scaled_v[t] - first - unit * second)
        result[t] = value.astype(BF16)


VMEM, HBM, SMEM = (
    pl.BlockSpec(memory_space=pltpu.VMEM),
    pl.BlockSpec(memory_space=pltpu.HBM),
    pl.BlockSpec(memory_space=pltpu.SMEM),
)


def call(body, out, scratch, *operands, far=(), out_far=(), scalars=0, flops=0, moved=1 << 20, aliases=(), limit=12):
    single = not isinstance(out, tuple)
    count = 1 if single else len(out)
    outs = tuple(HBM if i in out_far else VMEM for i in range(count))
    shapes = tuple(pltpu.HBM(o.shape, o.dtype) if i in out_far else o for i, o in enumerate((out,) if single else out))
    operands = [pltpu.with_memory_space_constraint(x, pltpu.HBM) if i in far else x for i, x in enumerate(operands)]
    return pl.pallas_call(
        body,
        out_shape=shapes[0] if single else shapes,
        in_specs=[SMEM if i < scalars else HBM if i in far else VMEM for i in range(len(operands))],
        out_specs=outs[0] if single else outs,
        scratch_shapes=scratch,
        compiler_params=pltpu.CompilerParams(vmem_limit_bytes=limit * MIB),
        input_output_aliases=dict(aliases),
        cost_estimate=pl.CostEstimate(flops=flops, bytes_accessed=moved, transcendentals=0),
    )(*operands)


def shape(*dims, dtype=F32):
    return jax.ShapeDtypeStruct(dims, dtype)


def sems(count):
    return pltpu.SemaphoreType.DMA((count,))


def swap(value, axis):
    return lax.ppermute(value, axis, [(0, 1), (1, 0)])


def exchange(parts, axes):
    return lax.all_to_all(parts, axes, 0, 0)


def per_device(latents, norm_gain, norm_shift, kernel, cotangent):
    lat = latents.reshape(T, ROWS, W)
    cot = cotangent.reshape(T, ROWS, W)
    gain, shift = norm_gain.reshape(1, C), norm_shift.reshape(1, C)
    zh, zm, core = (lax.axis_index(axis) for axis in ("zh", "zm", "core"))
    flags = jnp.stack([zh * 2 + core, core, zm]).astype(jnp.int32)
    slab = ("zh", "core")
    halo = shape(HALO, ROWS, W, dtype=BF16)
    frames = pltpu.VMEM((T, ROWS, W), BF16)
    tmp = pltpu.VMEM((ROWS, W), F32)
    row = pltpu.VMEM((1, C), F32)
    window_scratch = pltpu.VMEM((3 * ROWS, (T + HALO) * W), BF16)
    taps = pltpu.VMEM((3, ROWS, 3 * ROWS), BF16)
    kernel_scratch = pltpu.VMEM((27, C, C), BF16)
    scaled_scratch = pltpu.VMEM((T, ROWS, W), F32)
    own = call(start_kernel, shape(8, W), [frames, sems(T)], lat, far=(0,))
    adj, scales, head, tail = call(
        prepare_kernel,
        (shape(4 * C, T * PLANE, dtype=BF16), shape(2, C, W), halo, halo),
        [frames, frames, row, row, tmp, sems(6)],
        lat,
        cot,
        gain,
        shift,
        far=(0, 1, 2, 3),
        out_far=(3,),
    )
    across, scales = lax.optimization_barrier((swap(own, "zh"), scales))
    pair = own + across
    following = lax.ppermute(head, slab, [(i + 1, i) for i in range(SLABS - 1)])
    totals = jnp.concatenate([pair, swap(pair, "core")], axis=0)
    window, keep, send, last = call(
        grad_kernel,
        (
            shape(3 * ROWS, T * W, dtype=BF16),
            shape(COMM, C),
            shape(COMM, C),
            shape(3 * C, HALO * PLANE, dtype=BF16),
        ),
        [pltpu.VMEM((3 * C, T * PLANE), BF16), pltpu.VMEM((3 * ROWS, T * W), BF16), sems(1)],
        flags,
        adj,
        totals,
        scales,
        out_far=(0,),
        scalars=1,
        flops=4 * 10**9,
    )
    following, last = lax.optimization_barrier((following, last))
    keep, send = call(
        edge_kernel,
        (shape(COMM, C), shape(COMM, C)),
        [tmp, pltpu.VMEM((3 * C, HALO * PLANE), BF16)],
        flags,
        keep,
        send,
        following,
        last,
        scalars=1,
        aliases=((1, 0), (2, 1)),
    )
    chip = call(add_kernel, shape(COMM, C, dtype=WIRE), [], keep, swap(send, "core"))
    parts = exchange(chip.reshape(SIDE, PART, C), ("y", "zn", "x"))
    scaled, sums = call(
        back_kernel,
        (shape(T, ROWS, W), shape(8, W)),
        [tmp, window_scratch, taps, frames, frames, kernel_scratch, scaled_scratch, sems(3)],
        lat,
        cot,
        following,
        kernel,
        totals,
        scales,
        far=(0, 1, 3),
        out_far=(0,),
        limit=20,
        flops=4 * 10**9,
    )
    sums, tail = lax.optimization_barrier((sums, tail))
    previous = lax.ppermute(tail, slab, [(i, i + 1) for i in range(SLABS - 1)])
    sums = sums + swap(sums, "core")
    packed = call(part_kernel, shape(4, PART + 8, C), [], parts, sums)
    over_z, previous = lax.optimization_barrier((exchange(packed, ("zh", "zm")), previous))
    part, backward = call(
        merge_kernel, (shape(SIDE, PART, C, dtype=BF16), shape(8, C)), [], flags, over_z, scalars=1
    )
    part, window = lax.optimization_barrier((part, window))
    mine = exchange(part, ("y", "zn", "x")).reshape(COMM, C)
    output = call(
        conv_kernel,
        shape(T, ROWS, W, dtype=BF16),
        [tmp, taps, frames, kernel_scratch, window_scratch, sems(3)],
        flags,
        lat,
        previous,
        kernel,
        window,
        totals,
        scales,
        far=(1, 3, 4),
        limit=20,
        scalars=1,
        flops=4 * 10**9,
    )
    mine, output = lax.optimization_barrier((mine, output))
    other = swap(mine, "core")
    result = call(
        adjoint_kernel,
        shape(T, ROWS, W, dtype=BF16),
        [frames, frames, scaled_scratch, sems(3)],
        lat,
        cot,
        totals,
        backward,
        scaled,
        far=(0, 1, 4),
        flops=10**9,
    )
    kernel_grad = call(place_kernel, shape(27, C, C), [], flags, mine, other, scalars=1)
    return output.reshape(latents.shape), result.reshape(latents.shape), kernel_grad


WIRE = F32


def solution(mesh):
    fine = Mesh(mesh.devices.reshape(2, 2, 4, 2, 2, 4), ("zh", "core", "y", "zm", "zn", "x"))
    frames = P(("y", "zm", "zn", "x"), ("zh", "core"), None, None, None)
    return jax.shard_map(
        per_device,
        mesh=fine,
        in_specs=(frames, P(), P(), P(), frames),
        out_specs=(frames, frames, P()),
        check_vma=False,
    )
```

```python
import functools

import jax
import jax.numpy as jnp
from jax import lax
from jax.experimental import pallas as pl
from jax.experimental.pallas import tpu as pltpu
from jax.sharding import Mesh
from jax.sharding import PartitionSpec as P

C = 128
H = 4
W = 128
T = 4
HALO = 2
GROUPS = 32
PER = C // GROUPS
SLABS = 4
MEMBERS = SLABS * T * PER * H * W
ROWS = H * C
HALF = 27 * (C // 2)
COMM = HALF + 64
SIDE = 32
PART = COMM // SIDE
F32 = jnp.float32
BF16 = jnp.bfloat16
MIB = 1024 * 1024


def lanes():
    return lax.broadcasted_iota(jnp.int32, (C, W), 1)


def rows():
    return lax.broadcasted_iota(jnp.int32, (C, W), 0)


def shifted(block):
    left = jnp.where(lanes() == 0, 0.0, pltpu.roll(block, 1, 1))
    right = jnp.where(lanes() == W - 1, 0.0, pltpu.roll(block, W - 1, 1))
    return left, block, right


def row_of(column, offset):
    lane = lax.broadcasted_iota(jnp.int32, (GROUPS, W), 1)
    sub = lax.broadcasted_iota(jnp.int32, (GROUPS, W), 0)
    return jnp.sum(jnp.where(lane == sub + offset, column, 0.0), axis=0, keepdims=True)


def channel_column(row):
    return jnp.sum(jnp.where(lanes() == rows(), row, 0.0), axis=1, keepdims=True)


def group_column(row, offset, per_channel):
    lane = lax.broadcasted_iota(jnp.int32, (GROUPS * per_channel, W), 1)
    sub = lax.broadcasted_iota(jnp.int32, (GROUPS * per_channel, W), 0)
    return jnp.sum(jnp.where(lane == sub // per_channel + offset, row, 0.0), axis=1, keepdims=True)


def center_inverse(totals, per_channel):
    row = jnp.sum(totals[...].reshape(-1, 8, W), axis=0)[0:1] / MEMBERS
    center = group_column(row, 0, per_channel)
    square = group_column(row, GROUPS, per_channel)
    return center, lax.rsqrt(square - center * center + 1e-06)


def copies(sem, *pairs):
    started = [pltpu.make_async_copy(source, target, sem.at[i]) for i, (source, target) in enumerate(pairs)]
    for copy in started:
        copy.start()
    return started


def start_kernel(lat, sums, lat_v, sem):
    parts = copies(sem, *((lat.at[t], lat_v.at[t]) for t in range(T)))
    total = jnp.zeros((ROWS, W), F32)
    square = jnp.zeros((ROWS, W), F32)
    for t in range(T):
        parts[t].wait()
        x = lat_v[t].astype(F32)
        total = total + x
        square = square + x * x
    total = jnp.sum(jnp.sum(total.reshape(GROUPS, -1, W), axis=1), axis=1, keepdims=True)
    square = jnp.sum(jnp.sum(square.reshape(GROUPS, -1, W), axis=1), axis=1, keepdims=True)
    row = row_of(total, 0) + row_of(square, GROUPS)
    sums[...] = jnp.broadcast_to(row, (8, W))


def put_adjoint(adj, f, mine):
    zero = jnp.zeros((C, W), BF16)
    for h in range(H):
        for ki in range(3):
            source = h - ki + 1
            block = mine[source].astype(BF16) if 0 <= source < H else zero
            adj[ki * C : (ki + 1) * C, (f * H + h) * W : (f * H + h + 1) * W] = block


def prepare_kernel(lat, cot, gain, shift, adj, scales, head, tail, lat_v, cot_v, gain_v, shift_v, tmp, sem, tail_sem):
    from_lat, from_cot, *small = copies(
        sem,
        (lat, lat_v),
        (cot, cot_v),
        (gain, gain_v),
        (shift, shift_v),
        (cot.at[:HALO], head),
    )
    from_lat.wait()
    (to_tail,) = copies(tail_sem, (lat_v.at[T - HALO :], tail))
    for t in range(T):
        for h, block in enumerate(by_row(lat_v[t], tmp)):
            adj[3 * C :, (t * H + h) * W : (t * H + h + 1) * W] = block.astype(BF16)
    from_cot.wait()
    for t in range(T):
        put_adjoint(adj, t, by_row(cot_v[t], tmp))
    for copy in small:
        copy.wait()
    scales[0] = jnp.broadcast_to(channel_column(gain_v[...]), (C, W))
    scales[1] = jnp.broadcast_to(channel_column(shift_v[...]), (C, W))
    to_tail.wait()


def by_row(frame, tmp):
    tmp[...] = frame.astype(F32)
    return [tmp[pl.ds(h, C, stride=H), :] for h in range(H)]


def back_kernel(
    lat, cot, following, kernel, totals, scales, scaled, sums, tmp, window, taps, lat_v, cot_v, kernel_v, scaled_v, sem
):
    from_cot, from_kernel, from_lat = copies(sem, (cot, cot_v), (kernel, kernel_v), (lat, lat_v))
    from_cot.wait()
    for f in range(T + HALO):
        blocks = by_row(cot_v[f] if f < T else following[f - T], tmp)
        for h in range(H):
            for s, moved in enumerate(shifted(blocks[h])):
                at = (s * H + h) * C
                window[at : at + C, f * W : (f + 1) * W] = moved.astype(BF16)
    taps[...] = jnp.zeros_like(taps)
    from_kernel.wait()
    for kt in range(3):
        for ki in range(3):
            for kj in range(3):
                tap = kernel_v[9 * kt + 3 * ki + kj].astype(F32).T.astype(BF16)
                for h in range(H):
                    other = h + 1 - ki
                    if 0 <= other < H:
                        at = ((2 - kj) * H + other) * C
                        taps[2 - kt, h * C : (h + 1) * C, at : at + C] = tap
    back = jnp.dot(taps[0], window[:, 0 : T * W], preferred_element_type=F32)
    for f in range(1, 3):
        back = back + jnp.dot(taps[f], window[:, f * W : (f + T) * W], preferred_element_type=F32)
    center, inverse = center_inverse(totals, PER)
    from_lat.wait()
    first = jnp.zeros((C, W), F32)
    second = jnp.zeros((C, W), F32)
    for t in range(T):
        blocks = by_row(lat_v[t], tmp)
        for h in range(H):
            unit = (blocks[h] - center) * inverse
            normed = unit * scales[0] + scales[1]
            sig = 1.0 / (1.0 + jnp.exp(-normed))
            adjoint = back[h * C : (h + 1) * C, t * W : (t + 1) * W]
            value = adjoint * sig * (1.0 + normed * (1.0 - sig)) * scales[0]
            first = first + value
            second = second + value * unit
            scaled_v[t, pl.ds(h, C, stride=H), :] = value
    (to_scaled,) = copies(sem, (scaled_v, scaled))
    lane, sub = lanes(), rows()
    first = jnp.where(lane == sub // PER, jnp.sum(first, axis=1, keepdims=True), 0.0)
    second = jnp.where(lane == sub // PER + GROUPS, jnp.sum(second, axis=1, keepdims=True), 0.0)
    sums[...] = jnp.broadcast_to(jnp.sum(first + second, axis=0, keepdims=True), (8, W))
    to_scaled.wait()


def activated(block, center, inverse, scales):
    normed = (block - center) * inverse * scales[0] + scales[1]
    return (normed * (1.0 / (1.0 + jnp.exp(-normed)))).astype(BF16).astype(F32)


CONTRACT = (((1,), (1,)), ((), ()))
PLANE = H * W


def halves(core, grads):
    half = C // 2
    for ki in range(3):
        for kj in range(3):
            tap = grads[ki * C : (ki + 1) * C, kj * C : (kj + 1) * C]
            low, high = tap[:half], tap[half:]
            at = (3 * ki + kj) * half
            yield at, jnp.where(core == 0, low, high), jnp.where(core == 0, high, low)


def grad_kernel(flags, adj, totals, scales, window, keep, send, last, flat, window_v, sem):
    center, inverse = center_inverse(totals, PER)
    for t in range(T):
        for h in range(H):
            block = adj[3 * C :, (t * H + h) * W : (t * H + h + 1) * W].astype(F32)
            for s, moved in enumerate(shifted(activated(block, center, inverse, scales))):
                moved = moved.astype(BF16)
                window_v[(s * H + h) * C : (s * H + h + 1) * C, t * W : (t + 1) * W] = moved
                flat[s * C : (s + 1) * C, (t * H + h) * W : (t * H + h + 1) * W] = moved
                if t >= T - HALO:
                    at = ((t - T + HALO) * H + h) * W
                    last[s * C : (s + 1) * C, at : at + W] = moved
    (to_window,) = copies(sem, (window_v, window))
    for kt in range(3):
        ahead = 2 - kt
        grads = lax.dot_general(
            adj[: 3 * C, ahead * PLANE :], flat[:, : (T - ahead) * PLANE], CONTRACT, preferred_element_type=F32
        )
        for at, mine, other in halves(flags[1], grads):
            at += 9 * kt * (C // 2)
            keep[at : at + C // 2] = mine
            send[at : at + C // 2] = other
    keep[HALF:] = jnp.zeros((COMM - HALF, C), F32)
    send[HALF:] = jnp.zeros((COMM - HALF, C), F32)
    to_window.wait()


def edge_kernel(flags, keep_in, send_in, following, last, keep, send, tmp, adj):
    for f in range(HALO):
        put_adjoint(adj, f, by_row(following[f], tmp))
    for kt in range(2):
        ahead = 2 - kt
        grads = lax.dot_general(
            adj[:, : ahead * PLANE], last[:, (HALO - ahead) * PLANE :], CONTRACT, preferred_element_type=F32
        )
        for at, mine, other in halves(flags[1], grads):
            at += 9 * kt * (C // 2)
            keep[at : at + C // 2] = keep_in[at : at + C // 2] + mine
            send[at : at + C // 2] = send_in[at : at + C // 2] + other


def add_kernel(keep, received, chip):
    chip[...] = (keep[...] + received[...]).astype(chip.dtype)


def part_kernel(parts, sums, packed):
    part = jnp.sum(parts[...].astype(F32), axis=0)
    for i in range(4):
        packed[i, :PART] = part
        packed[i, PART:] = sums[...]


def merge_kernel(flags, over_z, parts, backward):
    part = jnp.sum(over_z[:, :PART], axis=0).astype(BF16)
    for i in range(SIDE):
        parts[i] = part
    first = jnp.where(flags[2] == 0, over_z[0, PART:], over_z[1, PART:])
    second = jnp.where(flags[2] == 0, over_z[2, PART:], over_z[3, PART:])
    backward[...] = first + second


def place_kernel(flags, half_grad, grad, grad_v, sem, first):
    half = C // 2
    core = flags[1] if first else 1 - flags[1]
    at = pl.multiple_of(core * half, half)
    started = []
    for kt in range(3):
        rows_of = half_grad[9 * kt * half : 9 * (kt + 1) * half].astype(F32)
        grad_v[9 * kt : 9 * (kt + 1)] = rows_of.reshape(9, half, C)
        taps = pl.ds(9 * kt, 9)
        started += copies(sem.at[pl.ds(kt, 1)], (grad_v.at[taps], grad.at[taps, pl.ds(at, half)]))
    for copy in started:
        copy.wait()


def place_first(flags, half_grad, grad, grad_v, sem):
    place_kernel(flags, half_grad, grad, grad_v, sem, True)


def place_second(flags, half_grad, grad_in, grad, grad_v, sem):
    place_kernel(flags, half_grad, grad, grad_v, sem, False)


def conv_kernel(
    flags, lat, previous, kernel, window, totals, scales, output, tmp, taps, lat_v, kernel_v, window_v, sem
):
    from_kernel, from_window, from_lat = copies(
        sem, (kernel, kernel_v), (window, window_v.at[:, HALO * W :]), (lat, lat_v)
    )
    center, inverse = center_inverse(totals, PER)
    for f in range(HALO):
        blocks = by_row(previous[f], tmp)
        for h in range(H):
            active = jnp.where(flags[0] > 0, activated(blocks[h], center, inverse, scales), 0.0)
            for s, moved in enumerate(shifted(active)):
                window_v[(s * H + h) * C : (s * H + h + 1) * C, f * W : (f + 1) * W] = moved.astype(BF16)
    taps[...] = jnp.zeros_like(taps)
    from_kernel.wait()
    for kt in range(3):
        for ki in range(3):
            for kj in range(3):
                tap = kernel_v[9 * kt + 3 * ki + kj]
                for h in range(H):
                    other = h - 1 + ki
                    if 0 <= other < H:
                        at = (kj * H + other) * C
                        taps[kt, h * C : (h + 1) * C, at : at + C] = tap
    from_window.wait()
    total = jnp.dot(taps[0], window_v[:, 0 : T * W], preferred_element_type=F32)
    for f in range(1, 3):
        total = total + jnp.dot(taps[f], window_v[:, f * W : (f + T) * W], preferred_element_type=F32)
    from_lat.wait()
    for t in range(T):
        for h in range(H):
            tmp[pl.ds(h, C, stride=H), :] = total[h * C : (h + 1) * C, t * W : (t + 1) * W]
        output[t] = (lat_v[t].astype(F32) + tmp[...]).astype(BF16)


def adjoint_kernel(lat, cot, totals, backward, scaled, result, lat_v, cot_v, scaled_v, sem):
    started = copies(sem, (lat, lat_v), (cot, cot_v), (scaled, scaled_v))
    center, inverse = center_inverse(totals, PER * H)
    row = backward[...][0:1] / MEMBERS
    first = group_column(row, 0, PER * H)
    second = group_column(row, GROUPS, PER * H)
    for copy in started:
        copy.wait()
    for t in range(T):
        unit = (lat_v[t].astype(F32) - center) * inverse
        value = cot_v[t].astype(F32) + inverse * (scaled_v[t] - first - unit * second)
        result[t] = value.astype(BF16)


VMEM, HBM, SMEM = (
    pl.BlockSpec(memory_space=pltpu.VMEM),
    pl.BlockSpec(memory_space=pltpu.HBM),
    pl.BlockSpec(memory_space=pltpu.SMEM),
)


def call(body, out, scratch, *operands, far=(), out_far=(), scalars=0, flops=0, moved=1 << 20, aliases=(), limit=12):
    single = not isinstance(out, tuple)
    count = 1 if single else len(out)
    outs = tuple(HBM if i in out_far else VMEM for i in range(count))
    shapes = tuple(pltpu.HBM(o.shape, o.dtype) if i in out_far else o for i, o in enumerate((out,) if single else out))
    operands = [pltpu.with_memory_space_constraint(x, pltpu.HBM) if i in far else x for i, x in enumerate(operands)]
    return pl.pallas_call(
        body,
        out_shape=shapes[0] if single else shapes,
        in_specs=[SMEM if i < scalars else HBM if i in far else VMEM for i in range(len(operands))],
        out_specs=outs[0] if single else outs,
        scratch_shapes=scratch,
        compiler_params=pltpu.CompilerParams(vmem_limit_bytes=limit * MIB),
        input_output_aliases=dict(aliases),
        cost_estimate=pl.CostEstimate(flops=flops, bytes_accessed=moved, transcendentals=0),
    )(*operands)


def shape(*dims, dtype=F32):
    return jax.ShapeDtypeStruct(dims, dtype)


def sems(count):
    return pltpu.SemaphoreType.DMA((count,))


def swap(value, axis):
    return lax.ppermute(value, axis, [(0, 1), (1, 0)])


def exchange(parts, axes):
    return lax.all_to_all(parts, axes, 0, 0)


def per_device(latents, norm_gain, norm_shift, kernel, cotangent):
    lat = latents.reshape(T, ROWS, W)
    cot = cotangent.reshape(T, ROWS, W)
    gain, shift = norm_gain.reshape(1, C), norm_shift.reshape(1, C)
    zh, zm, core = (lax.axis_index(axis) for axis in ("zh", "zm", "core"))
    flags = jnp.stack([zh * 2 + core, core, zm]).astype(jnp.int32)
    slab = ("zh", "core")
    halo = shape(HALO, ROWS, W, dtype=BF16)
    frames = pltpu.VMEM((T, ROWS, W), BF16)
    tmp = pltpu.VMEM((ROWS, W), F32)
    row = pltpu.VMEM((1, C), F32)
    window_scratch = pltpu.VMEM((3 * ROWS, (T + HALO) * W), BF16)
    taps = pltpu.VMEM((3, ROWS, 3 * ROWS), BF16)
    kernel_scratch = pltpu.VMEM((27, C, C), BF16)
    scaled_scratch = pltpu.VMEM((T, ROWS, W), F32)
    own = call(start_kernel, shape(8, W), [frames, sems(T)], lat, far=(0,))
    adj, scales, head, tail = call(
        prepare_kernel,
        (shape(4 * C, T * PLANE, dtype=BF16), shape(2, C, W), halo, halo),
        [frames, frames, row, row, tmp, sems(5), sems(1)],
        lat,
        cot,
        gain,
        shift,
        far=(0, 1, 2, 3),
        out_far=(3,),
    )
    across, scales = lax.optimization_barrier((swap(own, "zh"), scales))
    pair = own + across
    following = lax.ppermute(head, slab, [(i + 1, i) for i in range(SLABS - 1)])
    totals = jnp.concatenate([pair, swap(pair, "core")], axis=0)
    window, keep, send, last = call(
        grad_kernel,
        (
            shape(3 * ROWS, T * W, dtype=BF16),
            shape(COMM, C),
            shape(COMM, C),
            shape(3 * C, HALO * PLANE, dtype=BF16),
        ),
        [pltpu.VMEM((3 * C, T * PLANE), BF16), pltpu.VMEM((3 * ROWS, T * W), BF16), sems(1)],
        flags,
        adj,
        totals,
        scales,
        out_far=(0,),
        scalars=1,
        flops=4 * 10**9,
    )
    following, last = lax.optimization_barrier((following, last))
    keep, send = call(
        edge_kernel,
        (shape(COMM, C), shape(COMM, C)),
        [tmp, pltpu.VMEM((3 * C, HALO * PLANE), BF16)],
        flags,
        keep,
        send,
        following,
        last,
        scalars=1,
        aliases=((1, 0), (2, 1)),
    )
    chip = call(add_kernel, shape(COMM, C, dtype=WIRE), [], keep, swap(send, "core"))
    parts = exchange(chip.reshape(SIDE, PART, C), ("y", "zn", "x"))
    scaled, sums = call(
        back_kernel,
        (shape(T, ROWS, W), shape(8, W)),
        [tmp, window_scratch, taps, frames, frames, kernel_scratch, scaled_scratch, sems(3)],
        lat,
        cot,
        following,
        kernel,
        totals,
        scales,
        far=(0, 1, 3),
        out_far=(0,),
        limit=20,
        flops=4 * 10**9,
    )
    sums, tail = lax.optimization_barrier((sums, tail))
    previous = lax.ppermute(tail, slab, [(i, i + 1) for i in range(SLABS - 1)])
    sums = sums + swap(sums, "core")
    packed = call(part_kernel, shape(4, PART + 8, C), [], parts, sums)
    output = call(
        conv_kernel,
        shape(T, ROWS, W, dtype=BF16),
        [tmp, taps, frames, kernel_scratch, window_scratch, sems(3)],
        flags,
        lat,
        previous,
        kernel,
        window,
        totals,
        scales,
        far=(1, 3, 4),
        limit=20,
        scalars=1,
        flops=4 * 10**9,
    )
    over_z, output = lax.optimization_barrier((exchange(packed, ("zh", "zm")), output))
    part, backward = call(
        merge_kernel, (shape(SIDE, PART, C, dtype=BF16), shape(8, C)), [], flags, over_z, scalars=1
    )
    result = call(
        adjoint_kernel,
        shape(T, ROWS, W, dtype=BF16),
        [frames, frames, scaled_scratch, sems(3)],
        lat,
        cot,
        totals,
        backward,
        scaled,
        far=(0, 1, 4),
        flops=10**9,
    )
    mine, result = lax.optimization_barrier((exchange(part, ("y", "zn", "x")).reshape(COMM, C), result))
    other = swap(mine, "core")
    half_scratch = [pltpu.VMEM((27, C // 2, C), F32), sems(3)]
    kernel_grad = call(
        place_first, shape(27, C, C), half_scratch, flags, mine, out_far=(0,), scalars=1, flops=10**9
    )
    kernel_grad = call(
        place_second,
        shape(27, C, C),
        half_scratch,
        flags,
        other,
        kernel_grad,
        far=(2,),
        out_far=(0,),
        scalars=1,
        aliases=((2, 0),),
    )
    return output.reshape(latents.shape), result.reshape(latents.shape), kernel_grad


WIRE = F32


def solution(mesh):
    fine = Mesh(mesh.devices.reshape(2, 2, 4, 2, 2, 4), ("zh", "core", "y", "zm", "zn", "x"))
    frames = P(("y", "zm", "zn", "x"), ("zh", "core"), None, None, None)
    return jax.shard_map(
        per_device,
        mesh=fine,
        in_specs=(frames, P(), P(), P(), frames),
        out_specs=(frames, frames, P()),
        check_vma=False,
    )
```

```python
import functools

import jax
import jax.numpy as jnp
from jax import lax
from jax.experimental import pallas as pl
from jax.experimental.pallas import tpu as pltpu
from jax.sharding import Mesh
from jax.sharding import PartitionSpec as P

C = 128
H = 4
W = 128
T = 4
HALO = 2
GROUPS = 32
PER = C // GROUPS
SLABS = 4
MEMBERS = SLABS * T * PER * H * W
ROWS = H * C
HALF = 27 * (C // 2)
COMM = HALF + 64
SIDE = 32
PART = COMM // SIDE
F32 = jnp.float32
BF16 = jnp.bfloat16
MIB = 1024 * 1024


def lanes():
    return lax.broadcasted_iota(jnp.int32, (C, W), 1)


def rows():
    return lax.broadcasted_iota(jnp.int32, (C, W), 0)


def shifted(block):
    left = jnp.where(lanes() == 0, 0.0, pltpu.roll(block, 1, 1))
    right = jnp.where(lanes() == W - 1, 0.0, pltpu.roll(block, W - 1, 1))
    return left, block, right


def row_of(column, offset):
    lane = lax.broadcasted_iota(jnp.int32, (GROUPS, W), 1)
    sub = lax.broadcasted_iota(jnp.int32, (GROUPS, W), 0)
    return jnp.sum(jnp.where(lane == sub + offset, column, 0.0), axis=0, keepdims=True)


def channel_column(row):
    return jnp.sum(jnp.where(lanes() == rows(), row, 0.0), axis=1, keepdims=True)


def group_column(row, offset, per_channel):
    lane = lax.broadcasted_iota(jnp.int32, (GROUPS * per_channel, W), 1)
    sub = lax.broadcasted_iota(jnp.int32, (GROUPS * per_channel, W), 0)
    return jnp.sum(jnp.where(lane == sub // per_channel + offset, row, 0.0), axis=1, keepdims=True)


def center_inverse(totals, per_channel):
    row = jnp.sum(totals[...].reshape(-1, 8, W), axis=0)[0:1] / MEMBERS
    center = group_column(row, 0, per_channel)
    square = group_column(row, GROUPS, per_channel)
    return center, lax.rsqrt(square - center * center + 1e-06)


def copies(sem, *pairs):
    started = [pltpu.make_async_copy(source, target, sem.at[i]) for i, (source, target) in enumerate(pairs)]
    for copy in started:
        copy.start()
    return started


def start_kernel(lat, sums, lat_v, sem):
    parts = copies(sem, *((lat.at[t], lat_v.at[t]) for t in range(T)))
    total = jnp.zeros((ROWS, W), F32)
    square = jnp.zeros((ROWS, W), F32)
    for t in range(T):
        parts[t].wait()
        x = lat_v[t].astype(F32)
        total = total + x
        square = square + x * x
    total = jnp.sum(jnp.sum(total.reshape(GROUPS, -1, W), axis=1), axis=1, keepdims=True)
    square = jnp.sum(jnp.sum(square.reshape(GROUPS, -1, W), axis=1), axis=1, keepdims=True)
    row = row_of(total, 0) + row_of(square, GROUPS)
    sums[...] = jnp.broadcast_to(row, (8, W))


def put_adjoint(adj, f, mine):
    zero = jnp.zeros((C, W), BF16)
    for h in range(H):
        for ki in range(3):
            source = h - ki + 1
            block = mine[source].astype(BF16) if 0 <= source < H else zero
            adj[ki * C : (ki + 1) * C, (f * H + h) * W : (f * H + h + 1) * W] = block


def prepare_kernel(
    flags, lat, cot, gain, shift, adj, scales, near, far, lat_v, cot_v, gain_v, shift_v, tmp, sem, halo_sem
):
    tail, head = lat.at[T - HALO :], cot.at[:HALO]

    @pl.when(flags[1] == 0)
    def _():
        copies(halo_sem, (tail, near), (head, far))

    @pl.when(flags[1] != 0)
    def _():
        copies(halo_sem, (head, near), (tail, far))

    from_lat, from_cot, *small = copies(sem, (lat, lat_v), (cot, cot_v), (gain, gain_v), (shift, shift_v))
    from_lat.wait()
    for t in range(T):
        for h, block in enumerate(by_row(lat_v[t], tmp)):
            adj[3 * C :, (t * H + h) * W : (t * H + h + 1) * W] = block.astype(BF16)
    from_cot.wait()
    for t in range(T):
        put_adjoint(adj, t, by_row(cot_v[t], tmp))
    for copy in small:
        copy.wait()
    scales[0] = jnp.broadcast_to(channel_column(gain_v[...]), (C, W))
    scales[1] = jnp.broadcast_to(channel_column(shift_v[...]), (C, W))
    pltpu.make_async_copy(tail, near, halo_sem.at[0]).wait()
    pltpu.make_async_copy(head, far, halo_sem.at[1]).wait()


def pick(condition, first, second):
    return jnp.where(condition, first.astype(F32), second.astype(F32))


def by_row(frame, tmp):
    tmp[...] = frame.astype(F32)
    return [tmp[pl.ds(h, C, stride=H), :] for h in range(H)]


def back_kernel(
    flags, lat, cot, near, far, kernel, totals, scales, scaled, sums, tmp, window, taps, lat_v, cot_v, kernel_v, scaled_v, sem
):
    from_cot, from_kernel, from_lat = copies(sem, (cot, cot_v), (kernel, kernel_v), (lat, lat_v))
    from_cot.wait()
    for f in range(T + HALO):
        blocks = by_row(cot_v[f] if f < T else pick(flags[1] == 0, near[f - T], far[f - T]), tmp)
        for h in range(H):
            for s, moved in enumerate(shifted(blocks[h])):
                at = (s * H + h) * C
                window[at : at + C, f * W : (f + 1) * W] = moved.astype(BF16)
    taps[...] = jnp.zeros_like(taps)
    from_kernel.wait()
    for kt in range(3):
        for ki in range(3):
            for kj in range(3):
                tap = kernel_v[9 * kt + 3 * ki + kj].astype(F32).T.astype(BF16)
                for h in range(H):
                    other = h + 1 - ki
                    if 0 <= other < H:
                        at = ((2 - kj) * H + other) * C
                        taps[2 - kt, h * C : (h + 1) * C, at : at + C] = tap
    back = jnp.dot(taps[0], window[:, 0 : T * W], preferred_element_type=F32)
    for f in range(1, 3):
        back = back + jnp.dot(taps[f], window[:, f * W : (f + T) * W], preferred_element_type=F32)
    center, inverse = center_inverse(totals, PER)
    from_lat.wait()
    first = jnp.zeros((C, W), F32)
    second = jnp.zeros((C, W), F32)
    for t in range(T):
        blocks = by_row(lat_v[t], tmp)
        for h in range(H):
            unit = (blocks[h] - center) * inverse
            normed = unit * scales[0] + scales[1]
            sig = 1.0 / (1.0 + jnp.exp(-normed))
            adjoint = back[h * C : (h + 1) * C, t * W : (t + 1) * W]
            value = adjoint * sig * (1.0 + normed * (1.0 - sig)) * scales[0]
            first = first + value
            second = second + value * unit
            scaled_v[t, pl.ds(h, C, stride=H), :] = value
    (to_scaled,) = copies(sem, (scaled_v, scaled))
    lane, sub = lanes(), rows()
    first = jnp.where(lane == sub // PER, jnp.sum(first, axis=1, keepdims=True), 0.0)
    second = jnp.where(lane == sub // PER + GROUPS, jnp.sum(second, axis=1, keepdims=True), 0.0)
    sums[...] = jnp.broadcast_to(jnp.sum(first + second, axis=0, keepdims=True), (8, W))
    to_scaled.wait()


def activated(block, center, inverse, scales):
    normed = (block - center) * inverse * scales[0] + scales[1]
    return (normed * (1.0 / (1.0 + jnp.exp(-normed)))).astype(BF16).astype(F32)


CONTRACT = (((1,), (1,)), ((), ()))
PLANE = H * W


def halves(core, grads):
    half = C // 2
    for ki in range(3):
        for kj in range(3):
            tap = grads[ki * C : (ki + 1) * C, kj * C : (kj + 1) * C]
            low, high = tap[:half], tap[half:]
            at = (3 * ki + kj) * half
            yield at, jnp.where(core == 0, low, high), jnp.where(core == 0, high, low)


def grad_kernel(flags, adj, totals, scales, window, keep, send, last, flat, window_v, sem):
    center, inverse = center_inverse(totals, PER)
    for t in range(T):
        for h in range(H):
            block = adj[3 * C :, (t * H + h) * W : (t * H + h + 1) * W].astype(F32)
            for s, moved in enumerate(shifted(activated(block, center, inverse, scales))):
                moved = moved.astype(BF16)
                window_v[(s * H + h) * C : (s * H + h + 1) * C, t * W : (t + 1) * W] = moved
                flat[s * C : (s + 1) * C, (t * H + h) * W : (t * H + h + 1) * W] = moved
                if t >= T - HALO:
                    at = ((t - T + HALO) * H + h) * W
                    last[s * C : (s + 1) * C, at : at + W] = moved
    (to_window,) = copies(sem, (window_v, window))
    for kt in range(3):
        ahead = 2 - kt
        grads = lax.dot_general(
            adj[: 3 * C, ahead * PLANE :], flat[:, : (T - ahead) * PLANE], CONTRACT, preferred_element_type=F32
        )
        for at, mine, other in halves(flags[1], grads):
            at += 9 * kt * (C // 2)
            keep[at : at + C // 2] = mine
            send[at : at + C // 2] = other
    keep[HALF:] = jnp.zeros((COMM - HALF, C), F32)
    send[HALF:] = jnp.zeros((COMM - HALF, C), F32)
    to_window.wait()


def edge_kernel(flags, keep_in, send_in, near, far, last, keep, send, tmp, adj):
    for f in range(HALO):
        put_adjoint(adj, f, by_row(pick(flags[1] == 0, near[f], far[f]), tmp))
    for kt in range(2):
        ahead = 2 - kt
        grads = lax.dot_general(
            adj[:, : ahead * PLANE], last[:, (HALO - ahead) * PLANE :], CONTRACT, preferred_element_type=F32
        )
        for at, mine, other in halves(flags[1], grads):
            at += 9 * kt * (C // 2)
            keep[at : at + C // 2] = keep_in[at : at + C // 2] + mine
            send[at : at + C // 2] = send_in[at : at + C // 2] + other


def add_kernel(keep, received, chip):
    chip[...] = (keep[...] + received[...]).astype(chip.dtype)


def part_kernel(parts, sums, packed):
    packed[:PART] = jnp.sum(parts[...].astype(F32), axis=0)
    packed[PART:] = sums[...]


def merge_kernel(own, one, two, three, parts, backward):
    total = (own[...] + one[...]) + (two[...] + three[...])
    part = total[:PART].astype(BF16)
    for i in range(SIDE):
        parts[i] = part
    backward[...] = own[PART:] + two[PART:]


def place_kernel(flags, half_grad, grad, grad_v, sem, first):
    half = C // 2
    core = flags[1] if first else 1 - flags[1]
    at = pl.multiple_of(core * half, half)
    started = []
    for kt in range(3):
        rows_of = half_grad[9 * kt * half : 9 * (kt + 1) * half].astype(F32)
        grad_v[9 * kt : 9 * (kt + 1)] = rows_of.reshape(9, half, C)
        taps = pl.ds(9 * kt, 9)
        started += copies(sem.at[pl.ds(kt, 1)], (grad_v.at[taps], grad.at[taps, pl.ds(at, half)]))
    for copy in started:
        copy.wait()


def place_first(flags, half_grad, grad, grad_v, sem):
    place_kernel(flags, half_grad, grad, grad_v, sem, True)


def place_second(flags, half_grad, grad_in, grad, grad_v, sem):
    place_kernel(flags, half_grad, grad, grad_v, sem, False)


def conv_kernel(
    flags, lat, near, far, kernel, window, totals, scales, output, tmp, taps, lat_v, kernel_v, window_v, output_v, sem, out_sem
):
    from_kernel, from_window, from_lat = copies(
        sem, (kernel, kernel_v), (window, window_v.at[:, HALO * W :]), (lat, lat_v)
    )
    center, inverse = center_inverse(totals, PER)
    for f in range(HALO):
        blocks = by_row(pick(flags[1] == 0, far[f], near[f]), tmp)
        for h in range(H):
            active = jnp.where(flags[0] > 0, activated(blocks[h], center, inverse, scales), 0.0)
            for s, moved in enumerate(shifted(active)):
                window_v[(s * H + h) * C : (s * H + h + 1) * C, f * W : (f + 1) * W] = moved.astype(BF16)
    taps[...] = jnp.zeros_like(taps)
    from_kernel.wait()
    for kt in range(3):
        for ki in range(3):
            for kj in range(3):
                tap = kernel_v[9 * kt + 3 * ki + kj]
                for h in range(H):
                    other = h - 1 + ki
                    if 0 <= other < H:
                        at = (kj * H + other) * C
                        taps[kt, h * C : (h + 1) * C, at : at + C] = tap
    from_window.wait()
    total = jnp.dot(taps[0], window_v[:, 0 : T * W], preferred_element_type=F32)
    for f in range(1, 3):
        total = total + jnp.dot(taps[f], window_v[:, f * W : (f + T) * W], preferred_element_type=F32)
    from_lat.wait()
    started = []
    for t in range(T):
        for h in range(H):
            tmp[pl.ds(h, C, stride=H), :] = total[h * C : (h + 1) * C, t * W : (t + 1) * W]
        output_v[t] = (lat_v[t].astype(F32) + tmp[...]).astype(BF16)
        started += copies(out_sem.at[pl.ds(t, 1)], (output_v.at[t], output.at[t]))
    for copy in started:
        copy.wait()


def adjoint_kernel(
    lat, cot, totals, backward, scaled, result, lat_v, cot_v, scaled_v, result_v, lat_sem, cot_sem, scaled_sem, out_sem
):
    fetched = list(
        zip(
            *(
                copies(sem, *((source.at[t], target.at[t]) for t in range(T)))
                for sem, source, target in (
                    (lat_sem, lat, lat_v),
                    (cot_sem, cot, cot_v),
                    (scaled_sem, scaled, scaled_v),
                )
            )
        )
    )
    center, inverse = center_inverse(totals, PER * H)
    row = backward[...][0:1] / MEMBERS
    first = group_column(row, 0, PER * H)
    second = group_column(row, GROUPS, PER * H)
    started = []
    for t in range(T):
        for copy in fetched[t]:
            copy.wait()
        unit = (lat_v[t].astype(F32) - center) * inverse
        value = cot_v[t].astype(F32) + inverse * (scaled_v[t] - first - unit * second)
        result_v[t] = value.astype(BF16)
        started += copies(out_sem.at[pl.ds(t, 1)], (result_v.at[t], result.at[t]))
    for copy in started:
        copy.wait()


VMEM, HBM, SMEM = (
    pl.BlockSpec(memory_space=pltpu.VMEM),
    pl.BlockSpec(memory_space=pltpu.HBM),
    pl.BlockSpec(memory_space=pltpu.SMEM),
)


def call(body, out, scratch, *operands, far=(), out_far=(), scalars=0, flops=0, moved=1 << 20, aliases=(), limit=12):
    single = not isinstance(out, tuple)
    count = 1 if single else len(out)
    outs = tuple(HBM if i in out_far else VMEM for i in range(count))
    shapes = tuple(pltpu.HBM(o.shape, o.dtype) if i in out_far else o for i, o in enumerate((out,) if single else out))
    operands = [pltpu.with_memory_space_constraint(x, pltpu.HBM) if i in far else x for i, x in enumerate(operands)]
    return pl.pallas_call(
        body,
        out_shape=shapes[0] if single else shapes,
        in_specs=[SMEM if i < scalars else HBM if i in far else VMEM for i in range(len(operands))],
        out_specs=outs[0] if single else outs,
        scratch_shapes=scratch,
        compiler_params=pltpu.CompilerParams(vmem_limit_bytes=limit * MIB),
        input_output_aliases=dict(aliases),
        cost_estimate=pl.CostEstimate(flops=flops, bytes_accessed=moved, transcendentals=0),
    )(*operands)


def shape(*dims, dtype=F32):
    return jax.ShapeDtypeStruct(dims, dtype)


def sems(count):
    return pltpu.SemaphoreType.DMA((count,))


def swap(value, axis):
    return lax.ppermute(value, axis, [(0, 1), (1, 0)])


def exchange(parts, axes):
    return lax.all_to_all(parts, axes, 0, 0)


def per_device(latents, norm_gain, norm_shift, kernel, cotangent):
    lat = latents.reshape(T, ROWS, W)
    cot = cotangent.reshape(T, ROWS, W)
    gain, shift = norm_gain.reshape(1, C), norm_shift.reshape(1, C)
    zh, core = lax.axis_index("zh"), lax.axis_index("core")
    flags = jnp.stack([zh * 2 + core, core]).astype(jnp.int32)
    halo = shape(HALO, ROWS, W, dtype=BF16)
    frames = pltpu.VMEM((T, ROWS, W), BF16)
    tmp = pltpu.VMEM((ROWS, W), F32)
    row = pltpu.VMEM((1, C), F32)
    window_scratch = pltpu.VMEM((3 * ROWS, (T + HALO) * W), BF16)
    taps = pltpu.VMEM((3, ROWS, 3 * ROWS), BF16)
    kernel_scratch = pltpu.VMEM((27, C, C), BF16)
    scaled_scratch = pltpu.VMEM((T, ROWS, W), F32)
    own = call(start_kernel, shape(8, W), [frames, sems(T)], lat, far=(0,))
    gain, own = lax.optimization_barrier((gain, own))
    adj, scales, to_near, to_far = call(
        prepare_kernel,
        (shape(4 * C, T * PLANE, dtype=BF16), shape(2, C, W), halo, halo),
        [frames, frames, row, row, tmp, sems(4), sems(2)],
        flags,
        lat,
        cot,
        gain,
        shift,
        far=(1, 2, 3, 4),
        scalars=1,
    )
    across, scales = lax.optimization_barrier((swap(own, "zh"), scales))
    pair = own + across
    far = lax.ppermute(to_far, ("zh", "core"), [(1, 2), (2, 1)])
    near = swap(to_near, "core")
    totals = jnp.concatenate([pair, swap(pair, "core")], axis=0)
    window, keep, send, last = call(
        grad_kernel,
        (
            shape(3 * ROWS, T * W, dtype=BF16),
            shape(COMM, C),
            shape(COMM, C),
            shape(3 * C, HALO * PLANE, dtype=BF16),
        ),
        [pltpu.VMEM((3 * C, T * PLANE), BF16), pltpu.VMEM((3 * ROWS, T * W), BF16), sems(1)],
        flags,
        adj,
        totals,
        scales,
        out_far=(0,),
        scalars=1,
        flops=2 * 10**9,
    )
    near, far, last = lax.optimization_barrier((near, far, last))
    keep, send = call(
        edge_kernel,
        (shape(COMM, C), shape(COMM, C)),
        [tmp, pltpu.VMEM((3 * C, HALO * PLANE), BF16)],
        flags,
        keep,
        send,
        near,
        far,
        last,
        scalars=1,
        aliases=((1, 0), (2, 1)),
    )
    chip = call(add_kernel, shape(COMM, C, dtype=WIRE), [], keep, swap(send, "core"))
    parts = exchange(chip.reshape(SIDE, PART, C), ("y", "zn", "x"))
    scaled, sums = call(
        back_kernel,
        (shape(T, ROWS, W), shape(8, W)),
        [tmp, window_scratch, taps, frames, frames, kernel_scratch, scaled_scratch, sems(3)],
        flags,
        lat,
        cot,
        near,
        far,
        kernel,
        totals,
        scales,
        far=(1, 2, 5),
        out_far=(0,),
        scalars=1,
        limit=20,
        flops=4 * 10**9,
    )
    sums = sums + swap(sums, "core")
    packed = call(part_kernel, shape(PART + 8, C), [], parts, sums)
    others = [lax.ppermute(packed, ("zh", "zm"), [(i, i ^ flip) for i in range(4)]) for flip in (1, 2, 3)]
    part, backward = call(
        merge_kernel, (shape(SIDE, PART, C, dtype=BF16), shape(8, C)), [], packed, *others
    )
    part, window = lax.optimization_barrier((part, window))
    output = call(
        conv_kernel,
        shape(T, ROWS, W, dtype=BF16),
        [tmp, taps, frames, kernel_scratch, window_scratch, frames, sems(3), sems(T)],
        flags,
        lat,
        near,
        far,
        kernel,
        window,
        totals,
        scales,
        far=(1, 4, 5),
        out_far=(0,),
        limit=20,
        scalars=1,
        flops=4 * 10**9,
    )
    result = call(
        adjoint_kernel,
        shape(T, ROWS, W, dtype=BF16),
        [frames, frames, scaled_scratch, frames, sems(T), sems(T), sems(T), sems(T)],
        lat,
        cot,
        totals,
        backward,
        scaled,
        far=(0, 1, 4),
        out_far=(0,),
        flops=10**9,
    )
    mine, output, result = lax.optimization_barrier(
        (exchange(part, ("y", "zn", "x")).reshape(COMM, C), output, result)
    )
    other = swap(mine, "core")
    half_scratch = [pltpu.VMEM((27, C // 2, C), F32), sems(3)]
    kernel_grad = call(
        place_first, shape(27, C, C), half_scratch, flags, mine, out_far=(0,), scalars=1, flops=10**9
    )
    kernel_grad = call(
        place_second,
        shape(27, C, C),
        half_scratch,
        flags,
        other,
        kernel_grad,
        far=(2,),
        out_far=(0,),
        scalars=1,
        aliases=((2, 0),),
    )
    return output.reshape(latents.shape), result.reshape(latents.shape), kernel_grad


WIRE = F32


def solution(mesh):
    fine = Mesh(mesh.devices.reshape(2, 2, 4, 2, 2, 4), ("zh", "core", "y", "zm", "zn", "x"))
    frames = P(("y", "zm", "zn", "x"), ("zh", "core"), None, None, None)
    return jax.shard_map(
        per_device,
        mesh=fine,
        in_specs=(frames, P(), P(), P(), frames),
        out_specs=(frames, frames, P()),
        check_vma=False,
    )
```

```python
import functools

import jax
import jax.numpy as jnp
from jax import lax
from jax.experimental import pallas as pl
from jax.experimental.pallas import tpu as pltpu
from jax.sharding import Mesh
from jax.sharding import PartitionSpec as P

C = 128
H = 4
W = 128
T = 4
HALO = 2
GROUPS = 32
PER = C // GROUPS
SLABS = 4
MEMBERS = SLABS * T * PER * H * W
ROWS = H * C
HALF = 27 * (C // 2)
COMM = HALF + 64
SIDE = 32
PART = COMM // SIDE
F32 = jnp.float32
BF16 = jnp.bfloat16
MIB = 1024 * 1024


def lanes():
    return lax.broadcasted_iota(jnp.int32, (C, W), 1)


def rows():
    return lax.broadcasted_iota(jnp.int32, (C, W), 0)


def shifted(block):
    left = jnp.where(lanes() == 0, 0.0, pltpu.roll(block, 1, 1))
    right = jnp.where(lanes() == W - 1, 0.0, pltpu.roll(block, W - 1, 1))
    return left, block, right


def row_of(column, offset):
    lane = lax.broadcasted_iota(jnp.int32, (GROUPS, W), 1)
    sub = lax.broadcasted_iota(jnp.int32, (GROUPS, W), 0)
    return jnp.sum(jnp.where(lane == sub + offset, column, 0.0), axis=0, keepdims=True)


def channel_column(row):
    return jnp.sum(jnp.where(lanes() == rows(), row, 0.0), axis=1, keepdims=True)


def group_column(row, offset, per_channel):
    lane = lax.broadcasted_iota(jnp.int32, (GROUPS * per_channel, W), 1)
    sub = lax.broadcasted_iota(jnp.int32, (GROUPS * per_channel, W), 0)
    return jnp.sum(jnp.where(lane == sub // per_channel + offset, row, 0.0), axis=1, keepdims=True)


def center_inverse(totals, per_channel):
    row = jnp.sum(totals[...].reshape(-1, 8, W), axis=0)[0:1] / MEMBERS
    center = group_column(row, 0, per_channel)
    square = group_column(row, GROUPS, per_channel)
    return center, lax.rsqrt(square - center * center + 1e-06)


def copies(sem, *pairs):
    started = [pltpu.make_async_copy(source, target, sem.at[i]) for i, (source, target) in enumerate(pairs)]
    for copy in started:
        copy.start()
    return started


def start_kernel(lat, sums, lat_v, sem):
    parts = copies(sem, *((lat.at[t], lat_v.at[t]) for t in range(T)))
    total = jnp.zeros((ROWS, W), F32)
    square = jnp.zeros((ROWS, W), F32)
    for t in range(T):
        parts[t].wait()
        x = lat_v[t].astype(F32)
        total = total + x
        square = square + x * x
    total = jnp.sum(jnp.sum(total.reshape(GROUPS, -1, W), axis=1), axis=1, keepdims=True)
    square = jnp.sum(jnp.sum(square.reshape(GROUPS, -1, W), axis=1), axis=1, keepdims=True)
    row = row_of(total, 0) + row_of(square, GROUPS)
    sums[...] = jnp.broadcast_to(row, (8, W))


def put_adjoint(adj, f, mine):
    zero = jnp.zeros((C, W), BF16)
    for h in range(H):
        for ki in range(3):
            source = h - ki + 1
            block = mine[source].astype(BF16) if 0 <= source < H else zero
            adj[ki * C : (ki + 1) * C, (f * H + h) * W : (f * H + h + 1) * W] = block


def prepare_kernel(
    flags, lat, cot, gain, shift, adj, scales, near, far, lat_v, cot_v, gain_v, shift_v, tmp, sem, halo_sem
):
    tail, head = lat.at[T - HALO :], cot.at[:HALO]

    @pl.when(flags[1] == 0)
    def _():
        copies(halo_sem, (tail, near), (head, far))

    @pl.when(flags[1] != 0)
    def _():
        copies(halo_sem, (head, near), (tail, far))

    from_lat, from_cot, *small = copies(sem, (lat, lat_v), (cot, cot_v), (gain, gain_v), (shift, shift_v))
    from_lat.wait()
    for t in range(T):
        for h, block in enumerate(by_row(lat_v[t], tmp)):
            adj[3 * C :, (t * H + h) * W : (t * H + h + 1) * W] = block.astype(BF16)
    from_cot.wait()
    for t in range(T):
        put_adjoint(adj, t, by_row(cot_v[t], tmp))
    for copy in small:
        copy.wait()
    scales[0] = jnp.broadcast_to(channel_column(gain_v[...]), (C, W))
    scales[1] = jnp.broadcast_to(channel_column(shift_v[...]), (C, W))
    pltpu.make_async_copy(tail, near, halo_sem.at[0]).wait()
    pltpu.make_async_copy(head, far, halo_sem.at[1]).wait()


def clear(taps):
    zero = jnp.zeros((C, C), BF16)
    for f in range(3):
        for s in range(3):
            for h in range(H):
                for other in range(H):
                    if abs(h - other) > 1:
                        at = (s * H + other) * C
                        taps[f, h * C : (h + 1) * C, at : at + C] = zero


def pick(condition, first, second):
    return jnp.where(condition, first.astype(F32), second.astype(F32))


def by_row(frame, tmp):
    tmp[...] = frame.astype(F32)
    return [tmp[pl.ds(h, C, stride=H), :] for h in range(H)]


def back_kernel(
    flags, lat, cot, near, far, kernel, totals, scales, scaled, sums, tmp, window, taps, lat_v, cot_v, kernel_v, scaled_v, sem
):
    from_cot, from_kernel, from_lat = copies(sem, (cot, cot_v), (kernel, kernel_v), (lat, lat_v))
    from_cot.wait()
    for f in range(T + HALO):
        blocks = by_row(cot_v[f] if f < T else pick(flags[1] == 0, near[f - T], far[f - T]), tmp)
        for h in range(H):
            for s, moved in enumerate(shifted(blocks[h])):
                at = (s * H + h) * C
                window[at : at + C, f * W : (f + 1) * W] = moved.astype(BF16)
    clear(taps)
    from_kernel.wait()
    for kt in range(3):
        for ki in range(3):
            for kj in range(3):
                tap = kernel_v[9 * kt + 3 * ki + kj].astype(F32).T.astype(BF16)
                for h in range(H):
                    other = h + 1 - ki
                    if 0 <= other < H:
                        at = ((2 - kj) * H + other) * C
                        taps[2 - kt, h * C : (h + 1) * C, at : at + C] = tap
    back = jnp.dot(taps[0], window[:, 0 : T * W], preferred_element_type=F32)
    for f in range(1, 3):
        back = back + jnp.dot(taps[f], window[:, f * W : (f + T) * W], preferred_element_type=F32)
    center, inverse = center_inverse(totals, PER)
    from_lat.wait()
    first = jnp.zeros((C, W), F32)
    second = jnp.zeros((C, W), F32)
    for t in range(T):
        blocks = by_row(lat_v[t], tmp)
        for h in range(H):
            unit = (blocks[h] - center) * inverse
            normed = unit * scales[0] + scales[1]
            sig = 1.0 / (1.0 + jnp.exp(-normed))
            adjoint = back[h * C : (h + 1) * C, t * W : (t + 1) * W]
            value = adjoint * sig * (1.0 + normed * (1.0 - sig)) * scales[0]
            first = first + value
            second = second + value * unit
            scaled_v[t, pl.ds(h, C, stride=H), :] = value
    (to_scaled,) = copies(sem, (scaled_v, scaled))
    lane, sub = lanes(), rows()
    first = jnp.where(lane == sub // PER, jnp.sum(first, axis=1, keepdims=True), 0.0)
    second = jnp.where(lane == sub // PER + GROUPS, jnp.sum(second, axis=1, keepdims=True), 0.0)
    sums[...] = jnp.broadcast_to(jnp.sum(first + second, axis=0, keepdims=True), (8, W))
    to_scaled.wait()


def activated(block, center, inverse, scales):
    normed = (block - center) * inverse * scales[0] + scales[1]
    return (normed * (1.0 / (1.0 + jnp.exp(-normed)))).astype(BF16).astype(F32)


CONTRACT = (((1,), (1,)), ((), ()))
PLANE = H * W


def halves(core, grads):
    half = C // 2
    for ki in range(3):
        for kj in range(3):
            tap = grads[ki * C : (ki + 1) * C, kj * C : (kj + 1) * C]
            low, high = tap[:half], tap[half:]
            at = (3 * ki + kj) * half
            yield at, jnp.where(core == 0, low, high), jnp.where(core == 0, high, low)


def grad_kernel(flags, adj, totals, scales, window, keep, send, last, flat, window_v, sem):
    center, inverse = center_inverse(totals, PER)
    for t in range(T):
        for h in range(H):
            block = adj[3 * C :, (t * H + h) * W : (t * H + h + 1) * W].astype(F32)
            for s, moved in enumerate(shifted(activated(block, center, inverse, scales))):
                moved = moved.astype(BF16)
                window_v[(s * H + h) * C : (s * H + h + 1) * C, t * W : (t + 1) * W] = moved
                flat[s * C : (s + 1) * C, (t * H + h) * W : (t * H + h + 1) * W] = moved
                if t >= T - HALO:
                    at = ((t - T + HALO) * H + h) * W
                    last[s * C : (s + 1) * C, at : at + W] = moved
    (to_window,) = copies(sem, (window_v, window))
    for kt in range(3):
        ahead = 2 - kt
        grads = lax.dot_general(
            adj[: 3 * C, ahead * PLANE :], flat[:, : (T - ahead) * PLANE], CONTRACT, preferred_element_type=F32
        )
        for at, mine, other in halves(flags[1], grads):
            at += 9 * kt * (C // 2)
            keep[at : at + C // 2] = mine
            send[at : at + C // 2] = other
    keep[HALF:] = jnp.zeros((COMM - HALF, C), F32)
    send[HALF:] = jnp.zeros((COMM - HALF, C), F32)
    to_window.wait()


def edge_kernel(flags, keep_in, send_in, near, far, last, keep, send, tmp, adj):
    for f in range(HALO):
        put_adjoint(adj, f, by_row(pick(flags[1] == 0, near[f], far[f]), tmp))
    for kt in range(2):
        ahead = 2 - kt
        grads = lax.dot_general(
            adj[:, : ahead * PLANE], last[:, (HALO - ahead) * PLANE :], CONTRACT, preferred_element_type=F32
        )
        for at, mine, other in halves(flags[1], grads):
            at += 9 * kt * (C // 2)
            keep[at : at + C // 2] = keep_in[at : at + C // 2] + mine
            send[at : at + C // 2] = send_in[at : at + C // 2] + other


def add_kernel(keep, received, chip):
    chip[...] = (keep[...] + received[...]).astype(chip.dtype)


def part_kernel(parts, sums, packed):
    packed[:PART] = jnp.sum(parts[...].astype(F32), axis=0)
    packed[PART:] = sums[...]


def merge_kernel(own, one, two, three, parts, backward):
    total = (own[...] + one[...]) + (two[...] + three[...])
    part = total[:PART].astype(BF16)
    for i in range(SIDE):
        parts[i] = part
    backward[...] = own[PART:] + two[PART:]


def place_kernel(flags, half_grad, grad, grad_v, sem, first):
    half = C // 2
    core = flags[1] if first else 1 - flags[1]
    at = pl.multiple_of(core * half, half)
    started = []
    for kt in range(3):
        rows_of = half_grad[9 * kt * half : 9 * (kt + 1) * half].astype(F32)
        grad_v[9 * kt : 9 * (kt + 1)] = rows_of.reshape(9, half, C)
        taps = pl.ds(9 * kt, 9)
        started += copies(sem.at[pl.ds(kt, 1)], (grad_v.at[taps], grad.at[taps, pl.ds(at, half)]))
    for copy in started:
        copy.wait()


def place_first(flags, half_grad, grad, grad_v, sem):
    place_kernel(flags, half_grad, grad, grad_v, sem, True)


def place_second(flags, half_grad, grad_in, grad, grad_v, sem):
    place_kernel(flags, half_grad, grad, grad_v, sem, False)


def conv_kernel(
    flags, lat, near, far, kernel, window, totals, scales, output, tmp, taps, lat_v, kernel_v, window_v, output_v, sem, out_sem
):
    from_kernel, from_window, from_lat = copies(
        sem, (kernel, kernel_v), (window, window_v.at[:, HALO * W :]), (lat, lat_v)
    )
    center, inverse = center_inverse(totals, PER)
    for f in range(HALO):
        blocks = by_row(pick(flags[1] == 0, far[f], near[f]), tmp)
        for h in range(H):
            active = jnp.where(flags[0] > 0, activated(blocks[h], center, inverse, scales), 0.0)
            for s, moved in enumerate(shifted(active)):
                window_v[(s * H + h) * C : (s * H + h + 1) * C, f * W : (f + 1) * W] = moved.astype(BF16)
    clear(taps)
    from_kernel.wait()
    for kt in range(3):
        for ki in range(3):
            for kj in range(3):
                tap = kernel_v[9 * kt + 3 * ki + kj]
                for h in range(H):
                    other = h - 1 + ki
                    if 0 <= other < H:
                        at = (kj * H + other) * C
                        taps[kt, h * C : (h + 1) * C, at : at + C] = tap
    from_window.wait()
    total = jnp.dot(taps[0], window_v[:, 0 : T * W], preferred_element_type=F32)
    for f in range(1, 3):
        total = total + jnp.dot(taps[f], window_v[:, f * W : (f + T) * W], preferred_element_type=F32)
    from_lat.wait()
    started = []
    for t in range(T):
        for h in range(H):
            tmp[pl.ds(h, C, stride=H), :] = total[h * C : (h + 1) * C, t * W : (t + 1) * W]
        output_v[t] = (lat_v[t].astype(F32) + tmp[...]).astype(BF16)
        started += copies(out_sem.at[pl.ds(t, 1)], (output_v.at[t], output.at[t]))
    for copy in started:
        copy.wait()


def adjoint_kernel(
    lat, cot, totals, backward, scaled, result, lat_v, cot_v, scaled_v, result_v, lat_sem, cot_sem, scaled_sem, out_sem
):
    fetched = list(
        zip(
            *(
                copies(sem, *((source.at[t], target.at[t]) for t in range(T)))
                for sem, source, target in (
                    (lat_sem, lat, lat_v),
                    (cot_sem, cot, cot_v),
                    (scaled_sem, scaled, scaled_v),
                )
            )
        )
    )
    center, inverse = center_inverse(totals, PER * H)
    row = backward[...][0:1] / MEMBERS
    first = group_column(row, 0, PER * H)
    second = group_column(row, GROUPS, PER * H)
    started = []
    for t in range(T):
        for copy in fetched[t]:
            copy.wait()
        unit = (lat_v[t].astype(F32) - center) * inverse
        value = cot_v[t].astype(F32) + inverse * (scaled_v[t] - first - unit * second)
        result_v[t] = value.astype(BF16)
        started += copies(out_sem.at[pl.ds(t, 1)], (result_v.at[t], result.at[t]))
    for copy in started:
        copy.wait()


VMEM, HBM, SMEM = (
    pl.BlockSpec(memory_space=pltpu.VMEM),
    pl.BlockSpec(memory_space=pltpu.HBM),
    pl.BlockSpec(memory_space=pltpu.SMEM),
)


def call(body, out, scratch, *operands, far=(), out_far=(), scalars=0, flops=0, moved=1 << 20, aliases=(), limit=12):
    single = not isinstance(out, tuple)
    count = 1 if single else len(out)
    outs = tuple(HBM if i in out_far else VMEM for i in range(count))
    shapes = tuple(pltpu.HBM(o.shape, o.dtype) if i in out_far else o for i, o in enumerate((out,) if single else out))
    operands = [pltpu.with_memory_space_constraint(x, pltpu.HBM) if i in far else x for i, x in enumerate(operands)]
    return pl.pallas_call(
        body,
        out_shape=shapes[0] if single else shapes,
        in_specs=[SMEM if i < scalars else HBM if i in far else VMEM for i in range(len(operands))],
        out_specs=outs[0] if single else outs,
        scratch_shapes=scratch,
        compiler_params=pltpu.CompilerParams(vmem_limit_bytes=limit * MIB),
        input_output_aliases=dict(aliases),
        cost_estimate=pl.CostEstimate(flops=flops, bytes_accessed=moved, transcendentals=0),
    )(*operands)


def shape(*dims, dtype=F32):
    return jax.ShapeDtypeStruct(dims, dtype)


def sems(count):
    return pltpu.SemaphoreType.DMA((count,))


def swap(value, axis):
    return lax.ppermute(value, axis, [(0, 1), (1, 0)])


def exchange(parts, axes):
    return lax.all_to_all(parts, axes, 0, 0)


def per_device(latents, norm_gain, norm_shift, kernel, cotangent):
    lat = latents.reshape(T, ROWS, W)
    cot = cotangent.reshape(T, ROWS, W)
    gain, shift = norm_gain.reshape(1, C), norm_shift.reshape(1, C)
    zh, core = lax.axis_index("zh"), lax.axis_index("core")
    flags = jnp.stack([zh * 2 + core, core]).astype(jnp.int32)
    halo = shape(HALO, ROWS, W, dtype=BF16)
    frames = pltpu.VMEM((T, ROWS, W), BF16)
    tmp = pltpu.VMEM((ROWS, W), F32)
    row = pltpu.VMEM((1, C), F32)
    window_scratch = pltpu.VMEM((3 * ROWS, (T + HALO) * W), BF16)
    taps = pltpu.VMEM((3, ROWS, 3 * ROWS), BF16)
    kernel_scratch = pltpu.VMEM((27, C, C), BF16)
    scaled_scratch = pltpu.VMEM((T, ROWS, W), F32)
    own = call(start_kernel, shape(8, W), [frames, sems(T)], lat, far=(0,))
    gain, own = lax.optimization_barrier((gain, own))
    adj, scales, to_near, to_far = call(
        prepare_kernel,
        (shape(4 * C, T * PLANE, dtype=BF16), shape(2, C, W), halo, halo),
        [frames, frames, row, row, tmp, sems(4), sems(2)],
        flags,
        lat,
        cot,
        gain,
        shift,
        far=(1, 2, 3, 4),
        scalars=1,
    )
    slab = ("zh", "core")
    before = lax.ppermute(to_far, slab, [(1, 2), (2, 1)])
    far = before
    across, scales = lax.optimization_barrier((swap(own, "zh"), scales))
    pair = own + across
    to_near, pair = lax.optimization_barrier((to_near, pair))
    near = swap(to_near, "core")
    totals = jnp.concatenate([pair, swap(pair, "core")], axis=0)
    window, keep, send, last = call(
        grad_kernel,
        (
            shape(3 * ROWS, T * W, dtype=BF16),
            shape(COMM, C),
            shape(COMM, C),
            shape(3 * C, HALO * PLANE, dtype=BF16),
        ),
        [pltpu.VMEM((3 * C, T * PLANE), BF16), pltpu.VMEM((3 * ROWS, T * W), BF16), sems(1)],
        flags,
        adj,
        totals,
        scales,
        out_far=(0,),
        scalars=1,
        flops=2 * 10**9,
    )
    near, far, last = lax.optimization_barrier((near, far, last))
    keep, send = call(
        edge_kernel,
        (shape(COMM, C), shape(COMM, C)),
        [tmp, pltpu.VMEM((3 * C, HALO * PLANE), BF16)],
        flags,
        keep,
        send,
        near,
        far,
        last,
        scalars=1,
        aliases=((1, 0), (2, 1)),
    )
    chip = call(add_kernel, shape(COMM, C, dtype=WIRE), [], keep, swap(send, "core"))
    parts = exchange(chip.reshape(SIDE, PART, C), ("y", "zn", "x"))
    scaled, sums = call(
        back_kernel,
        (shape(T, ROWS, W), shape(8, W)),
        [tmp, window_scratch, taps, frames, frames, kernel_scratch, scaled_scratch, sems(3)],
        flags,
        lat,
        cot,
        near,
        far,
        kernel,
        totals,
        scales,
        far=(1, 2, 5),
        out_far=(0,),
        scalars=1,
        limit=20,
        flops=4 * 10**9,
    )
    sums = sums + swap(sums, "core")
    packed = call(part_kernel, shape(PART + 8, C), [], parts, sums)
    others = [lax.ppermute(packed, ("zh", "zm"), [(i, i ^ flip) for i in range(4)]) for flip in (1, 2, 3)]
    part, backward = call(
        merge_kernel, (shape(SIDE, PART, C, dtype=BF16), shape(8, C)), [], packed, *others
    )
    part, window = lax.optimization_barrier((part, window))
    output = call(
        conv_kernel,
        shape(T, ROWS, W, dtype=BF16),
        [tmp, taps, frames, kernel_scratch, window_scratch, frames, sems(3), sems(T)],
        flags,
        lat,
        near,
        far,
        kernel,
        window,
        totals,
        scales,
        far=(1, 4, 5),
        out_far=(0,),
        limit=20,
        scalars=1,
        flops=4 * 10**9,
    )
    result = call(
        adjoint_kernel,
        shape(T, ROWS, W, dtype=BF16),
        [frames, frames, scaled_scratch, frames, sems(T), sems(T), sems(T), sems(T)],
        lat,
        cot,
        totals,
        backward,
        scaled,
        far=(0, 1, 4),
        out_far=(0,),
        flops=10**9,
    )
    mine, output, result = lax.optimization_barrier(
        (exchange(part, ("y", "zn", "x")).reshape(COMM, C), output, result)
    )
    other = swap(mine, "core")
    half_scratch = [pltpu.VMEM((27, C // 2, C), F32), sems(3)]
    kernel_grad = call(
        place_first, shape(27, C, C), half_scratch, flags, mine, out_far=(0,), scalars=1, flops=10**9
    )
    kernel_grad = call(
        place_second,
        shape(27, C, C),
        half_scratch,
        flags,
        other,
        kernel_grad,
        far=(2,),
        out_far=(0,),
        scalars=1,
        aliases=((2, 0),),
    )
    return output.reshape(latents.shape), result.reshape(latents.shape), kernel_grad


WIRE = F32


def solution(mesh):
    fine = Mesh(mesh.devices.reshape(2, 2, 4, 2, 2, 4), ("zh", "core", "y", "zm", "zn", "x"))
    frames = P(("y", "zm", "zn", "x"), ("zh", "core"), None, None, None)
    return jax.shard_map(
        per_device,
        mesh=fine,
        in_specs=(frames, P(), P(), P(), frames),
        out_specs=(frames, frames, P()),
        check_vma=False,
    )
```

```python
import functools

import jax
import jax.numpy as jnp
from jax import lax
from jax.experimental import pallas as pl
from jax.experimental.pallas import tpu as pltpu
from jax.sharding import Mesh
from jax.sharding import PartitionSpec as P

C = 128
H = 4
W = 128
T = 4
HALO = 2
GROUPS = 32
PER = C // GROUPS
SLABS = 4
MEMBERS = SLABS * T * PER * H * W
ROWS = H * C
HALF = 27 * (C // 2)
COMM = HALF + 64
SIDE = 32
PART = COMM // SIDE
F32 = jnp.float32
BF16 = jnp.bfloat16
MIB = 1024 * 1024


def lanes():
    return lax.broadcasted_iota(jnp.int32, (C, W), 1)


def rows():
    return lax.broadcasted_iota(jnp.int32, (C, W), 0)


def shifted(block):
    left = jnp.where(lanes() == 0, 0.0, pltpu.roll(block, 1, 1))
    right = jnp.where(lanes() == W - 1, 0.0, pltpu.roll(block, W - 1, 1))
    return left, block, right


def row_of(column, offset):
    lane = lax.broadcasted_iota(jnp.int32, (GROUPS, W), 1)
    sub = lax.broadcasted_iota(jnp.int32, (GROUPS, W), 0)
    return jnp.sum(jnp.where(lane == sub + offset, column, 0.0), axis=0, keepdims=True)


def channel_column(row):
    return jnp.sum(jnp.where(lanes() == rows(), row, 0.0), axis=1, keepdims=True)


def group_column(row, offset, per_channel):
    lane = lax.broadcasted_iota(jnp.int32, (GROUPS * per_channel, W), 1)
    sub = lax.broadcasted_iota(jnp.int32, (GROUPS * per_channel, W), 0)
    return jnp.sum(jnp.where(lane == sub // per_channel + offset, row, 0.0), axis=1, keepdims=True)


def center_inverse(totals, per_channel):
    row = jnp.sum(totals[...].reshape(-1, 8, W), axis=0)[0:1] / MEMBERS
    center = group_column(row, 0, per_channel)
    square = group_column(row, GROUPS, per_channel)
    return center, lax.rsqrt(square - center * center + 1e-06)


def copies(sem, *pairs):
    started = [pltpu.make_async_copy(source, target, sem.at[i]) for i, (source, target) in enumerate(pairs)]
    for copy in started:
        copy.start()
    return started


def start_kernel(lat, sums, lat_v, sem):
    parts = copies(sem, *((lat.at[t], lat_v.at[t]) for t in range(T)))
    total = jnp.zeros((ROWS, W), F32)
    square = jnp.zeros((ROWS, W), F32)
    for t in range(T):
        parts[t].wait()
        x = lat_v[t].astype(F32)
        total = total + x
        square = square + x * x
    total = jnp.sum(jnp.sum(total.reshape(GROUPS, -1, W), axis=1), axis=1, keepdims=True)
    square = jnp.sum(jnp.sum(square.reshape(GROUPS, -1, W), axis=1), axis=1, keepdims=True)
    row = row_of(total, 0) + row_of(square, GROUPS)
    sums[...] = jnp.broadcast_to(row, (8, W))


def put_adjoint(adj, f, mine):
    zero = jnp.zeros((C, W), BF16)
    for h in range(H):
        for ki in range(3):
            source = h - ki + 1
            block = mine[source].astype(BF16) if 0 <= source < H else zero
            adj[ki * C : (ki + 1) * C, (f * H + h) * W : (f * H + h + 1) * W] = block


def prepare_kernel(
    flags, lat, cot, gain, shift, adj, scales, near, far, lat_v, cot_v, gain_v, shift_v, tmp, sem, halo_sem
):
    tail, head = lat.at[T - HALO :], cot.at[:HALO]

    @pl.when(flags[1] == 0)
    def _():
        copies(halo_sem, (tail, near), (head, far))

    @pl.when(flags[1] != 0)
    def _():
        copies(halo_sem, (head, near), (tail, far))

    from_lat, from_cot, *small = copies(sem, (lat, lat_v), (cot, cot_v), (gain, gain_v), (shift, shift_v))
    from_lat.wait()
    for t in range(T):
        for h, block in enumerate(by_row(lat_v[t], tmp)):
            adj[3 * C :, (t * H + h) * W : (t * H + h + 1) * W] = block.astype(BF16)
    from_cot.wait()
    for t in range(T):
        put_adjoint(adj, t, by_row(cot_v[t], tmp))
    for copy in small:
        copy.wait()
    scales[0] = jnp.broadcast_to(channel_column(gain_v[...]), (C, W))
    scales[1] = jnp.broadcast_to(channel_column(shift_v[...]), (C, W))
    pltpu.make_async_copy(tail, near, halo_sem.at[0]).wait()
    pltpu.make_async_copy(head, far, halo_sem.at[1]).wait()


def clear(taps):
    zero = jnp.zeros((C, C), BF16)
    for f in range(3):
        for s in range(3):
            for h in range(H):
                for other in range(H):
                    if abs(h - other) > 1:
                        at = (s * H + other) * C
                        taps[f, h * C : (h + 1) * C, at : at + C] = zero


def pick(condition, first, second):
    return jnp.where(condition, first.astype(F32), second.astype(F32))


def by_row(frame, tmp):
    tmp[...] = frame.astype(F32)
    return [tmp[pl.ds(h, C, stride=H), :] for h in range(H)]


def back_kernel(
    flags, lat, cot, near, far, kernel, totals, scales, scaled, sums, tmp, window, taps, lat_v, cot_v, kernel_v, scaled_v, sem
):
    from_cot, from_kernel, from_lat = copies(sem, (cot, cot_v), (kernel, kernel_v), (lat, lat_v))
    from_cot.wait()
    for f in range(T + HALO):
        blocks = by_row(cot_v[f] if f < T else pick(flags[1] == 0, near[f - T], far[f - T]), tmp)
        for h in range(H):
            for s, moved in enumerate(shifted(blocks[h])):
                at = (s * H + h) * C
                window[at : at + C, f * W : (f + 1) * W] = moved.astype(BF16)
    clear(taps)
    from_kernel.wait()
    for kt in range(3):
        for ki in range(3):
            for kj in range(3):
                tap = kernel_v[9 * kt + 3 * ki + kj].astype(F32).T.astype(BF16)
                for h in range(H):
                    other = h + 1 - ki
                    if 0 <= other < H:
                        at = ((2 - kj) * H + other) * C
                        taps[2 - kt, h * C : (h + 1) * C, at : at + C] = tap
    back = jnp.dot(taps[0], window[:, 0 : T * W], preferred_element_type=F32)
    for f in range(1, 3):
        back = back + jnp.dot(taps[f], window[:, f * W : (f + T) * W], preferred_element_type=F32)
    center, inverse = center_inverse(totals, PER)
    from_lat.wait()
    first = jnp.zeros((C, W), F32)
    second = jnp.zeros((C, W), F32)
    for t in range(T):
        blocks = by_row(lat_v[t], tmp)
        for h in range(H):
            unit = (blocks[h] - center) * inverse
            normed = unit * scales[0] + scales[1]
            sig = 1.0 / (1.0 + jnp.exp(-normed))
            adjoint = back[h * C : (h + 1) * C, t * W : (t + 1) * W]
            value = adjoint * sig * (1.0 + normed * (1.0 - sig)) * scales[0]
            first = first + value
            second = second + value * unit
            scaled_v[t, pl.ds(h, C, stride=H), :] = value
    (to_scaled,) = copies(sem, (scaled_v, scaled))
    lane, sub = lanes(), rows()
    first = jnp.where(lane == sub // PER, jnp.sum(first, axis=1, keepdims=True), 0.0)
    second = jnp.where(lane == sub // PER + GROUPS, jnp.sum(second, axis=1, keepdims=True), 0.0)
    sums[...] = jnp.broadcast_to(jnp.sum(first + second, axis=0, keepdims=True), (8, W))
    to_scaled.wait()


def activated(block, center, inverse, scales):
    normed = (block - center) * inverse * scales[0] + scales[1]
    return (normed * (1.0 / (1.0 + jnp.exp(-normed)))).astype(BF16).astype(F32)


CONTRACT = (((1,), (1,)), ((), ()))
PLANE = H * W


def halves(core, grads):
    half = C // 2
    for ki in range(3):
        for kj in range(3):
            tap = grads[ki * C : (ki + 1) * C, kj * C : (kj + 1) * C]
            low, high = tap[:half], tap[half:]
            at = (3 * ki + kj) * half
            yield at, jnp.where(core == 0, low, high), jnp.where(core == 0, high, low)


def grad_kernel(flags, adj, totals, scales, window, keep, send, last, flat, window_v, sem):
    center, inverse = center_inverse(totals, PER)
    for t in range(T):
        for h in range(H):
            block = adj[3 * C :, (t * H + h) * W : (t * H + h + 1) * W].astype(F32)
            for s, moved in enumerate(shifted(activated(block, center, inverse, scales))):
                moved = moved.astype(BF16)
                window_v[(s * H + h) * C : (s * H + h + 1) * C, t * W : (t + 1) * W] = moved
                flat[s * C : (s + 1) * C, (t * H + h) * W : (t * H + h + 1) * W] = moved
                if t >= T - HALO:
                    at = ((t - T + HALO) * H + h) * W
                    last[s * C : (s + 1) * C, at : at + W] = moved
    (to_window,) = copies(sem, (window_v, window))
    for kt in range(3):
        ahead = 2 - kt
        grads = lax.dot_general(
            adj[: 3 * C, ahead * PLANE :], flat[:, : (T - ahead) * PLANE], CONTRACT, preferred_element_type=F32
        )
        for at, mine, other in halves(flags[1], grads):
            at += 9 * kt * (C // 2)
            keep[at : at + C // 2] = mine
            send[at : at + C // 2] = other
    keep[HALF:] = jnp.zeros((COMM - HALF, C), F32)
    send[HALF:] = jnp.zeros((COMM - HALF, C), F32)
    to_window.wait()


def edge_kernel(flags, keep_in, send_in, near, far, last, keep, send, tmp, adj):
    for f in range(HALO):
        put_adjoint(adj, f, by_row(pick(flags[1] == 0, near[f], far[f]), tmp))
    for kt in range(2):
        ahead = 2 - kt
        grads = lax.dot_general(
            adj[:, : ahead * PLANE], last[:, (HALO - ahead) * PLANE :], CONTRACT, preferred_element_type=F32
        )
        for at, mine, other in halves(flags[1], grads):
            at += 9 * kt * (C // 2)
            keep[at : at + C // 2] = keep_in[at : at + C // 2] + mine
            send[at : at + C // 2] = send_in[at : at + C // 2] + other


def add_kernel(keep, received, chip):
    chip[...] = (keep[...] + received[...]).astype(chip.dtype)


def part_kernel(parts, sums, packed):
    packed[:PART] = jnp.sum(parts[...].astype(F32), axis=0)
    packed[PART:] = sums[...]


def merge_kernel(own, one, two, three, parts, backward):
    total = (own[...] + one[...]) + (two[...] + three[...])
    part = total[:PART].astype(BF16)
    for i in range(SIDE):
        parts[i] = part
    backward[...] = own[PART:] + two[PART:]


def place_kernel(flags, half_grad, grad, grad_v, sem, first):
    half = C // 2
    core = flags[1] if first else 1 - flags[1]
    at = pl.multiple_of(core * half, half)
    started = []
    for kt in range(3):
        rows_of = half_grad[9 * kt * half : 9 * (kt + 1) * half].astype(F32)
        grad_v[9 * kt : 9 * (kt + 1)] = rows_of.reshape(9, half, C)
        taps = pl.ds(9 * kt, 9)
        started += copies(sem.at[pl.ds(kt, 1)], (grad_v.at[taps], grad.at[taps, pl.ds(at, half)]))
    for copy in started:
        copy.wait()


def place_first(flags, half_grad, grad, grad_v, sem):
    place_kernel(flags, half_grad, grad, grad_v, sem, True)


def place_second(flags, half_grad, grad_in, grad, grad_v, sem):
    place_kernel(flags, half_grad, grad, grad_v, sem, False)


def conv_kernel(
    flags, lat, near, far, kernel, window, totals, scales, output, tmp, taps, lat_v, kernel_v, window_v, output_v, sem, out_sem
):
    from_kernel, from_window, from_lat = copies(
        sem, (kernel, kernel_v), (window, window_v.at[:, HALO * W :]), (lat, lat_v)
    )
    center, inverse = center_inverse(totals, PER)
    for f in range(HALO):
        blocks = by_row(pick(flags[1] == 0, far[f], near[f]), tmp)
        for h in range(H):
            active = jnp.where(flags[0] > 0, activated(blocks[h], center, inverse, scales), 0.0)
            for s, moved in enumerate(shifted(active)):
                window_v[(s * H + h) * C : (s * H + h + 1) * C, f * W : (f + 1) * W] = moved.astype(BF16)
    clear(taps)
    from_kernel.wait()
    for kt in range(3):
        for ki in range(3):
            for kj in range(3):
                tap = kernel_v[9 * kt + 3 * ki + kj]
                for h in range(H):
                    other = h - 1 + ki
                    if 0 <= other < H:
                        at = (kj * H + other) * C
                        taps[kt, h * C : (h + 1) * C, at : at + C] = tap
    from_window.wait()
    total = jnp.dot(taps[0], window_v[:, 0 : T * W], preferred_element_type=F32)
    for f in range(1, 3):
        total = total + jnp.dot(taps[f], window_v[:, f * W : (f + T) * W], preferred_element_type=F32)
    from_lat.wait()
    started = []
    for t in range(T):
        for h in range(H):
            tmp[pl.ds(h, C, stride=H), :] = total[h * C : (h + 1) * C, t * W : (t + 1) * W]
        output_v[t] = (lat_v[t].astype(F32) + tmp[...]).astype(BF16)
        started += copies(out_sem.at[pl.ds(t, 1)], (output_v.at[t], output.at[t]))
    for copy in started:
        copy.wait()


def adjoint_kernel(
    lat, cot, totals, backward, scaled, result, lat_v, cot_v, scaled_v, result_v, lat_sem, cot_sem, scaled_sem, out_sem
):
    fetched = list(
        zip(
            *(
                copies(sem, *((source.at[t], target.at[t]) for t in range(T)))
                for sem, source, target in (
                    (lat_sem, lat, lat_v),
                    (cot_sem, cot, cot_v),
                    (scaled_sem, scaled, scaled_v),
                )
            )
        )
    )
    center, inverse = center_inverse(totals, PER * H)
    row = backward[...][0:1] / MEMBERS
    first = group_column(row, 0, PER * H)
    second = group_column(row, GROUPS, PER * H)
    started = []
    for t in range(T):
        for copy in fetched[t]:
            copy.wait()
        unit = (lat_v[t].astype(F32) - center) * inverse
        value = cot_v[t].astype(F32) + inverse * (scaled_v[t] - first - unit * second)
        result_v[t] = value.astype(BF16)
        started += copies(out_sem.at[pl.ds(t, 1)], (result_v.at[t], result.at[t]))
    for copy in started:
        copy.wait()


VMEM, HBM, SMEM = (
    pl.BlockSpec(memory_space=pltpu.VMEM),
    pl.BlockSpec(memory_space=pltpu.HBM),
    pl.BlockSpec(memory_space=pltpu.SMEM),
)


def call(body, out, scratch, *operands, far=(), out_far=(), scalars=0, flops=0, moved=1 << 20, aliases=(), limit=12):
    single = not isinstance(out, tuple)
    count = 1 if single else len(out)
    outs = tuple(HBM if i in out_far else VMEM for i in range(count))
    shapes = tuple(pltpu.HBM(o.shape, o.dtype) if i in out_far else o for i, o in enumerate((out,) if single else out))
    operands = [pltpu.with_memory_space_constraint(x, pltpu.HBM) if i in far else x for i, x in enumerate(operands)]
    return pl.pallas_call(
        body,
        out_shape=shapes[0] if single else shapes,
        in_specs=[SMEM if i < scalars else HBM if i in far else VMEM for i in range(len(operands))],
        out_specs=outs[0] if single else outs,
        scratch_shapes=scratch,
        compiler_params=pltpu.CompilerParams(vmem_limit_bytes=limit * MIB),
        input_output_aliases=dict(aliases),
        cost_estimate=pl.CostEstimate(flops=flops, bytes_accessed=moved, transcendentals=0),
    )(*operands)


def shape(*dims, dtype=F32):
    return jax.ShapeDtypeStruct(dims, dtype)


def sems(count):
    return pltpu.SemaphoreType.DMA((count,))


def swap(value, axis):
    return lax.ppermute(value, axis, [(0, 1), (1, 0)])


def exchange(parts, axes):
    return lax.all_to_all(parts, axes, 0, 0)


def per_device(latents, norm_gain, norm_shift, kernel, cotangent):
    lat = latents.reshape(T, ROWS, W)
    cot = cotangent.reshape(T, ROWS, W)
    gain, shift = norm_gain.reshape(1, C), norm_shift.reshape(1, C)
    zh, core = lax.axis_index("zh"), lax.axis_index("core")
    flags = jnp.stack([zh * 2 + core, core]).astype(jnp.int32)
    halo = shape(HALO, ROWS, W, dtype=BF16)
    frames = pltpu.VMEM((T, ROWS, W), BF16)
    tmp = pltpu.VMEM((ROWS, W), F32)
    row = pltpu.VMEM((1, C), F32)
    window_scratch = pltpu.VMEM((3 * ROWS, (T + HALO) * W), BF16)
    taps = pltpu.VMEM((3, ROWS, 3 * ROWS), BF16)
    kernel_scratch = pltpu.VMEM((27, C, C), BF16)
    scaled_scratch = pltpu.VMEM((T, ROWS, W), F32)
    own = call(start_kernel, shape(8, W), [frames, sems(T)], lat, far=(0,))
    gain, own = lax.optimization_barrier((gain, own))
    adj, scales, to_near, to_far = call(
        prepare_kernel,
        (shape(4 * C, T * PLANE, dtype=BF16), shape(2, C, W), halo, halo),
        [frames, frames, row, row, tmp, sems(4), sems(2)],
        flags,
        lat,
        cot,
        gain,
        shift,
        far=(1, 2, 3, 4),
        scalars=1,
    )
    slab = ("zh", "core")
    before = lax.ppermute(to_far, slab, [(1, 2), (2, 1)])
    far = before
    across, scales = lax.optimization_barrier((swap(own, "zh"), scales))
    pair = own + across
    to_near, pair = lax.optimization_barrier((to_near, pair))
    near = swap(to_near, "core")
    totals = jnp.concatenate([pair, swap(pair, "core")], axis=0)
    window, keep, send, last = call(
        grad_kernel,
        (
            shape(3 * ROWS, T * W, dtype=BF16),
            shape(COMM, C),
            shape(COMM, C),
            shape(3 * C, HALO * PLANE, dtype=BF16),
        ),
        [pltpu.VMEM((3 * C, T * PLANE), BF16), pltpu.VMEM((3 * ROWS, T * W), BF16), sems(1)],
        flags,
        adj,
        totals,
        scales,
        out_far=(0,),
        scalars=1,
        flops=2 * 10**9,
    )
    near, far, last = lax.optimization_barrier((near, far, last))
    keep, send = call(
        edge_kernel,
        (shape(COMM, C), shape(COMM, C)),
        [tmp, pltpu.VMEM((3 * C, HALO * PLANE), BF16)],
        flags,
        keep,
        send,
        near,
        far,
        last,
        scalars=1,
        aliases=((1, 0), (2, 1)),
    )
    chip = call(add_kernel, shape(COMM, C, dtype=WIRE), [], keep, swap(send, "core"))
    parts = exchange(chip.reshape(SIDE, PART, C), ("y", "zn", "x"))
    scaled, sums = call(
        back_kernel,
        (shape(T, ROWS, W), shape(8, W)),
        [tmp, window_scratch, taps, frames, frames, kernel_scratch, scaled_scratch, sems(3)],
        flags,
        lat,
        cot,
        near,
        far,
        kernel,
        totals,
        scales,
        far=(1, 2, 5),
        out_far=(0,),
        scalars=1,
        limit=20,
        flops=4 * 10**9,
    )
    sums, window = lax.optimization_barrier((sums, window))
    sums = sums + swap(sums, "core")
    output = call(
        conv_kernel,
        shape(T, ROWS, W, dtype=BF16),
        [tmp, taps, frames, kernel_scratch, window_scratch, frames, sems(3), sems(T)],
        flags,
        lat,
        near,
        far,
        kernel,
        window,
        totals,
        scales,
        far=(1, 4, 5),
        out_far=(0,),
        limit=20,
        scalars=1,
        flops=4 * 10**9,
    )
    parts, output = lax.optimization_barrier((parts, output))
    packed = call(part_kernel, shape(PART + 8, C), [], parts, sums)
    others = [lax.ppermute(packed, ("zh", "zm"), [(i, i ^ flip) for i in range(4)]) for flip in (1, 2, 3)]
    part, backward = call(
        merge_kernel, (shape(SIDE, PART, C, dtype=BF16), shape(8, C)), [], packed, *others
    )
    result = call(
        adjoint_kernel,
        shape(T, ROWS, W, dtype=BF16),
        [frames, frames, scaled_scratch, frames, sems(T), sems(T), sems(T), sems(T)],
        lat,
        cot,
        totals,
        backward,
        scaled,
        far=(0, 1, 4),
        out_far=(0,),
        flops=10**9,
    )
    mine, result = lax.optimization_barrier((exchange(part, ("y", "zn", "x")).reshape(COMM, C), result))
    other = swap(mine, "core")
    half_scratch = [pltpu.VMEM((27, C // 2, C), F32), sems(3)]
    kernel_grad = call(
        place_first, shape(27, C, C), half_scratch, flags, mine, out_far=(0,), scalars=1, flops=10**9
    )
    kernel_grad = call(
        place_second,
        shape(27, C, C),
        half_scratch,
        flags,
        other,
        kernel_grad,
        far=(2,),
        out_far=(0,),
        scalars=1,
        aliases=((2, 0),),
    )
    return output.reshape(latents.shape), result.reshape(latents.shape), kernel_grad


WIRE = F32


def solution(mesh):
    fine = Mesh(mesh.devices.reshape(2, 2, 4, 2, 2, 4), ("zh", "core", "y", "zm", "zn", "x"))
    frames = P(("y", "zm", "zn", "x"), ("zh", "core"), None, None, None)
    return jax.shard_map(
        per_device,
        mesh=fine,
        in_specs=(frames, P(), P(), P(), frames),
        out_specs=(frames, frames, P()),
        check_vma=False,
    )
```

```python
import functools

import jax
import jax.numpy as jnp
from jax import lax
from jax.experimental import pallas as pl
from jax.experimental.pallas import tpu as pltpu
from jax.sharding import Mesh
from jax.sharding import PartitionSpec as P

C = 128
H = 4
W = 128
T = 4
HALO = 2
GROUPS = 32
PER = C // GROUPS
SLABS = 4
MEMBERS = SLABS * T * PER * H * W
ROWS = H * C
HALF = 27 * (C // 2)
COMM = HALF + 64
SIDE = 32
PART = COMM // SIDE
F32 = jnp.float32
BF16 = jnp.bfloat16
MIB = 1024 * 1024


def lanes():
    return lax.broadcasted_iota(jnp.int32, (C, W), 1)


def rows():
    return lax.broadcasted_iota(jnp.int32, (C, W), 0)


def shifted(block):
    left = jnp.where(lanes() == 0, 0.0, pltpu.roll(block, 1, 1))
    right = jnp.where(lanes() == W - 1, 0.0, pltpu.roll(block, W - 1, 1))
    return left, block, right


def row_of(column, offset):
    lane = lax.broadcasted_iota(jnp.int32, (GROUPS, W), 1)
    sub = lax.broadcasted_iota(jnp.int32, (GROUPS, W), 0)
    return jnp.sum(jnp.where(lane == sub + offset, column, 0.0), axis=0, keepdims=True)


def channel_column(row):
    return jnp.sum(jnp.where(lanes() == rows(), row, 0.0), axis=1, keepdims=True)


def group_column(row, offset, per_channel):
    lane = lax.broadcasted_iota(jnp.int32, (GROUPS * per_channel, W), 1)
    sub = lax.broadcasted_iota(jnp.int32, (GROUPS * per_channel, W), 0)
    return jnp.sum(jnp.where(lane == sub // per_channel + offset, row, 0.0), axis=1, keepdims=True)


def center_inverse(totals, per_channel):
    row = jnp.sum(totals[...].reshape(-1, 8, W), axis=0)[0:1] / MEMBERS
    center = group_column(row, 0, per_channel)
    square = group_column(row, GROUPS, per_channel)
    return center, lax.rsqrt(square - center * center + 1e-06)


def copies(sem, *pairs):
    started = [pltpu.make_async_copy(source, target, sem.at[i]) for i, (source, target) in enumerate(pairs)]
    for copy in started:
        copy.start()
    return started


def start_kernel(lat, sums, lat_v, sem):
    parts = copies(sem, *((lat.at[t], lat_v.at[t]) for t in range(T)))
    total = jnp.zeros((ROWS, W), F32)
    square = jnp.zeros((ROWS, W), F32)
    for t in range(T):
        parts[t].wait()
        x = lat_v[t].astype(F32)
        total = total + x
        square = square + x * x
    total = jnp.sum(jnp.sum(total.reshape(GROUPS, -1, W), axis=1), axis=1, keepdims=True)
    square = jnp.sum(jnp.sum(square.reshape(GROUPS, -1, W), axis=1), axis=1, keepdims=True)
    row = row_of(total, 0) + row_of(square, GROUPS)
    sums[...] = jnp.broadcast_to(row, (8, W))


def put_adjoint(adj, f, mine):
    zero = jnp.zeros((C, W), BF16)
    for h in range(H):
        for ki in range(3):
            source = h - ki + 1
            block = mine[source].astype(BF16) if 0 <= source < H else zero
            adj[ki * C : (ki + 1) * C, (f * H + h) * W : (f * H + h + 1) * W] = block


def halo_kernel(flags, sums, lat, cot, near, far, sem):
    tail, head = lat.at[T - HALO :], cot.at[:HALO]

    @pl.when(flags[1] == 0)
    def _():
        copies(sem, (tail, near), (head, far))

    @pl.when(flags[1] != 0)
    def _():
        copies(sem, (head, near), (tail, far))

    pltpu.make_async_copy(tail, near, sem.at[0]).wait()
    pltpu.make_async_copy(head, far, sem.at[1]).wait()


def prepare_kernel(lat, cot, gain, shift, adj, scales, lat_v, cot_v, gain_v, shift_v, tmp, sem):
    from_lat, from_cot, *small = copies(sem, (lat, lat_v), (cot, cot_v), (gain, gain_v), (shift, shift_v))
    from_lat.wait()
    for t in range(T):
        for h, block in enumerate(by_row(lat_v[t], tmp)):
            adj[3 * C :, (t * H + h) * W : (t * H + h + 1) * W] = block.astype(BF16)
    from_cot.wait()
    for t in range(T):
        put_adjoint(adj, t, by_row(cot_v[t], tmp))
    for copy in small:
        copy.wait()
    scales[0] = jnp.broadcast_to(channel_column(gain_v[...]), (C, W))
    scales[1] = jnp.broadcast_to(channel_column(shift_v[...]), (C, W))


def clear(taps):
    zero = jnp.zeros((C, C), BF16)
    for f in range(3):
        for s in range(3):
            for h in range(H):
                for other in range(H):
                    if abs(h - other) > 1:
                        at = (s * H + other) * C
                        taps[f, h * C : (h + 1) * C, at : at + C] = zero


def pick(condition, first, second):
    return jnp.where(condition, first.astype(F32), second.astype(F32))


def by_row(frame, tmp):
    tmp[...] = frame.astype(F32)
    return [tmp[pl.ds(h, C, stride=H), :] for h in range(H)]


def back_kernel(
    flags, lat, cot, near, far, kernel, totals, scales, scaled, sums, tmp, window, taps, lat_v, cot_v, kernel_v, scaled_v, sem
):
    from_cot, from_kernel, from_lat = copies(sem, (cot, cot_v), (kernel, kernel_v), (lat, lat_v))
    from_cot.wait()
    for f in range(T + HALO):
        blocks = by_row(cot_v[f] if f < T else pick(flags[1] == 0, near[f - T], far[f - T]), tmp)
        for h in range(H):
            for s, moved in enumerate(shifted(blocks[h])):
                at = (s * H + h) * C
                window[at : at + C, f * W : (f + 1) * W] = moved.astype(BF16)
    clear(taps)
    from_kernel.wait()
    for kt in range(3):
        for ki in range(3):
            for kj in range(3):
                tap = kernel_v[9 * kt + 3 * ki + kj].astype(F32).T.astype(BF16)
                for h in range(H):
                    other = h + 1 - ki
                    if 0 <= other < H:
                        at = ((2 - kj) * H + other) * C
                        taps[2 - kt, h * C : (h + 1) * C, at : at + C] = tap
    back = jnp.dot(taps[0], window[:, 0 : T * W], preferred_element_type=F32)
    for f in range(1, 3):
        back = back + jnp.dot(taps[f], window[:, f * W : (f + T) * W], preferred_element_type=F32)
    center, inverse = center_inverse(totals, PER)
    from_lat.wait()
    first = jnp.zeros((C, W), F32)
    second = jnp.zeros((C, W), F32)
    for t in range(T):
        blocks = by_row(lat_v[t], tmp)
        for h in range(H):
            unit = (blocks[h] - center) * inverse
            normed = unit * scales[0] + scales[1]
            sig = 1.0 / (1.0 + jnp.exp(-normed))
            adjoint = back[h * C : (h + 1) * C, t * W : (t + 1) * W]
            value = adjoint * sig * (1.0 + normed * (1.0 - sig)) * scales[0]
            first = first + value
            second = second + value * unit
            scaled_v[t, pl.ds(h, C, stride=H), :] = value
    (to_scaled,) = copies(sem, (scaled_v, scaled))
    lane, sub = lanes(), rows()
    first = jnp.where(lane == sub // PER, jnp.sum(first, axis=1, keepdims=True), 0.0)
    second = jnp.where(lane == sub // PER + GROUPS, jnp.sum(second, axis=1, keepdims=True), 0.0)
    sums[...] = jnp.broadcast_to(jnp.sum(first + second, axis=0, keepdims=True), (8, W))
    to_scaled.wait()


def activated(block, center, inverse, scales):
    normed = (block - center) * inverse * scales[0] + scales[1]
    return (normed * (1.0 / (1.0 + jnp.exp(-normed)))).astype(BF16).astype(F32)


CONTRACT = (((1,), (1,)), ((), ()))
PLANE = H * W


def halves(core, grads):
    half = C // 2
    for ki in range(3):
        for kj in range(3):
            tap = grads[ki * C : (ki + 1) * C, kj * C : (kj + 1) * C]
            low, high = tap[:half], tap[half:]
            at = (3 * ki + kj) * half
            yield at, jnp.where(core == 0, low, high), jnp.where(core == 0, high, low)


def grad_kernel(flags, adj, totals, scales, window, keep, send, last, flat, window_v, sem):
    center, inverse = center_inverse(totals, PER)
    for t in range(T):
        for h in range(H):
            block = adj[3 * C :, (t * H + h) * W : (t * H + h + 1) * W].astype(F32)
            for s, moved in enumerate(shifted(activated(block, center, inverse, scales))):
                moved = moved.astype(BF16)
                window_v[(s * H + h) * C : (s * H + h + 1) * C, t * W : (t + 1) * W] = moved
                flat[s * C : (s + 1) * C, (t * H + h) * W : (t * H + h + 1) * W] = moved
                if t >= T - HALO:
                    at = ((t - T + HALO) * H + h) * W
                    last[s * C : (s + 1) * C, at : at + W] = moved
    (to_window,) = copies(sem, (window_v, window))
    for kt in range(3):
        ahead = 2 - kt
        grads = lax.dot_general(
            adj[: 3 * C, ahead * PLANE :], flat[:, : (T - ahead) * PLANE], CONTRACT, preferred_element_type=F32
        )
        for at, mine, other in halves(flags[1], grads):
            at += 9 * kt * (C // 2)
            keep[at : at + C // 2] = mine
            send[at : at + C // 2] = other
    keep[HALF:] = jnp.zeros((COMM - HALF, C), F32)
    send[HALF:] = jnp.zeros((COMM - HALF, C), F32)
    to_window.wait()


def edge_kernel(flags, keep_in, send_in, near, far, last, keep, send, tmp, adj):
    for f in range(HALO):
        put_adjoint(adj, f, by_row(pick(flags[1] == 0, near[f], far[f]), tmp))
    for kt in range(2):
        ahead = 2 - kt
        grads = lax.dot_general(
            adj[:, : ahead * PLANE], last[:, (HALO - ahead) * PLANE :], CONTRACT, preferred_element_type=F32
        )
        for at, mine, other in halves(flags[1], grads):
            at += 9 * kt * (C // 2)
            keep[at : at + C // 2] = keep_in[at : at + C // 2] + mine
            send[at : at + C // 2] = send_in[at : at + C // 2] + other


def add_kernel(keep, received, chip):
    chip[...] = (keep[...] + received[...]).astype(chip.dtype)


def part_kernel(parts, sums, packed):
    packed[:PART] = jnp.sum(parts[...].astype(F32), axis=0)
    packed[PART:] = sums[...]


def merge_kernel(own, one, two, three, parts, backward):
    total = (own[...] + one[...]) + (two[...] + three[...])
    part = total[:PART].astype(BF16)
    for i in range(SIDE):
        parts[i] = part
    backward[...] = own[PART:] + two[PART:]


def place_kernel(flags, half_grad, grad, grad_v, sem, first):
    half = C // 2
    core = flags[1] if first else 1 - flags[1]
    at = pl.multiple_of(core * half, half)
    started = []
    for kt in range(3):
        rows_of = half_grad[9 * kt * half : 9 * (kt + 1) * half].astype(F32)
        grad_v[9 * kt : 9 * (kt + 1)] = rows_of.reshape(9, half, C)
        taps = pl.ds(9 * kt, 9)
        started += copies(sem.at[pl.ds(kt, 1)], (grad_v.at[taps], grad.at[taps, pl.ds(at, half)]))
    for copy in started:
        copy.wait()


def place_first(flags, half_grad, grad, grad_v, sem):
    place_kernel(flags, half_grad, grad, grad_v, sem, True)


def place_second(flags, half_grad, grad_in, grad, grad_v, sem):
    place_kernel(flags, half_grad, grad, grad_v, sem, False)


def finish_kernel(
    flags,
    lat,
    cot,
    near,
    far,
    kernel,
    window,
    totals,
    scales,
    backward,
    scaled,
    output,
    result,
    tmp,
    taps,
    lat_v,
    cot_v,
    kernel_v,
    window_v,
    scaled_v,
    output_v,
    result_v,
    sem,
    out_sem,
):
    from_kernel, from_window, from_lat, from_cot, from_scaled = copies(
        sem,
        (kernel, kernel_v),
        (window, window_v.at[:, HALO * W :]),
        (lat, lat_v),
        (cot, cot_v),
        (scaled, scaled_v),
    )
    center, inverse = center_inverse(totals, PER)
    for f in range(HALO):
        blocks = by_row(pick(flags[1] == 0, far[f], near[f]), tmp)
        for h in range(H):
            active = jnp.where(flags[0] > 0, activated(blocks[h], center, inverse, scales), 0.0)
            for s, moved in enumerate(shifted(active)):
                window_v[(s * H + h) * C : (s * H + h + 1) * C, f * W : (f + 1) * W] = moved.astype(BF16)
    clear(taps)
    from_kernel.wait()
    for kt in range(3):
        for ki in range(3):
            for kj in range(3):
                tap = kernel_v[9 * kt + 3 * ki + kj]
                for h in range(H):
                    other = h - 1 + ki
                    if 0 <= other < H:
                        at = (kj * H + other) * C
                        taps[kt, h * C : (h + 1) * C, at : at + C] = tap
    from_window.wait()
    total = jnp.dot(taps[0], window_v[:, 0 : T * W], preferred_element_type=F32)
    for f in range(1, 3):
        total = total + jnp.dot(taps[f], window_v[:, f * W : (f + T) * W], preferred_element_type=F32)
    center, inverse = center_inverse(totals, PER * H)
    row = backward[...][0:1] / MEMBERS
    first = group_column(row, 0, PER * H)
    second = group_column(row, GROUPS, PER * H)
    for copy in (from_lat, from_cot, from_scaled):
        copy.wait()
    started = []
    for t in range(T):
        frame = lat_v[t].astype(F32)
        value = cot_v[t].astype(F32) + inverse * (scaled_v[t] - first - (frame - center) * inverse * second)
        result_v[t] = value.astype(BF16)
        started += copies(out_sem.at[pl.ds(T + t, 1)], (result_v.at[t], result.at[t]))
        for h in range(H):
            tmp[pl.ds(h, C, stride=H), :] = total[h * C : (h + 1) * C, t * W : (t + 1) * W]
        output_v[t] = (frame + tmp[...]).astype(BF16)
        started += copies(out_sem.at[pl.ds(t, 1)], (output_v.at[t], output.at[t]))
    for copy in started:
        copy.wait()


VMEM, HBM, SMEM = (
    pl.BlockSpec(memory_space=pltpu.VMEM),
    pl.BlockSpec(memory_space=pltpu.HBM),
    pl.BlockSpec(memory_space=pltpu.SMEM),
)


def call(body, out, scratch, *operands, far=(), out_far=(), scalars=0, flops=0, moved=1 << 20, aliases=(), limit=12):
    single = not isinstance(out, tuple)
    count = 1 if single else len(out)
    outs = tuple(HBM if i in out_far else VMEM for i in range(count))
    shapes = tuple(pltpu.HBM(o.shape, o.dtype) if i in out_far else o for i, o in enumerate((out,) if single else out))
    operands = [pltpu.with_memory_space_constraint(x, pltpu.HBM) if i in far else x for i, x in enumerate(operands)]
    return pl.pallas_call(
        body,
        out_shape=shapes[0] if single else shapes,
        in_specs=[SMEM if i < scalars else HBM if i in far else VMEM for i in range(len(operands))],
        out_specs=outs[0] if single else outs,
        scratch_shapes=scratch,
        compiler_params=pltpu.CompilerParams(vmem_limit_bytes=limit * MIB),
        input_output_aliases=dict(aliases),
        cost_estimate=pl.CostEstimate(flops=flops, bytes_accessed=moved, transcendentals=0),
    )(*operands)


def shape(*dims, dtype=F32):
    return jax.ShapeDtypeStruct(dims, dtype)


def sems(count):
    return pltpu.SemaphoreType.DMA((count,))


def swap(value, axis):
    return lax.ppermute(value, axis, [(0, 1), (1, 0)])


def exchange(parts, axes):
    return lax.all_to_all(parts, axes, 0, 0)


def per_device(latents, norm_gain, norm_shift, kernel, cotangent):
    lat = latents.reshape(T, ROWS, W)
    cot = cotangent.reshape(T, ROWS, W)
    gain, shift = norm_gain.reshape(1, C), norm_shift.reshape(1, C)
    zh, core = lax.axis_index("zh"), lax.axis_index("core")
    flags = jnp.stack([zh * 2 + core, core]).astype(jnp.int32)
    halo = shape(HALO, ROWS, W, dtype=BF16)
    frames = pltpu.VMEM((T, ROWS, W), BF16)
    tmp = pltpu.VMEM((ROWS, W), F32)
    row = pltpu.VMEM((1, C), F32)
    window_scratch = pltpu.VMEM((3 * ROWS, (T + HALO) * W), BF16)
    taps = pltpu.VMEM((3, ROWS, 3 * ROWS), BF16)
    kernel_scratch = pltpu.VMEM((27, C, C), BF16)
    scaled_scratch = pltpu.VMEM((T, ROWS, W), F32)
    own = call(start_kernel, shape(8, W), [frames, sems(T)], lat, far=(0,))
    to_near, to_far = call(halo_kernel, (halo, halo), [sems(2)], flags, own, lat, cot, far=(2, 3), scalars=1)
    gain, to_far = lax.optimization_barrier((gain, to_far))
    adj, scales = call(
        prepare_kernel,
        (shape(4 * C, T * PLANE, dtype=BF16), shape(2, C, W)),
        [frames, frames, row, row, tmp, sems(4)],
        lat,
        cot,
        gain,
        shift,
        far=(0, 1, 2, 3),
        flops=0,
    )
    slab = ("zh", "core")
    before = lax.ppermute(to_far, slab, [(1, 2), (2, 1)])
    far = before
    across, scales = lax.optimization_barrier((swap(own, "zh"), scales))
    pair = own + across
    to_near, pair = lax.optimization_barrier((to_near, pair))
    near = swap(to_near, "core")
    totals = jnp.concatenate([pair, swap(pair, "core")], axis=0)
    window, keep, send, last = call(
        grad_kernel,
        (
            shape(3 * ROWS, T * W, dtype=BF16),
            shape(COMM, C),
            shape(COMM, C),
            shape(3 * C, HALO * PLANE, dtype=BF16),
        ),
        [pltpu.VMEM((3 * C, T * PLANE), BF16), pltpu.VMEM((3 * ROWS, T * W), BF16), sems(1)],
        flags,
        adj,
        totals,
        scales,
        out_far=(0,),
        scalars=1,
        flops=2 * 10**9,
    )
    near, far, last = lax.optimization_barrier((near, far, last))
    keep, send = call(
        edge_kernel,
        (shape(COMM, C), shape(COMM, C)),
        [tmp, pltpu.VMEM((3 * C, HALO * PLANE), BF16)],
        flags,
        keep,
        send,
        near,
        far,
        last,
        scalars=1,
        aliases=((1, 0), (2, 1)),
    )
    chip = call(add_kernel, shape(COMM, C, dtype=WIRE), [], keep, swap(send, "core"))
    parts = exchange(chip.reshape(SIDE, PART, C), ("y", "zn", "x"))
    scaled, sums = call(
        back_kernel,
        (shape(T, ROWS, W), shape(8, W)),
        [tmp, window_scratch, taps, frames, frames, kernel_scratch, scaled_scratch, sems(3)],
        flags,
        lat,
        cot,
        near,
        far,
        kernel,
        totals,
        scales,
        far=(1, 2, 5),
        out_far=(0,),
        scalars=1,
        limit=20,
        flops=4 * 10**9,
    )
    sums = sums + swap(sums, "core")
    packed = call(part_kernel, shape(PART + 8, C), [], parts, sums)
    others = [lax.ppermute(packed, ("zh", "zm"), [(i, i ^ flip) for i in range(4)]) for flip in (1, 2, 3)]
    part, backward = call(
        merge_kernel, (shape(SIDE, PART, C, dtype=BF16), shape(8, C)), [], packed, *others
    )
    part, window = lax.optimization_barrier((part, window))
    block = shape(T, ROWS, W, dtype=BF16)
    output, result = call(
        finish_kernel,
        (block, block),
        [tmp, taps, frames, frames, kernel_scratch, window_scratch, scaled_scratch, frames, frames, sems(5), sems(2 * T)],
        flags,
        lat,
        cot,
        near,
        far,
        kernel,
        window,
        totals,
        scales,
        backward,
        scaled,
        far=(1, 2, 5, 6, 10),
        out_far=(0, 1),
        limit=20,
        scalars=1,
        flops=4 * 10**9,
    )
    mine, output, result = lax.optimization_barrier(
        (exchange(part, ("y", "zn", "x")).reshape(COMM, C), output, result)
    )
    other = swap(mine, "core")
    half_scratch = [pltpu.VMEM((27, C // 2, C), F32), sems(3)]
    kernel_grad = call(
        place_first, shape(27, C, C), half_scratch, flags, mine, out_far=(0,), scalars=1, flops=10**9
    )
    kernel_grad = call(
        place_second,
        shape(27, C, C),
        half_scratch,
        flags,
        other,
        kernel_grad,
        far=(2,),
        out_far=(0,),
        scalars=1,
        aliases=((2, 0),),
    )
    return output.reshape(latents.shape), result.reshape(latents.shape), kernel_grad


WIRE = F32


def solution(mesh):
    fine = Mesh(mesh.devices.reshape(2, 2, 4, 2, 2, 4), ("zh", "core", "y", "zm", "zn", "x"))
    frames = P(("y", "zm", "zn", "x"), ("zh", "core"), None, None, None)
    return jax.shard_map(
        per_device,
        mesh=fine,
        in_specs=(frames, P(), P(), P(), frames),
        out_specs=(frames, frames, P()),
        check_vma=False,
    )
```

```python
import functools

import jax
import jax.numpy as jnp
from jax import lax
from jax.experimental import pallas as pl
from jax.experimental.pallas import tpu as pltpu
from jax.sharding import Mesh
from jax.sharding import PartitionSpec as P

C = 128
H = 4
W = 128
T = 4
HALO = 2
GROUPS = 32
PER = C // GROUPS
SLABS = 4
MEMBERS = SLABS * T * PER * H * W
ROWS = H * C
HALF = 27 * (C // 2)
COMM = HALF + 64
SIDE = 32
PART = COMM // SIDE
F32 = jnp.float32
BF16 = jnp.bfloat16
MIB = 1024 * 1024


def lanes():
    return lax.broadcasted_iota(jnp.int32, (C, W), 1)


def rows():
    return lax.broadcasted_iota(jnp.int32, (C, W), 0)


def shifted(block):
    left = jnp.where(lanes() == 0, 0.0, pltpu.roll(block, 1, 1))
    right = jnp.where(lanes() == W - 1, 0.0, pltpu.roll(block, W - 1, 1))
    return left, block, right


def row_of(column, offset):
    lane = lax.broadcasted_iota(jnp.int32, (GROUPS, W), 1)
    sub = lax.broadcasted_iota(jnp.int32, (GROUPS, W), 0)
    return jnp.sum(jnp.where(lane == sub + offset, column, 0.0), axis=0, keepdims=True)


def channel_column(row):
    return jnp.sum(jnp.where(lanes() == rows(), row, 0.0), axis=1, keepdims=True)


def group_column(row, offset, per_channel):
    lane = lax.broadcasted_iota(jnp.int32, (GROUPS * per_channel, W), 1)
    sub = lax.broadcasted_iota(jnp.int32, (GROUPS * per_channel, W), 0)
    return jnp.sum(jnp.where(lane == sub // per_channel + offset, row, 0.0), axis=1, keepdims=True)


def center_inverse(totals, per_channel):
    row = jnp.sum(totals[...].reshape(-1, 8, W), axis=0)[0:1] / MEMBERS
    center = group_column(row, 0, per_channel)
    square = group_column(row, GROUPS, per_channel)
    return center, lax.rsqrt(square - center * center + 1e-06)


def copies(sem, *pairs):
    started = [pltpu.make_async_copy(source, target, sem.at[i]) for i, (source, target) in enumerate(pairs)]
    for copy in started:
        copy.start()
    return started


def start_kernel(lat, sums, lat_v, sem):
    parts = copies(sem, *((lat.at[t], lat_v.at[t]) for t in range(T)))
    total = jnp.zeros((ROWS, W), F32)
    square = jnp.zeros((ROWS, W), F32)
    for t in range(T):
        parts[t].wait()
        x = lat_v[t].astype(F32)
        total = total + x
        square = square + x * x
    total = jnp.sum(jnp.sum(total.reshape(GROUPS, -1, W), axis=1), axis=1, keepdims=True)
    square = jnp.sum(jnp.sum(square.reshape(GROUPS, -1, W), axis=1), axis=1, keepdims=True)
    row = row_of(total, 0) + row_of(square, GROUPS)
    sums[...] = jnp.broadcast_to(row, (8, W))


def put_adjoint(adj, f, mine):
    zero = jnp.zeros((C, W), BF16)
    for h in range(H):
        for ki in range(3):
            source = h - ki + 1
            block = mine[source].astype(BF16) if 0 <= source < H else zero
            adj[ki * C : (ki + 1) * C, (f * H + h) * W : (f * H + h + 1) * W] = block


def halo_kernel(flags, sums, lat, cot, near, far, sem):
    tail, head = lat.at[T - HALO :], cot.at[:HALO]

    @pl.when(flags[1] == 0)
    def _():
        copies(sem, (tail, near), (head, far))

    @pl.when(flags[1] != 0)
    def _():
        copies(sem, (head, near), (tail, far))

    pltpu.make_async_copy(tail, near, sem.at[0]).wait()
    pltpu.make_async_copy(head, far, sem.at[1]).wait()


def prepare_kernel(lat, cot, gain, shift, adj, scales, lat_v, cot_v, gain_v, shift_v, tmp, sem):
    from_lat, from_cot, *small = copies(sem, (lat, lat_v), (cot, cot_v), (gain, gain_v), (shift, shift_v))
    from_lat.wait()
    for t in range(T):
        for h, block in enumerate(by_row(lat_v[t], tmp)):
            adj[3 * C :, (t * H + h) * W : (t * H + h + 1) * W] = block.astype(BF16)
    from_cot.wait()
    for t in range(T):
        put_adjoint(adj, t, by_row(cot_v[t], tmp))
    for copy in small:
        copy.wait()
    scales[0] = jnp.broadcast_to(channel_column(gain_v[...]), (C, W))
    scales[1] = jnp.broadcast_to(channel_column(shift_v[...]), (C, W))


def clear(taps):
    zero = jnp.zeros((C, C), BF16)
    for f in range(3):
        for s in range(3):
            for h in range(H):
                for other in range(H):
                    if abs(h - other) > 1:
                        at = (s * H + other) * C
                        taps[f, h * C : (h + 1) * C, at : at + C] = zero


def pick(condition, first, second):
    return jnp.where(condition, first.astype(F32), second.astype(F32))


def by_row(frame, tmp):
    tmp[...] = frame.astype(F32)
    return [tmp[pl.ds(h, C, stride=H), :] for h in range(H)]


def back_kernel(
    flags, lat, cot, near, far, kernel, totals, scales, scaled, sums, tmp, window, taps, lat_v, cot_v, kernel_v, scaled_v, sem
):
    from_cot, from_kernel, from_lat = copies(sem, (cot, cot_v), (kernel, kernel_v), (lat, lat_v))
    from_cot.wait()
    for f in range(T + HALO):
        blocks = by_row(cot_v[f] if f < T else pick(flags[1] == 0, near[f - T], far[f - T]), tmp)
        for h in range(H):
            for s, moved in enumerate(shifted(blocks[h])):
                at = (s * H + h) * C
                window[at : at + C, f * W : (f + 1) * W] = moved.astype(BF16)
    clear(taps)
    from_kernel.wait()
    for kt in range(3):
        for ki in range(3):
            for kj in range(3):
                tap = kernel_v[9 * kt + 3 * ki + kj].astype(F32).T.astype(BF16)
                for h in range(H):
                    other = h + 1 - ki
                    if 0 <= other < H:
                        at = ((2 - kj) * H + other) * C
                        taps[2 - kt, h * C : (h + 1) * C, at : at + C] = tap
    back = jnp.dot(taps[0], window[:, 0 : T * W], preferred_element_type=F32)
    for f in range(1, 3):
        back = back + jnp.dot(taps[f], window[:, f * W : (f + T) * W], preferred_element_type=F32)
    center, inverse = center_inverse(totals, PER)
    from_lat.wait()
    first = jnp.zeros((C, W), F32)
    second = jnp.zeros((C, W), F32)
    for t in range(T):
        blocks = by_row(lat_v[t], tmp)
        for h in range(H):
            unit = (blocks[h] - center) * inverse
            normed = unit * scales[0] + scales[1]
            sig = 1.0 / (1.0 + jnp.exp(-normed))
            adjoint = back[h * C : (h + 1) * C, t * W : (t + 1) * W]
            value = adjoint * sig * (1.0 + normed * (1.0 - sig)) * scales[0]
            first = first + value
            second = second + value * unit
            scaled_v[t, pl.ds(h, C, stride=H), :] = value
    (to_scaled,) = copies(sem, (scaled_v, scaled))
    lane, sub = lanes(), rows()
    first = jnp.where(lane == sub // PER, jnp.sum(first, axis=1, keepdims=True), 0.0)
    second = jnp.where(lane == sub // PER + GROUPS, jnp.sum(second, axis=1, keepdims=True), 0.0)
    sums[...] = jnp.broadcast_to(jnp.sum(first + second, axis=0, keepdims=True), (8, W))
    to_scaled.wait()


def activated(block, center, inverse, scales):
    normed = (block - center) * inverse * scales[0] + scales[1]
    return (normed * (1.0 / (1.0 + jnp.exp(-normed)))).astype(BF16).astype(F32)


CONTRACT = (((1,), (1,)), ((), ()))
PLANE = H * W


def halves(core, grads):
    half = C // 2
    for ki in range(3):
        for kj in range(3):
            tap = grads[ki * C : (ki + 1) * C, kj * C : (kj + 1) * C]
            low, high = tap[:half], tap[half:]
            at = (3 * ki + kj) * half
            yield at, jnp.where(core == 0, low, high), jnp.where(core == 0, high, low)


def grad_kernel(flags, adj, totals, scales, window, keep, send, last, flat, window_v, sem):
    center, inverse = center_inverse(totals, PER)
    for t in range(T):
        for h in range(H):
            block = adj[3 * C :, (t * H + h) * W : (t * H + h + 1) * W].astype(F32)
            for s, moved in enumerate(shifted(activated(block, center, inverse, scales))):
                moved = moved.astype(BF16)
                window_v[(s * H + h) * C : (s * H + h + 1) * C, t * W : (t + 1) * W] = moved
                flat[s * C : (s + 1) * C, (t * H + h) * W : (t * H + h + 1) * W] = moved
                if t >= T - HALO:
                    at = ((t - T + HALO) * H + h) * W
                    last[s * C : (s + 1) * C, at : at + W] = moved
    (to_window,) = copies(sem, (window_v, window))
    for kt in range(3):
        ahead = 2 - kt
        grads = lax.dot_general(
            adj[: 3 * C, ahead * PLANE :], flat[:, : (T - ahead) * PLANE], CONTRACT, preferred_element_type=F32
        )
        for at, mine, other in halves(flags[1], grads):
            at += 9 * kt * (C // 2)
            keep[at : at + C // 2] = mine
            send[at : at + C // 2] = other
    keep[HALF:] = jnp.zeros((COMM - HALF, C), F32)
    send[HALF:] = jnp.zeros((COMM - HALF, C), F32)
    to_window.wait()


def edge_kernel(flags, keep_in, send_in, near, far, last, keep, send, tmp, adj):
    for f in range(HALO):
        put_adjoint(adj, f, by_row(pick(flags[1] == 0, near[f], far[f]), tmp))
    for kt in range(2):
        ahead = 2 - kt
        grads = lax.dot_general(
            adj[:, : ahead * PLANE], last[:, (HALO - ahead) * PLANE :], CONTRACT, preferred_element_type=F32
        )
        for at, mine, other in halves(flags[1], grads):
            at += 9 * kt * (C // 2)
            keep[at : at + C // 2] = keep_in[at : at + C // 2] + mine
            send[at : at + C // 2] = send_in[at : at + C // 2] + other


def add_kernel(keep, received, chip, chip_v, sem):
    started = []
    step = COMM // 4
    for i in range(4):
        piece = pl.ds(i * step, step)
        chip_v[piece] = keep[piece] + received[piece]
        started += copies(sem.at[pl.ds(i, 1)], (chip_v.at[piece], chip.at[piece]))
    for copy in started:
        copy.wait()


def part_kernel(parts, sums, packed):
    packed[:PART] = jnp.sum(parts[...].astype(F32), axis=0)
    packed[PART:] = sums[...]


def merge_kernel(own, one, three, two, parts, backward, parts_v, sem):
    total = (own[...] + one[...]) + (two[...] + three[...])
    part = total[:PART].astype(BF16)
    for i in range(SIDE // 4):
        parts_v[i] = part
    started = copies(sem, *((parts_v, parts.at[pl.ds(i * (SIDE // 4), SIDE // 4)]) for i in range(4)))
    backward[...] = own[PART:] + two[PART:]
    for copy in started:
        copy.wait()


def place_kernel(flags, half_grad, grad, grad_v, sem, first):
    half = C // 2
    core = flags[1] if first else 1 - flags[1]
    at = pl.multiple_of(core * half, half)
    started = []
    for kt in range(3):
        rows_of = half_grad[9 * kt * half : 9 * (kt + 1) * half].astype(F32)
        grad_v[9 * kt : 9 * (kt + 1)] = rows_of.reshape(9, half, C)
        taps = pl.ds(9 * kt, 9)
        started += copies(sem.at[pl.ds(kt, 1)], (grad_v.at[taps], grad.at[taps, pl.ds(at, half)]))
    for copy in started:
        copy.wait()


def place_first(flags, half_grad, grad, grad_v, sem):
    place_kernel(flags, half_grad, grad, grad_v, sem, True)


def place_second(flags, half_grad, grad_in, grad, grad_v, sem):
    place_kernel(flags, half_grad, grad, grad_v, sem, False)


def finish_kernel(
    flags,
    lat,
    cot,
    near,
    far,
    kernel,
    window,
    totals,
    scales,
    backward,
    scaled,
    output,
    result,
    tmp,
    taps,
    lat_v,
    cot_v,
    kernel_v,
    window_v,
    scaled_v,
    output_v,
    result_v,
    sem,
    out_sem,
):
    from_kernel, from_window, from_lat, from_cot, from_scaled = copies(
        sem,
        (kernel, kernel_v),
        (window, window_v.at[:, HALO * W :]),
        (lat, lat_v),
        (cot, cot_v),
        (scaled, scaled_v),
    )
    center, inverse = center_inverse(totals, PER)
    for f in range(HALO):
        blocks = by_row(pick(flags[1] == 0, far[f], near[f]), tmp)
        for h in range(H):
            active = jnp.where(flags[0] > 0, activated(blocks[h], center, inverse, scales), 0.0)
            for s, moved in enumerate(shifted(active)):
                window_v[(s * H + h) * C : (s * H + h + 1) * C, f * W : (f + 1) * W] = moved.astype(BF16)
    clear(taps)
    from_kernel.wait()
    for kt in range(3):
        for ki in range(3):
            for kj in range(3):
                tap = kernel_v[9 * kt + 3 * ki + kj]
                for h in range(H):
                    other = h - 1 + ki
                    if 0 <= other < H:
                        at = (kj * H + other) * C
                        taps[kt, h * C : (h + 1) * C, at : at + C] = tap
    from_window.wait()
    total = jnp.dot(taps[0], window_v[:, 0 : T * W], preferred_element_type=F32)
    for f in range(1, 3):
        total = total + jnp.dot(taps[f], window_v[:, f * W : (f + T) * W], preferred_element_type=F32)
    center, inverse = center_inverse(totals, PER * H)
    row = backward[...][0:1] / MEMBERS
    first = group_column(row, 0, PER * H)
    second = group_column(row, GROUPS, PER * H)
    for copy in (from_lat, from_cot, from_scaled):
        copy.wait()
    started = []
    for t in range(T):
        frame = lat_v[t].astype(F32)
        value = cot_v[t].astype(F32) + inverse * (scaled_v[t] - first - (frame - center) * inverse * second)
        result_v[t] = value.astype(BF16)
        started += copies(out_sem.at[pl.ds(T + t, 1)], (result_v.at[t], result.at[t]))
        for h in range(H):
            tmp[pl.ds(h, C, stride=H), :] = total[h * C : (h + 1) * C, t * W : (t + 1) * W]
        output_v[t] = (frame + tmp[...]).astype(BF16)
        started += copies(out_sem.at[pl.ds(t, 1)], (output_v.at[t], output.at[t]))
    for copy in started:
        copy.wait()


VMEM, HBM, SMEM = (
    pl.BlockSpec(memory_space=pltpu.VMEM),
    pl.BlockSpec(memory_space=pltpu.HBM),
    pl.BlockSpec(memory_space=pltpu.SMEM),
)


def call(body, out, scratch, *operands, far=(), out_far=(), scalars=0, flops=0, moved=1 << 20, aliases=(), limit=12):
    single = not isinstance(out, tuple)
    count = 1 if single else len(out)
    outs = tuple(HBM if i in out_far else VMEM for i in range(count))
    shapes = tuple(pltpu.HBM(o.shape, o.dtype) if i in out_far else o for i, o in enumerate((out,) if single else out))
    operands = [pltpu.with_memory_space_constraint(x, pltpu.HBM) if i in far else x for i, x in enumerate(operands)]
    return pl.pallas_call(
        body,
        out_shape=shapes[0] if single else shapes,
        in_specs=[SMEM if i < scalars else HBM if i in far else VMEM for i in range(len(operands))],
        out_specs=outs[0] if single else outs,
        scratch_shapes=scratch,
        compiler_params=pltpu.CompilerParams(vmem_limit_bytes=limit * MIB),
        input_output_aliases=dict(aliases),
        cost_estimate=pl.CostEstimate(flops=flops, bytes_accessed=moved, transcendentals=0),
    )(*operands)


def shape(*dims, dtype=F32):
    return jax.ShapeDtypeStruct(dims, dtype)


def sems(count):
    return pltpu.SemaphoreType.DMA((count,))


def swap(value, axis):
    return lax.ppermute(value, axis, [(0, 1), (1, 0)])


def exchange(parts, axes):
    return lax.all_to_all(parts, axes, 0, 0)


def per_device(latents, norm_gain, norm_shift, kernel, cotangent):
    lat = latents.reshape(T, ROWS, W)
    cot = cotangent.reshape(T, ROWS, W)
    gain, shift = norm_gain.reshape(1, C), norm_shift.reshape(1, C)
    zh, core = lax.axis_index("zh"), lax.axis_index("core")
    flags = jnp.stack([zh * 2 + core, core]).astype(jnp.int32)
    halo = shape(HALO, ROWS, W, dtype=BF16)
    frames = pltpu.VMEM((T, ROWS, W), BF16)
    tmp = pltpu.VMEM((ROWS, W), F32)
    row = pltpu.VMEM((1, C), F32)
    window_scratch = pltpu.VMEM((3 * ROWS, (T + HALO) * W), BF16)
    taps = pltpu.VMEM((3, ROWS, 3 * ROWS), BF16)
    kernel_scratch = pltpu.VMEM((27, C, C), BF16)
    scaled_scratch = pltpu.VMEM((T, ROWS, W), F32)
    own = call(start_kernel, shape(8, W), [frames, sems(T)], lat, far=(0,))
    to_near, to_far = call(halo_kernel, (halo, halo), [sems(2)], flags, own, lat, cot, far=(2, 3), scalars=1)
    gain, to_far = lax.optimization_barrier((gain, to_far))
    adj, scales = call(
        prepare_kernel,
        (shape(4 * C, T * PLANE, dtype=BF16), shape(2, C, W)),
        [frames, frames, row, row, tmp, sems(4)],
        lat,
        cot,
        gain,
        shift,
        far=(0, 1, 2, 3),
        flops=0,
    )
    slab = ("zh", "core")
    before = lax.ppermute(to_far, slab, [(1, 2), (2, 1)])
    far = before
    across, scales = lax.optimization_barrier((swap(own, "zh"), scales))
    pair = own + across
    to_near, pair = lax.optimization_barrier((to_near, pair))
    near = swap(to_near, "core")
    totals = jnp.concatenate([pair, swap(pair, "core")], axis=0)
    window, keep, send, last = call(
        grad_kernel,
        (
            shape(3 * ROWS, T * W, dtype=BF16),
            shape(COMM, C),
            shape(COMM, C),
            shape(3 * C, HALO * PLANE, dtype=BF16),
        ),
        [pltpu.VMEM((3 * C, T * PLANE), BF16), pltpu.VMEM((3 * ROWS, T * W), BF16), sems(1)],
        flags,
        adj,
        totals,
        scales,
        out_far=(0,),
        scalars=1,
        flops=2 * 10**9,
    )
    near, far, last = lax.optimization_barrier((near, far, last))
    keep, send = call(
        edge_kernel,
        (shape(COMM, C), shape(COMM, C)),
        [tmp, pltpu.VMEM((3 * C, HALO * PLANE), BF16)],
        flags,
        keep,
        send,
        near,
        far,
        last,
        scalars=1,
        aliases=((1, 0), (2, 1)),
    )
    chip = call(
        add_kernel,
        shape(COMM, C),
        [pltpu.VMEM((COMM, C), F32), sems(4)],
        keep,
        swap(send, "core"),
        out_far=(0,),
    )
    parts = exchange(chip.reshape(SIDE, PART, C), ("y", "zn", "x"))
    scaled, sums = call(
        back_kernel,
        (shape(T, ROWS, W), shape(8, W)),
        [tmp, window_scratch, taps, frames, frames, kernel_scratch, scaled_scratch, sems(3)],
        flags,
        lat,
        cot,
        near,
        far,
        kernel,
        totals,
        scales,
        far=(1, 2, 5),
        out_far=(0,),
        scalars=1,
        limit=20,
        flops=4 * 10**9,
    )
    sums = sums + swap(sums, "core")
    packed = call(part_kernel, shape(PART + 8, C), [], parts, sums)
    others = [lax.ppermute(packed, ("zh", "zm"), [(i, i ^ flip) for i in range(4)]) for flip in (1, 3, 2)]
    part, backward = call(
        merge_kernel,
        (shape(SIDE, PART, C, dtype=BF16), shape(8, C)),
        [pltpu.VMEM((SIDE // 4, PART, C), BF16), sems(4)],
        packed,
        *others,
        out_far=(0,),
    )
    part, window = lax.optimization_barrier((part, window))
    block = shape(T, ROWS, W, dtype=BF16)
    output, result = call(
        finish_kernel,
        (block, block),
        [tmp, taps, frames, frames, kernel_scratch, window_scratch, scaled_scratch, frames, frames, sems(5), sems(2 * T)],
        flags,
        lat,
        cot,
        near,
        far,
        kernel,
        window,
        totals,
        scales,
        backward,
        scaled,
        far=(1, 2, 5, 6, 10),
        out_far=(0, 1),
        limit=20,
        scalars=1,
        flops=4 * 10**9,
    )
    mine, output, result = lax.optimization_barrier(
        (exchange(part, ("y", "zn", "x")).reshape(COMM, C), output, result)
    )
    other = swap(mine, "core")
    half_scratch = [pltpu.VMEM((27, C // 2, C), F32), sems(3)]
    kernel_grad = call(
        place_first, shape(27, C, C), half_scratch, flags, mine, out_far=(0,), scalars=1, flops=10**9
    )
    kernel_grad = call(
        place_second,
        shape(27, C, C),
        half_scratch,
        flags,
        other,
        kernel_grad,
        far=(2,),
        out_far=(0,),
        scalars=1,
        aliases=((2, 0),),
    )
    return output.reshape(latents.shape), result.reshape(latents.shape), kernel_grad


def solution(mesh):
    fine = Mesh(mesh.devices.reshape(2, 2, 4, 2, 2, 4), ("zh", "core", "y", "zm", "zn", "x"))
    frames = P(("y", "zm", "zn", "x"), ("zh", "core"), None, None, None)
    return jax.shard_map(
        per_device,
        mesh=fine,
        in_specs=(frames, P(), P(), P(), frames),
        out_specs=(frames, frames, P()),
        check_vma=False,
    )
```

```python
import functools

import jax
import jax.numpy as jnp
from jax import lax
from jax.experimental import pallas as pl
from jax.experimental.pallas import tpu as pltpu
from jax.sharding import Mesh
from jax.sharding import PartitionSpec as P

C = 128
H = 4
W = 128
T = 4
HALO = 2
GROUPS = 32
PER = C // GROUPS
SLABS = 4
MEMBERS = SLABS * T * PER * H * W
ROWS = H * C
HALF = 27 * (C // 2)
COMM = HALF + 64
SIDE = 32
PART = COMM // SIDE
F32 = jnp.float32
BF16 = jnp.bfloat16
MIB = 1024 * 1024


def lanes():
    return lax.broadcasted_iota(jnp.int32, (C, W), 1)


def rows():
    return lax.broadcasted_iota(jnp.int32, (C, W), 0)


def shifted(block):
    left = jnp.where(lanes() == 0, 0.0, pltpu.roll(block, 1, 1))
    right = jnp.where(lanes() == W - 1, 0.0, pltpu.roll(block, W - 1, 1))
    return left, block, right


def row_of(column, offset):
    lane = lax.broadcasted_iota(jnp.int32, (GROUPS, W), 1)
    sub = lax.broadcasted_iota(jnp.int32, (GROUPS, W), 0)
    return jnp.sum(jnp.where(lane == sub + offset, column, 0.0), axis=0, keepdims=True)


def channel_column(row):
    return jnp.sum(jnp.where(lanes() == rows(), row, 0.0), axis=1, keepdims=True)


def group_column(row, offset, per_channel):
    lane = lax.broadcasted_iota(jnp.int32, (GROUPS * per_channel, W), 1)
    sub = lax.broadcasted_iota(jnp.int32, (GROUPS * per_channel, W), 0)
    return jnp.sum(jnp.where(lane == sub // per_channel + offset, row, 0.0), axis=1, keepdims=True)


def center_inverse(totals, per_channel):
    row = jnp.sum(totals[...].reshape(-1, 8, W), axis=0)[0:1] / MEMBERS
    center = group_column(row, 0, per_channel)
    square = group_column(row, GROUPS, per_channel)
    return center, lax.rsqrt(square - center * center + 1e-06)


def copies(sem, *pairs):
    started = [pltpu.make_async_copy(source, target, sem.at[i]) for i, (source, target) in enumerate(pairs)]
    for copy in started:
        copy.start()
    return started


def start_kernel(flags, lat, cot, sums, near, far, lat_v, sem, halo_sem):
    parts = copies(sem, *((lat.at[t], lat_v.at[t]) for t in range(T)))
    tail, head = lat.at[T - HALO :], cot.at[:HALO]

    @pl.when(flags[1] == 0)
    def _():
        copies(halo_sem, (tail, near), (head, far))

    @pl.when(flags[1] != 0)
    def _():
        copies(halo_sem, (head, near), (tail, far))

    total = jnp.zeros((ROWS, W), F32)
    square = jnp.zeros((ROWS, W), F32)
    for t in range(T):
        parts[t].wait()
        x = lat_v[t].astype(F32)
        total = total + x
        square = square + x * x
    total = jnp.sum(jnp.sum(total.reshape(GROUPS, -1, W), axis=1), axis=1, keepdims=True)
    square = jnp.sum(jnp.sum(square.reshape(GROUPS, -1, W), axis=1), axis=1, keepdims=True)
    row = row_of(total, 0) + row_of(square, GROUPS)
    sums[...] = jnp.broadcast_to(row, (8, W))
    pltpu.make_async_copy(tail, near, halo_sem.at[0]).wait()
    pltpu.make_async_copy(head, far, halo_sem.at[1]).wait()


def put_adjoint(adj, f, mine):
    zero = jnp.zeros((C, W), BF16)
    for h in range(H):
        for ki in range(3):
            source = h - ki + 1
            block = mine[source].astype(BF16) if 0 <= source < H else zero
            adj[ki * C : (ki + 1) * C, (f * H + h) * W : (f * H + h + 1) * W] = block


def prepare_kernel(lat, cot, gain, shift, adj, scales, lat_v, cot_v, gain_v, shift_v, tmp, sem):
    from_lat, from_cot, *small = copies(sem, (lat, lat_v), (cot, cot_v), (gain, gain_v), (shift, shift_v))
    from_lat.wait()
    for t in range(T):
        for h, block in enumerate(by_row(lat_v[t], tmp)):
            adj[3 * C :, (t * H + h) * W : (t * H + h + 1) * W] = block.astype(BF16)
    from_cot.wait()
    for t in range(T):
        put_adjoint(adj, t, by_row(cot_v[t], tmp))
    for copy in small:
        copy.wait()
    scales[0] = jnp.broadcast_to(channel_column(gain_v[...]), (C, W))
    scales[1] = jnp.broadcast_to(channel_column(shift_v[...]), (C, W))


def clear(taps):
    zero = jnp.zeros((C, C), BF16)
    for f in range(3):
        for s in range(3):
            for h in range(H):
                for other in range(H):
                    if abs(h - other) > 1:
                        at = (s * H + other) * C
                        taps[f, h * C : (h + 1) * C, at : at + C] = zero


def pick(condition, first, second):
    return jnp.where(condition, first.astype(F32), second.astype(F32))


def by_row(frame, tmp):
    tmp[...] = frame.astype(F32)
    return [tmp[pl.ds(h, C, stride=H), :] for h in range(H)]


def back_kernel(
    flags, lat, cot, near, far, kernel, totals, scales, scaled, sums, tmp, window, taps, lat_v, cot_v, kernel_v, scaled_v, sem
):
    from_cot, from_kernel, from_lat = copies(sem, (cot, cot_v), (kernel, kernel_v), (lat, lat_v))
    from_cot.wait()
    for f in range(T + HALO):
        blocks = by_row(cot_v[f] if f < T else pick(flags[1] == 0, near[f - T], far[f - T]), tmp)
        for h in range(H):
            for s, moved in enumerate(shifted(blocks[h])):
                at = (s * H + h) * C
                window[at : at + C, f * W : (f + 1) * W] = moved.astype(BF16)
    clear(taps)
    from_kernel.wait()
    for kt in range(3):
        for ki in range(3):
            for kj in range(3):
                tap = kernel_v[9 * kt + 3 * ki + kj].astype(F32).T.astype(BF16)
                for h in range(H):
                    other = h + 1 - ki
                    if 0 <= other < H:
                        at = ((2 - kj) * H + other) * C
                        taps[2 - kt, h * C : (h + 1) * C, at : at + C] = tap
    back = jnp.dot(taps[0], window[:, 0 : T * W], preferred_element_type=F32)
    for f in range(1, 3):
        back = back + jnp.dot(taps[f], window[:, f * W : (f + T) * W], preferred_element_type=F32)
    center, inverse = center_inverse(totals, PER)
    from_lat.wait()
    first = jnp.zeros((C, W), F32)
    second = jnp.zeros((C, W), F32)
    for t in range(T):
        blocks = by_row(lat_v[t], tmp)
        for h in range(H):
            unit = (blocks[h] - center) * inverse
            normed = unit * scales[0] + scales[1]
            sig = 1.0 / (1.0 + jnp.exp(-normed))
            adjoint = back[h * C : (h + 1) * C, t * W : (t + 1) * W]
            value = adjoint * sig * (1.0 + normed * (1.0 - sig)) * scales[0]
            first = first + value
            second = second + value * unit
            scaled_v[t, pl.ds(h, C, stride=H), :] = value
    (to_scaled,) = copies(sem, (scaled_v, scaled))
    lane, sub = lanes(), rows()
    first = jnp.where(lane == sub // PER, jnp.sum(first, axis=1, keepdims=True), 0.0)
    second = jnp.where(lane == sub // PER + GROUPS, jnp.sum(second, axis=1, keepdims=True), 0.0)
    sums[...] = jnp.broadcast_to(jnp.sum(first + second, axis=0, keepdims=True), (8, W))
    to_scaled.wait()


def activated(block, center, inverse, scales):
    normed = (block - center) * inverse * scales[0] + scales[1]
    return (normed * (1.0 / (1.0 + jnp.exp(-normed)))).astype(BF16).astype(F32)


CONTRACT = (((1,), (1,)), ((), ()))
PLANE = H * W


def halves(core, grads):
    half = C // 2
    for ki in range(3):
        for kj in range(3):
            tap = grads[ki * C : (ki + 1) * C, kj * C : (kj + 1) * C]
            low, high = tap[:half], tap[half:]
            at = (3 * ki + kj) * half
            yield at, jnp.where(core == 0, low, high), jnp.where(core == 0, high, low)


def grad_kernel(flags, adj, totals, scales, window, keep, send, last, flat, window_v, sem):
    center, inverse = center_inverse(totals, PER)
    for t in range(T):
        for h in range(H):
            block = adj[3 * C :, (t * H + h) * W : (t * H + h + 1) * W].astype(F32)
            for s, moved in enumerate(shifted(activated(block, center, inverse, scales))):
                moved = moved.astype(BF16)
                window_v[(s * H + h) * C : (s * H + h + 1) * C, t * W : (t + 1) * W] = moved
                flat[s * C : (s + 1) * C, (t * H + h) * W : (t * H + h + 1) * W] = moved
                if t >= T - HALO:
                    at = ((t - T + HALO) * H + h) * W
                    last[s * C : (s + 1) * C, at : at + W] = moved
    (to_window,) = copies(sem, (window_v, window))
    for kt in range(3):
        ahead = 2 - kt
        grads = lax.dot_general(
            adj[: 3 * C, ahead * PLANE :], flat[:, : (T - ahead) * PLANE], CONTRACT, preferred_element_type=F32
        )
        for at, mine, other in halves(flags[1], grads):
            at += 9 * kt * (C // 2)
            keep[at : at + C // 2] = mine
            send[at : at + C // 2] = other
    keep[HALF:] = jnp.zeros((COMM - HALF, C), F32)
    send[HALF:] = jnp.zeros((COMM - HALF, C), F32)
    to_window.wait()


def edge_kernel(flags, keep_in, send_in, near, far, last, keep, send, tmp, adj):
    for f in range(HALO):
        put_adjoint(adj, f, by_row(pick(flags[1] == 0, near[f], far[f]), tmp))
    for kt in range(2):
        ahead = 2 - kt
        grads = lax.dot_general(
            adj[:, : ahead * PLANE], last[:, (HALO - ahead) * PLANE :], CONTRACT, preferred_element_type=F32
        )
        for at, mine, other in halves(flags[1], grads):
            at += 9 * kt * (C // 2)
            keep[at : at + C // 2] = keep_in[at : at + C // 2] + mine
            send[at : at + C // 2] = send_in[at : at + C // 2] + other


def add_kernel(keep, received, chip, chip_v, sem):
    started = []
    step = COMM // 4
    for i in range(4):
        piece = pl.ds(i * step, step)
        chip_v[piece] = keep[piece] + received[piece]
        started += copies(sem.at[pl.ds(i, 1)], (chip_v.at[piece], chip.at[piece]))
    for copy in started:
        copy.wait()


def part_kernel(parts, sums, packed):
    packed[:PART] = jnp.sum(parts[...].astype(F32), axis=0)
    packed[PART:] = sums[...]


def merge_kernel(own, one, three, two, parts, backward, parts_v, sem):
    total = (own[...] + one[...]) + (two[...] + three[...])
    part = total[:PART].astype(BF16)
    for i in range(SIDE // 4):
        parts_v[i] = part
    started = copies(sem, *((parts_v, parts.at[pl.ds(i * (SIDE // 4), SIDE // 4)]) for i in range(4)))
    backward[...] = own[PART:] + two[PART:]
    for copy in started:
        copy.wait()


def place_kernel(flags, half_grad, grad, grad_v, sem, first):
    half = C // 2
    core = flags[1] if first else 1 - flags[1]
    at = pl.multiple_of(core * half, half)
    started = []
    for kt in range(3):
        rows_of = half_grad[9 * kt * half : 9 * (kt + 1) * half].astype(F32)
        grad_v[9 * kt : 9 * (kt + 1)] = rows_of.reshape(9, half, C)
        taps = pl.ds(9 * kt, 9)
        started += copies(sem.at[pl.ds(kt, 1)], (grad_v.at[taps], grad.at[taps, pl.ds(at, half)]))
    for copy in started:
        copy.wait()


def place_first(flags, half_grad, grad, grad_v, sem):
    place_kernel(flags, half_grad, grad, grad_v, sem, True)


def place_second(flags, half_grad, grad_in, grad, grad_v, sem):
    place_kernel(flags, half_grad, grad, grad_v, sem, False)


def finish_kernel(
    flags,
    lat,
    cot,
    near,
    far,
    kernel,
    window,
    totals,
    scales,
    backward,
    scaled,
    output,
    result,
    tmp,
    taps,
    lat_v,
    cot_v,
    kernel_v,
    window_v,
    scaled_v,
    output_v,
    result_v,
    sem,
    out_sem,
):
    from_kernel, from_window, from_lat, from_cot, from_scaled = copies(
        sem,
        (kernel, kernel_v),
        (window, window_v.at[:, HALO * W :]),
        (lat, lat_v),
        (cot, cot_v),
        (scaled, scaled_v),
    )
    center, inverse = center_inverse(totals, PER)
    for f in range(HALO):
        blocks = by_row(pick(flags[1] == 0, far[f], near[f]), tmp)
        for h in range(H):
            active = jnp.where(flags[0] > 0, activated(blocks[h], center, inverse, scales), 0.0)
            for s, moved in enumerate(shifted(active)):
                window_v[(s * H + h) * C : (s * H + h + 1) * C, f * W : (f + 1) * W] = moved.astype(BF16)
    clear(taps)
    from_kernel.wait()
    for kt in range(3):
        for ki in range(3):
            for kj in range(3):
                tap = kernel_v[9 * kt + 3 * ki + kj]
                for h in range(H):
                    other = h - 1 + ki
                    if 0 <= other < H:
                        at = (kj * H + other) * C
                        taps[kt, h * C : (h + 1) * C, at : at + C] = tap
    from_window.wait()
    total = jnp.dot(taps[0], window_v[:, 0 : T * W], preferred_element_type=F32)
    for f in range(1, 3):
        total = total + jnp.dot(taps[f], window_v[:, f * W : (f + T) * W], preferred_element_type=F32)
    center, inverse = center_inverse(totals, PER * H)
    row = backward[...][0:1] / MEMBERS
    first = group_column(row, 0, PER * H)
    second = group_column(row, GROUPS, PER * H)
    for copy in (from_lat, from_cot, from_scaled):
        copy.wait()
    started = []
    for t in range(T):
        frame = lat_v[t].astype(F32)
        value = cot_v[t].astype(F32) + inverse * (scaled_v[t] - first - (frame - center) * inverse * second)
        result_v[t] = value.astype(BF16)
        started += copies(out_sem.at[pl.ds(T + t, 1)], (result_v.at[t], result.at[t]))
        for h in range(H):
            tmp[pl.ds(h, C, stride=H), :] = total[h * C : (h + 1) * C, t * W : (t + 1) * W]
        output_v[t] = (frame + tmp[...]).astype(BF16)
        started += copies(out_sem.at[pl.ds(t, 1)], (output_v.at[t], output.at[t]))
    for copy in started:
        copy.wait()


VMEM, HBM, SMEM = (
    pl.BlockSpec(memory_space=pltpu.VMEM),
    pl.BlockSpec(memory_space=pltpu.HBM),
    pl.BlockSpec(memory_space=pltpu.SMEM),
)


def call(body, out, scratch, *operands, far=(), out_far=(), scalars=0, flops=0, moved=1 << 20, aliases=(), limit=12):
    single = not isinstance(out, tuple)
    count = 1 if single else len(out)
    outs = tuple(HBM if i in out_far else VMEM for i in range(count))
    shapes = tuple(pltpu.HBM(o.shape, o.dtype) if i in out_far else o for i, o in enumerate((out,) if single else out))
    operands = [pltpu.with_memory_space_constraint(x, pltpu.HBM) if i in far else x for i, x in enumerate(operands)]
    return pl.pallas_call(
        body,
        out_shape=shapes[0] if single else shapes,
        in_specs=[SMEM if i < scalars else HBM if i in far else VMEM for i in range(len(operands))],
        out_specs=outs[0] if single else outs,
        scratch_shapes=scratch,
        compiler_params=pltpu.CompilerParams(vmem_limit_bytes=limit * MIB),
        input_output_aliases=dict(aliases),
        cost_estimate=pl.CostEstimate(flops=flops, bytes_accessed=moved, transcendentals=0),
    )(*operands)


def shape(*dims, dtype=F32):
    return jax.ShapeDtypeStruct(dims, dtype)


def sems(count):
    return pltpu.SemaphoreType.DMA((count,))


def swap(value, axis):
    return lax.ppermute(value, axis, [(0, 1), (1, 0)])


def exchange(parts, axes):
    return lax.all_to_all(parts, axes, 0, 0)


def per_device(latents, norm_gain, norm_shift, kernel, cotangent):
    lat = latents.reshape(T, ROWS, W)
    cot = cotangent.reshape(T, ROWS, W)
    gain, shift = norm_gain.reshape(1, C), norm_shift.reshape(1, C)
    zh, core = lax.axis_index("zh"), lax.axis_index("core")
    flags = jnp.stack([zh * 2 + core, core]).astype(jnp.int32)
    halo = shape(HALO, ROWS, W, dtype=BF16)
    frames = pltpu.VMEM((T, ROWS, W), BF16)
    tmp = pltpu.VMEM((ROWS, W), F32)
    row = pltpu.VMEM((1, C), F32)
    window_scratch = pltpu.VMEM((3 * ROWS, (T + HALO) * W), BF16)
    taps = pltpu.VMEM((3, ROWS, 3 * ROWS), BF16)
    kernel_scratch = pltpu.VMEM((27, C, C), BF16)
    scaled_scratch = pltpu.VMEM((T, ROWS, W), F32)
    own, to_near, to_far = call(
        start_kernel,
        (shape(8, W), halo, halo),
        [frames, sems(T), sems(2)],
        flags,
        lat,
        cot,
        far=(1, 2),
        scalars=1,
    )
    gain, to_far = lax.optimization_barrier((gain, to_far))
    adj, scales = call(
        prepare_kernel,
        (shape(4 * C, T * PLANE, dtype=BF16), shape(2, C, W)),
        [frames, frames, row, row, tmp, sems(4)],
        lat,
        cot,
        gain,
        shift,
        far=(0, 1, 2, 3),
        flops=0,
    )
    slab = ("zh", "core")
    before = lax.ppermute(to_far, slab, [(1, 2), (2, 1)])
    far = before
    across, scales = lax.optimization_barrier((swap(own, "zh"), scales))
    pair = own + across
    to_near, pair = lax.optimization_barrier((to_near, pair))
    near = swap(to_near, "core")
    totals = jnp.concatenate([pair, swap(pair, "core")], axis=0)
    window, keep, send, last = call(
        grad_kernel,
        (
            shape(3 * ROWS, T * W, dtype=BF16),
            shape(COMM, C),
            shape(COMM, C),
            shape(3 * C, HALO * PLANE, dtype=BF16),
        ),
        [pltpu.VMEM((3 * C, T * PLANE), BF16), pltpu.VMEM((3 * ROWS, T * W), BF16), sems(1)],
        flags,
        adj,
        totals,
        scales,
        out_far=(0,),
        scalars=1,
        flops=2 * 10**9,
    )
    near, far, last = lax.optimization_barrier((near, far, last))
    keep, send = call(
        edge_kernel,
        (shape(COMM, C), shape(COMM, C)),
        [tmp, pltpu.VMEM((3 * C, HALO * PLANE), BF16)],
        flags,
        keep,
        send,
        near,
        far,
        last,
        scalars=1,
        aliases=((1, 0), (2, 1)),
    )
    chip = call(
        add_kernel,
        shape(COMM, C),
        [pltpu.VMEM((COMM, C), F32), sems(4)],
        keep,
        swap(send, "core"),
        out_far=(0,),
    )
    parts = exchange(chip.reshape(SIDE, PART, C), ("y", "zn", "x"))
    scaled, sums = call(
        back_kernel,
        (shape(T, ROWS, W), shape(8, W)),
        [tmp, window_scratch, taps, frames, frames, kernel_scratch, scaled_scratch, sems(3)],
        flags,
        lat,
        cot,
        near,
        far,
        kernel,
        totals,
        scales,
        far=(1, 2, 5),
        out_far=(0,),
        scalars=1,
        limit=20,
        flops=4 * 10**9,
    )
    sums = sums + swap(sums, "core")
    packed = call(part_kernel, shape(PART + 8, C), [], parts, sums)
    others = [lax.ppermute(packed, ("zh", "zm"), [(i, i ^ flip) for i in range(4)]) for flip in (1, 3, 2)]
    part, backward = call(
        merge_kernel,
        (shape(SIDE, PART, C, dtype=BF16), shape(8, C)),
        [pltpu.VMEM((SIDE // 4, PART, C), BF16), sems(4)],
        packed,
        *others,
        out_far=(0,),
    )
    part, window = lax.optimization_barrier((part, window))
    block = shape(T, ROWS, W, dtype=BF16)
    output, result = call(
        finish_kernel,
        (block, block),
        [tmp, taps, frames, frames, kernel_scratch, window_scratch, scaled_scratch, frames, frames, sems(5), sems(2 * T)],
        flags,
        lat,
        cot,
        near,
        far,
        kernel,
        window,
        totals,
        scales,
        backward,
        scaled,
        far=(1, 2, 5, 6, 10),
        out_far=(0, 1),
        limit=20,
        scalars=1,
        flops=4 * 10**9,
    )
    mine, output, result = lax.optimization_barrier(
        (exchange(part, ("y", "zn", "x")).reshape(COMM, C), output, result)
    )
    other = swap(mine, "core")
    half_scratch = [pltpu.VMEM((27, C // 2, C), F32), sems(3)]
    kernel_grad = call(
        place_first, shape(27, C, C), half_scratch, flags, mine, out_far=(0,), scalars=1, flops=10**9
    )
    kernel_grad = call(
        place_second,
        shape(27, C, C),
        half_scratch,
        flags,
        other,
        kernel_grad,
        far=(2,),
        out_far=(0,),
        scalars=1,
        aliases=((2, 0),),
    )
    return output.reshape(latents.shape), result.reshape(latents.shape), kernel_grad


def solution(mesh):
    fine = Mesh(mesh.devices.reshape(2, 2, 4, 2, 2, 4), ("zh", "core", "y", "zm", "zn", "x"))
    frames = P(("y", "zm", "zn", "x"), ("zh", "core"), None, None, None)
    return jax.shard_map(
        per_device,
        mesh=fine,
        in_specs=(frames, P(), P(), P(), frames),
        out_specs=(frames, frames, P()),
        check_vma=False,
    )
```

```python
import functools

import jax
import jax.numpy as jnp
from jax import lax
from jax.experimental import pallas as pl
from jax.experimental.pallas import tpu as pltpu
from jax.sharding import Mesh
from jax.sharding import PartitionSpec as P

C = 128
H = 4
W = 128
T = 4
HALO = 2
GROUPS = 32
PER = C // GROUPS
SLABS = 4
MEMBERS = SLABS * T * PER * H * W
ROWS = H * C
HALF = 27 * (C // 2)
COMM = HALF + 64
SIDE = 32
PART = COMM // SIDE
F32 = jnp.float32
BF16 = jnp.bfloat16
MIB = 1024 * 1024


def lanes():
    return lax.broadcasted_iota(jnp.int32, (C, W), 1)


def rows():
    return lax.broadcasted_iota(jnp.int32, (C, W), 0)


def shifted(block):
    left = jnp.where(lanes() == 0, 0.0, pltpu.roll(block, 1, 1))
    right = jnp.where(lanes() == W - 1, 0.0, pltpu.roll(block, W - 1, 1))
    return left, block, right


def row_of(column, offset):
    lane = lax.broadcasted_iota(jnp.int32, (GROUPS, W), 1)
    sub = lax.broadcasted_iota(jnp.int32, (GROUPS, W), 0)
    return jnp.sum(jnp.where(lane == sub + offset, column, 0.0), axis=0, keepdims=True)


def channel_column(row):
    return jnp.sum(jnp.where(lanes() == rows(), row, 0.0), axis=1, keepdims=True)


def group_column(row, offset, per_channel):
    lane = lax.broadcasted_iota(jnp.int32, (GROUPS * per_channel, W), 1)
    sub = lax.broadcasted_iota(jnp.int32, (GROUPS * per_channel, W), 0)
    return jnp.sum(jnp.where(lane == sub // per_channel + offset, row, 0.0), axis=1, keepdims=True)


def center_inverse(totals, per_channel):
    row = jnp.sum(totals[...].reshape(-1, 8, W), axis=0)[0:1] / MEMBERS
    center = group_column(row, 0, per_channel)
    square = group_column(row, GROUPS, per_channel)
    return center, lax.rsqrt(square - center * center + 1e-06)


def copies(sem, *pairs):
    started = [pltpu.make_async_copy(source, target, sem.at[i]) for i, (source, target) in enumerate(pairs)]
    for copy in started:
        copy.start()
    return started


def start_kernel(flags, lat, cot, sums, far, lat_v, sem, halo_sem):
    parts = copies(sem, *((lat.at[t], lat_v.at[t]) for t in range(T)))
    tail, head = lat.at[T - HALO :], cot.at[:HALO]

    @pl.when(flags[1] == 0)
    def _():
        copies(halo_sem, (head, far))

    @pl.when(flags[1] != 0)
    def _():
        copies(halo_sem, (tail, far))

    total = jnp.zeros((ROWS, W), F32)
    square = jnp.zeros((ROWS, W), F32)
    for t in range(T):
        parts[t].wait()
        x = lat_v[t].astype(F32)
        total = total + x
        square = square + x * x
    total = jnp.sum(jnp.sum(total.reshape(GROUPS, -1, W), axis=1), axis=1, keepdims=True)
    square = jnp.sum(jnp.sum(square.reshape(GROUPS, -1, W), axis=1), axis=1, keepdims=True)
    row = row_of(total, 0) + row_of(square, GROUPS)
    sums[...] = jnp.broadcast_to(row, (8, W))
    pltpu.make_async_copy(head, far, halo_sem.at[0]).wait()


def put_adjoint(adj, f, mine):
    zero = jnp.zeros((C, W), BF16)
    for h in range(H):
        for ki in range(3):
            source = h - ki + 1
            block = mine[source].astype(BF16) if 0 <= source < H else zero
            adj[ki * C : (ki + 1) * C, (f * H + h) * W : (f * H + h + 1) * W] = block


def prepare_kernel(
    flags, lat, cot, gain, shift, adj, scales, near, lat_v, cot_v, gain_v, shift_v, tmp, sem, halo_sem
):
    tail, head = lat.at[T - HALO :], cot.at[:HALO]

    @pl.when(flags[1] == 0)
    def _():
        copies(halo_sem, (tail, near))

    @pl.when(flags[1] != 0)
    def _():
        copies(halo_sem, (head, near))

    from_lat, from_cot, *small = copies(sem, (lat, lat_v), (cot, cot_v), (gain, gain_v), (shift, shift_v))
    from_lat.wait()
    for t in range(T):
        for h, block in enumerate(by_row(lat_v[t], tmp)):
            adj[3 * C :, (t * H + h) * W : (t * H + h + 1) * W] = block.astype(BF16)
    from_cot.wait()
    for t in range(T):
        put_adjoint(adj, t, by_row(cot_v[t], tmp))
    for copy in small:
        copy.wait()
    scales[0] = jnp.broadcast_to(channel_column(gain_v[...]), (C, W))
    scales[1] = jnp.broadcast_to(channel_column(shift_v[...]), (C, W))
    pltpu.make_async_copy(tail, near, halo_sem.at[0]).wait()


def clear(taps):
    zero = jnp.zeros((C, C), BF16)
    for f in range(3):
        for s in range(3):
            for h in range(H):
                for other in range(H):
                    if abs(h - other) > 1:
                        at = (s * H + other) * C
                        taps[f, h * C : (h + 1) * C, at : at + C] = zero


def pick(condition, first, second):
    return jnp.where(condition, first.astype(F32), second.astype(F32))


def by_row(frame, tmp):
    tmp[...] = frame.astype(F32)
    return [tmp[pl.ds(h, C, stride=H), :] for h in range(H)]


def back_kernel(
    flags, lat, cot, near, far, kernel, totals, scales, scaled, sums, tmp, window, taps, lat_v, cot_v, kernel_v, scaled_v, sem
):
    from_cot, from_kernel, from_lat = copies(sem, (cot, cot_v), (kernel, kernel_v), (lat, lat_v))
    from_cot.wait()
    for f in range(T + HALO):
        blocks = by_row(cot_v[f] if f < T else pick(flags[1] == 0, near[f - T], far[f - T]), tmp)
        for h in range(H):
            for s, moved in enumerate(shifted(blocks[h])):
                at = (s * H + h) * C
                window[at : at + C, f * W : (f + 1) * W] = moved.astype(BF16)
    clear(taps)
    from_kernel.wait()
    for kt in range(3):
        for ki in range(3):
            for kj in range(3):
                tap = kernel_v[9 * kt + 3 * ki + kj].astype(F32).T.astype(BF16)
                for h in range(H):
                    other = h + 1 - ki
                    if 0 <= other < H:
                        at = ((2 - kj) * H + other) * C
                        taps[2 - kt, h * C : (h + 1) * C, at : at + C] = tap
    back = jnp.dot(taps[0], window[:, 0 : T * W], preferred_element_type=F32)
    for f in range(1, 3):
        back = back + jnp.dot(taps[f], window[:, f * W : (f + T) * W], preferred_element_type=F32)
    center, inverse = center_inverse(totals, PER)
    from_lat.wait()
    first = jnp.zeros((C, W), F32)
    second = jnp.zeros((C, W), F32)
    for t in range(T):
        blocks = by_row(lat_v[t], tmp)
        for h in range(H):
            unit = (blocks[h] - center) * inverse
            normed = unit * scales[0] + scales[1]
            sig = 1.0 / (1.0 + jnp.exp(-normed))
            adjoint = back[h * C : (h + 1) * C, t * W : (t + 1) * W]
            value = adjoint * sig * (1.0 + normed * (1.0 - sig)) * scales[0]
            first = first + value
            second = second + value * unit
            scaled_v[t, pl.ds(h, C, stride=H), :] = value
    (to_scaled,) = copies(sem, (scaled_v, scaled))
    lane, sub = lanes(), rows()
    first = jnp.where(lane == sub // PER, jnp.sum(first, axis=1, keepdims=True), 0.0)
    second = jnp.where(lane == sub // PER + GROUPS, jnp.sum(second, axis=1, keepdims=True), 0.0)
    sums[...] = jnp.broadcast_to(jnp.sum(first + second, axis=0, keepdims=True), (8, W))
    to_scaled.wait()


def activated(block, center, inverse, scales):
    normed = (block - center) * inverse * scales[0] + scales[1]
    return (normed * (1.0 / (1.0 + jnp.exp(-normed)))).astype(BF16).astype(F32)


CONTRACT = (((1,), (1,)), ((), ()))
PLANE = H * W


def halves(core, grads):
    half = C // 2
    for ki in range(3):
        for kj in range(3):
            tap = grads[ki * C : (ki + 1) * C, kj * C : (kj + 1) * C]
            low, high = tap[:half], tap[half:]
            at = (3 * ki + kj) * half
            yield at, jnp.where(core == 0, low, high), jnp.where(core == 0, high, low)


def grad_kernel(flags, adj, totals, scales, window, keep, send, last, flat, window_v, sem):
    center, inverse = center_inverse(totals, PER)
    for t in range(T):
        for h in range(H):
            block = adj[3 * C :, (t * H + h) * W : (t * H + h + 1) * W].astype(F32)
            for s, moved in enumerate(shifted(activated(block, center, inverse, scales))):
                moved = moved.astype(BF16)
                window_v[(s * H + h) * C : (s * H + h + 1) * C, t * W : (t + 1) * W] = moved
                flat[s * C : (s + 1) * C, (t * H + h) * W : (t * H + h + 1) * W] = moved
                if t >= T - HALO:
                    at = ((t - T + HALO) * H + h) * W
                    last[s * C : (s + 1) * C, at : at + W] = moved
    (to_window,) = copies(sem, (window_v, window))
    for kt in range(3):
        ahead = 2 - kt
        grads = lax.dot_general(
            adj[: 3 * C, ahead * PLANE :], flat[:, : (T - ahead) * PLANE], CONTRACT, preferred_element_type=F32
        )
        for at, mine, other in halves(flags[1], grads):
            at += 9 * kt * (C // 2)
            keep[at : at + C // 2] = mine
            send[at : at + C // 2] = other
    keep[HALF:] = jnp.zeros((COMM - HALF, C), F32)
    send[HALF:] = jnp.zeros((COMM - HALF, C), F32)
    to_window.wait()


def edge_kernel(flags, keep_in, send_in, near, far, last, keep, send, tmp, adj):
    for f in range(HALO):
        put_adjoint(adj, f, by_row(pick(flags[1] == 0, near[f], far[f]), tmp))
    for kt in range(2):
        ahead = 2 - kt
        grads = lax.dot_general(
            adj[:, : ahead * PLANE], last[:, (HALO - ahead) * PLANE :], CONTRACT, preferred_element_type=F32
        )
        for at, mine, other in halves(flags[1], grads):
            at += 9 * kt * (C // 2)
            keep[at : at + C // 2] = keep_in[at : at + C // 2] + mine
            send[at : at + C // 2] = send_in[at : at + C // 2] + other


def add_kernel(keep, received, chip, chip_v, sem):
    started = []
    step = COMM // 4
    for i in range(4):
        piece = pl.ds(i * step, step)
        chip_v[piece] = keep[piece] + received[piece]
        started += copies(sem.at[pl.ds(i, 1)], (chip_v.at[piece], chip.at[piece]))
    for copy in started:
        copy.wait()


def part_kernel(parts, sums, packed):
    packed[:PART] = jnp.sum(parts[...].astype(F32), axis=0)
    packed[PART:] = sums[...]


def merge_kernel(own, one, three, two, parts, backward, parts_v, sem):
    total = (own[...] + one[...]) + (two[...] + three[...])
    part = total[:PART].astype(BF16)
    for i in range(SIDE // 4):
        parts_v[i] = part
    started = copies(sem, *((parts_v, parts.at[pl.ds(i * (SIDE // 4), SIDE // 4)]) for i in range(4)))
    backward[...] = own[PART:] + two[PART:]
    for copy in started:
        copy.wait()


def place_kernel(flags, half_grad, grad, grad_v, sem, first):
    half = C // 2
    core = flags[1] if first else 1 - flags[1]
    at = pl.multiple_of(core * half, half)
    started = []
    for i in range(9):
        rows_of = half_grad[3 * i * half : 3 * (i + 1) * half].astype(F32)
        grad_v[3 * i : 3 * (i + 1)] = rows_of.reshape(3, half, C)
        taps = pl.ds(3 * i, 3)
        started += copies(sem.at[pl.ds(i, 1)], (grad_v.at[taps], grad.at[taps, pl.ds(at, half)]))
    for copy in started:
        copy.wait()


def place_first(flags, half_grad, grad, grad_v, sem):
    place_kernel(flags, half_grad, grad, grad_v, sem, True)


def place_second(flags, half_grad, grad_in, grad, grad_v, sem):
    place_kernel(flags, half_grad, grad, grad_v, sem, False)


def finish_kernel(
    flags,
    lat,
    cot,
    near,
    far,
    kernel,
    window,
    totals,
    scales,
    backward,
    scaled,
    output,
    result,
    tmp,
    taps,
    lat_v,
    cot_v,
    kernel_v,
    window_v,
    scaled_v,
    output_v,
    result_v,
    sem,
    out_sem,
):
    from_kernel, from_window, from_lat, from_cot, from_scaled = copies(
        sem,
        (kernel, kernel_v),
        (window, window_v.at[:, HALO * W :]),
        (lat, lat_v),
        (cot, cot_v),
        (scaled, scaled_v),
    )
    center, inverse = center_inverse(totals, PER)
    for f in range(HALO):
        blocks = by_row(pick(flags[1] == 0, far[f], near[f]), tmp)
        for h in range(H):
            active = jnp.where(flags[0] > 0, activated(blocks[h], center, inverse, scales), 0.0)
            for s, moved in enumerate(shifted(active)):
                window_v[(s * H + h) * C : (s * H + h + 1) * C, f * W : (f + 1) * W] = moved.astype(BF16)
    clear(taps)
    from_kernel.wait()
    for kt in range(3):
        for ki in range(3):
            for kj in range(3):
                tap = kernel_v[9 * kt + 3 * ki + kj]
                for h in range(H):
                    other = h - 1 + ki
                    if 0 <= other < H:
                        at = (kj * H + other) * C
                        taps[kt, h * C : (h + 1) * C, at : at + C] = tap
    from_window.wait()
    total = jnp.dot(taps[0], window_v[:, 0 : T * W], preferred_element_type=F32)
    for f in range(1, 3):
        total = total + jnp.dot(taps[f], window_v[:, f * W : (f + T) * W], preferred_element_type=F32)
    center, inverse = center_inverse(totals, PER * H)
    row = backward[...][0:1] / MEMBERS
    first = group_column(row, 0, PER * H)
    second = group_column(row, GROUPS, PER * H)
    for copy in (from_lat, from_cot, from_scaled):
        copy.wait()
    started = []
    for t in range(T):
        frame = lat_v[t].astype(F32)
        value = cot_v[t].astype(F32) + inverse * (scaled_v[t] - first - (frame - center) * inverse * second)
        result_v[t] = value.astype(BF16)
        started += copies(out_sem.at[pl.ds(T + t, 1)], (result_v.at[t], result.at[t]))
        for h in range(H):
            tmp[pl.ds(h, C, stride=H), :] = total[h * C : (h + 1) * C, t * W : (t + 1) * W]
        output_v[t] = (frame + tmp[...]).astype(BF16)
        started += copies(out_sem.at[pl.ds(t, 1)], (output_v.at[t], output.at[t]))
    for copy in started:
        copy.wait()


VMEM, HBM, SMEM = (
    pl.BlockSpec(memory_space=pltpu.VMEM),
    pl.BlockSpec(memory_space=pltpu.HBM),
    pl.BlockSpec(memory_space=pltpu.SMEM),
)


def call(body, out, scratch, *operands, far=(), out_far=(), scalars=0, flops=0, moved=1 << 20, aliases=(), limit=12):
    single = not isinstance(out, tuple)
    count = 1 if single else len(out)
    outs = tuple(HBM if i in out_far else VMEM for i in range(count))
    shapes = tuple(pltpu.HBM(o.shape, o.dtype) if i in out_far else o for i, o in enumerate((out,) if single else out))
    operands = [pltpu.with_memory_space_constraint(x, pltpu.HBM) if i in far else x for i, x in enumerate(operands)]
    return pl.pallas_call(
        body,
        out_shape=shapes[0] if single else shapes,
        in_specs=[SMEM if i < scalars else HBM if i in far else VMEM for i in range(len(operands))],
        out_specs=outs[0] if single else outs,
        scratch_shapes=scratch,
        compiler_params=pltpu.CompilerParams(vmem_limit_bytes=limit * MIB),
        input_output_aliases=dict(aliases),
        cost_estimate=pl.CostEstimate(flops=flops, bytes_accessed=moved, transcendentals=0),
    )(*operands)


def shape(*dims, dtype=F32):
    return jax.ShapeDtypeStruct(dims, dtype)


def sems(count):
    return pltpu.SemaphoreType.DMA((count,))


def swap(value, axis):
    return lax.ppermute(value, axis, [(0, 1), (1, 0)])


def exchange(parts, axes):
    return lax.all_to_all(parts, axes, 0, 0)


def per_device(latents, norm_gain, norm_shift, kernel, cotangent):
    lat = latents.reshape(T, ROWS, W)
    cot = cotangent.reshape(T, ROWS, W)
    gain, shift = norm_gain.reshape(1, C), norm_shift.reshape(1, C)
    zh, core = lax.axis_index("zh"), lax.axis_index("core")
    flags = jnp.stack([zh * 2 + core, core]).astype(jnp.int32)
    halo = shape(HALO, ROWS, W, dtype=BF16)
    frames = pltpu.VMEM((T, ROWS, W), BF16)
    tmp = pltpu.VMEM((ROWS, W), F32)
    row = pltpu.VMEM((1, C), F32)
    window_scratch = pltpu.VMEM((3 * ROWS, (T + HALO) * W), BF16)
    taps = pltpu.VMEM((3, ROWS, 3 * ROWS), BF16)
    kernel_scratch = pltpu.VMEM((27, C, C), BF16)
    scaled_scratch = pltpu.VMEM((T, ROWS, W), F32)
    own, to_far = call(
        start_kernel,
        (shape(8, W), halo),
        [frames, sems(T), sems(1)],
        flags,
        lat,
        cot,
        far=(1, 2),
        scalars=1,
    )
    gain, to_far = lax.optimization_barrier((gain, to_far))
    adj, scales, to_near = call(
        prepare_kernel,
        (shape(4 * C, T * PLANE, dtype=BF16), shape(2, C, W), halo),
        [frames, frames, row, row, tmp, sems(4), sems(1)],
        flags,
        lat,
        cot,
        gain,
        shift,
        far=(1, 2, 3, 4),
        scalars=1,
        flops=0,
    )
    slab = ("zh", "core")
    before = lax.ppermute(to_far, slab, [(1, 2), (2, 1)])
    far = before
    across, scales = lax.optimization_barrier((swap(own, "zh"), scales))
    pair = own + across
    to_near, pair = lax.optimization_barrier((to_near, pair))
    near = swap(to_near, "core")
    totals = jnp.concatenate([pair, swap(pair, "core")], axis=0)
    window, keep, send, last = call(
        grad_kernel,
        (
            shape(3 * ROWS, T * W, dtype=BF16),
            shape(COMM, C),
            shape(COMM, C),
            shape(3 * C, HALO * PLANE, dtype=BF16),
        ),
        [pltpu.VMEM((3 * C, T * PLANE), BF16), pltpu.VMEM((3 * ROWS, T * W), BF16), sems(1)],
        flags,
        adj,
        totals,
        scales,
        out_far=(0,),
        scalars=1,
        flops=2 * 10**9,
    )
    near, far, last = lax.optimization_barrier((near, far, last))
    keep, send = call(
        edge_kernel,
        (shape(COMM, C), shape(COMM, C)),
        [tmp, pltpu.VMEM((3 * C, HALO * PLANE), BF16)],
        flags,
        keep,
        send,
        near,
        far,
        last,
        scalars=1,
        aliases=((1, 0), (2, 1)),
    )
    chip = call(
        add_kernel,
        shape(COMM, C),
        [pltpu.VMEM((COMM, C), F32), sems(4)],
        keep,
        swap(send, "core"),
        out_far=(0,),
    )
    parts = exchange(chip.reshape(SIDE, PART, C), ("y", "zn", "x"))
    scaled, sums = call(
        back_kernel,
        (shape(T, ROWS, W), shape(8, W)),
        [tmp, window_scratch, taps, frames, frames, kernel_scratch, scaled_scratch, sems(3)],
        flags,
        lat,
        cot,
        near,
        far,
        kernel,
        totals,
        scales,
        far=(1, 2, 5),
        out_far=(0,),
        scalars=1,
        limit=20,
        flops=4 * 10**9,
    )
    sums = sums + swap(sums, "core")
    packed = call(part_kernel, shape(PART + 8, C), [], parts, sums)
    others = [lax.ppermute(packed, ("zh", "zm"), [(i, i ^ flip) for i in range(4)]) for flip in (1, 3, 2)]
    part, backward = call(
        merge_kernel,
        (shape(SIDE, PART, C, dtype=BF16), shape(8, C)),
        [pltpu.VMEM((SIDE // 4, PART, C), BF16), sems(4)],
        packed,
        *others,
        out_far=(0,),
    )
    part, window = lax.optimization_barrier((part, window))
    block = shape(T, ROWS, W, dtype=BF16)
    output, result = call(
        finish_kernel,
        (block, block),
        [tmp, taps, frames, frames, kernel_scratch, window_scratch, scaled_scratch, frames, frames, sems(5), sems(2 * T)],
        flags,
        lat,
        cot,
        near,
        far,
        kernel,
        window,
        totals,
        scales,
        backward,
        scaled,
        far=(1, 2, 5, 6, 10),
        out_far=(0, 1),
        limit=20,
        scalars=1,
        flops=4 * 10**9,
    )
    mine, output, result = lax.optimization_barrier(
        (exchange(part, ("y", "zn", "x")).reshape(COMM, C), output, result)
    )
    other = swap(mine, "core")
    half_scratch = [pltpu.VMEM((27, C // 2, C), F32), sems(9)]
    kernel_grad = call(
        place_first, shape(27, C, C), half_scratch, flags, mine, out_far=(0,), scalars=1, flops=10**9
    )
    kernel_grad = call(
        place_second,
        shape(27, C, C),
        half_scratch,
        flags,
        other,
        kernel_grad,
        far=(2,),
        out_far=(0,),
        scalars=1,
        aliases=((2, 0),),
    )
    return output.reshape(latents.shape), result.reshape(latents.shape), kernel_grad


def solution(mesh):
    fine = Mesh(mesh.devices.reshape(2, 2, 4, 2, 2, 4), ("zh", "core", "y", "zm", "zn", "x"))
    frames = P(("y", "zm", "zn", "x"), ("zh", "core"), None, None, None)
    return jax.shard_map(
        per_device,
        mesh=fine,
        in_specs=(frames, P(), P(), P(), frames),
        out_specs=(frames, frames, P()),
        check_vma=False,
    )
```
